32 devices in a mesh: wall: 2 (over x), row: 16 (over z, y, core).
Axes of the slice: x: 2, y: 2, z: 4, core: 2. Of those that a mesh axis runs over, the one named last changes fastest.
Arguments:
- thermal_scalars: float32 [2, 8, 1024, 1024], P(None, 'wall', 'row'), may hold values from -6 to 6
- conductive_number: float32 [2, 8], P(None, 'wall'), may hold values from 0.05 to 0.45
Outputs:
- advanced: float32 [2, 8, 1024, 1024], P(None, 'wall', 'row')
The draws below stay inside these ranges and needn't reach their ends.
All inputs are finite; a program needn't handle non-finite values.
Results may differ from the reference program's by a relative error of at most 0.00007.
Values sent between devices are 32-bit elements; how exact they have to be, the bound alone decides.
No kernel may reach another device: no remote copies, remote signals or barrier semaphores. Data moves between devices by JAX's collectives and lax.ppermute only.
A program may use at most 64 MiB of HBM per device.

```python
import math
import jax
import jax.numpy as jnp

DOWNSTREAM_COUNT = 1024
LATERAL_COUNT = 1024
STEPS = 3
NORMAL_LAYERS = 8


def levels(stream_key, shape, split, smallest, high):
    def one(dim, blocks):
        heights = jax.random.uniform(jax.random.fold_in(jax.random.fold_in(stream_key, 6), dim), (blocks,), jnp.float32, smallest / len(split), high / len(split))
        return jnp.repeat(jnp.exp(heights), shape[dim] // blocks).reshape((-1,) + (1,) * (len(shape) - dim - 1))

    gain = one(*split[0])
    for cut in split[1:]:
        gain = gain * one(*cut)
    return gain


def normal_values(key, shape, width, most, shards=(), kind=jnp.bfloat16):
    loudness = levels(key, shape, shards, -0.22, 0.18) if shards else 1.0
    result = jax.random.normal(key, shape, jnp.float32) * width * loudness
    return jnp.minimum(jnp.maximum(result, -most), most).astype(kind)


def setup_inputs(seed: int = 0) -> dict:
    streams_of = jax.random.split(jax.random.key(seed), 3)
    return {
        "thermal_scalars": normal_values(streams_of[0], (2, NORMAL_LAYERS, DOWNSTREAM_COUNT, LATERAL_COUNT), 1.0, 6.0, ((1, 2), (2, 16)), jnp.float32),
        "conductive_number": jnp.clip(jnp.exp(math.log(0.45) - 2.1972245 * jax.random.uniform(streams_of[1], (2, NORMAL_LAYERS), jnp.float32) ** levels(streams_of[1], (2, NORMAL_LAYERS), ((1, 2),), -0.2, 0.2)), 0.05, 0.45),
    }


def signed_square(waves, length):
    signed = jnp.where(waves > length // 2, waves - length, waves).astype(jnp.int32)
    scaled = (2.0 * math.pi / length) * signed.astype(jnp.float32)
    return scaled * scaled


def reference(thermal_scalars, conductive_number):
    complex_combined_fields = jnp.fft.fft2(thermal_scalars[0] + 1j * thermal_scalars[1], axes=(1, 2))
    mirror = jnp.roll(jnp.flip(complex_combined_fields, axis=(1, 2)), 1, axis=(1, 2))
    first_hat = 0.5 * (complex_combined_fields + jnp.conj(mirror))
    second_hat = -0.5j * (complex_combined_fields - jnp.conj(mirror))
    square_x = signed_square(jnp.arange(DOWNSTREAM_COUNT, dtype=jnp.int32), DOWNSTREAM_COUNT)
    square_y = signed_square(jnp.arange(LATERAL_COUNT, dtype=jnp.int32), LATERAL_COUNT)
    wave_sq = square_x[:, None] + square_y[None, :]
    results = []
    for scalar, scalar_field in enumerate([first_hat, second_hat]):
        rate_col = conductive_number[scalar][:, None, None]
        damping = jnp.exp(-rate_col * wave_sq[None, :, :])
        for substep in range(STEPS):
            padded = jnp.pad(scalar_field, ((1, 1), (0, 0), (0, 0)))
            curve_term = padded[2:] + padded[:-2] - 2.0 * scalar_field
            scalar_field = damping * (scalar_field + rate_col * curve_term)
        results.append(scalar_field)
    joined = results[0] + 1j * results[1]
    spatial = jnp.fft.ifft2(joined, axes=(1, 2))
    return jnp.stack([jnp.real(spatial), jnp.imag(spatial)]).astype(jnp.float32)
```

```python
import functools

import jax
import jax.numpy as jnp
import ml_dtypes
import numpy as np
from jax import lax
from jax.experimental import pallas as pl
from jax.experimental.pallas import tpu as pltpu
from jax.sharding import PartitionSpec as P

STEPS = 3
AXES = ("wall", "row")
VMEM_BYTES = 48 * 1024 * 1024


def cas_table(length, offset, step):
    half = length // 2
    samples = np.arange(half, dtype=np.int64)
    waves = offset + step * np.arange(half, dtype=np.int64)
    angle = (samples[:, None] * waves[None, :] % length) * (2.0 * np.pi / length)
    return np.cos(angle) + np.sin(angle)


def split_table(table):
    high = table.astype(np.float32).astype(ml_dtypes.bfloat16)
    low = (table - high.astype(np.float64)).astype(np.float32).astype(ml_dtypes.bfloat16)
    return np.stack([high, low])


def tables(length):
    even = split_table(cas_table(length, 0, 2))
    odd = split_table(cas_table(length, 1, 2))
    return even, odd, np.ascontiguousarray(odd.transpose(0, 2, 1))


def split(value):
    high = value.astype(jnp.bfloat16)
    low = (value - high.astype(jnp.float32)).astype(jnp.bfloat16)
    return high, low


def product(a, b, dims):
    dot = functools.partial(
        lax.dot_general, dimension_numbers=(dims, ((), ())), preferred_element_type=jnp.float32
    )
    return dot(a[0], b[0]) + (dot(a[0], b[1]) + dot(a[1], b[0]))


NN = ((1,), (0,))
NT = ((1,), (1,))


def pair(ref):
    return ref[0], ref[1]


def y_forward_kernel(field_ref, even_ref, odd_ref, out_ref):
    planes, lines, length = field_ref.shape[1:]
    half = length // 2
    rows = planes * lines
    low_part = field_ref[0, :, :, :half].reshape(rows, half)
    high_part = field_ref[0, :, :, half:].reshape(rows, half)
    devices = out_ref.shape[0] // 2
    even = product(pair(even_ref), split(low_part + high_part), NT)
    out_ref[:devices] = even.reshape(devices, -1, rows)
    odd = product(pair(odd_ref), split(low_part - high_part), NT)
    out_ref[devices:] = odd.reshape(devices, -1, rows)


def y_inverse_kernel(norm, spectrum_ref, even_ref, odd_ref, *rest):
    out_ref = rest[-1]
    devices, waves, rows = spectrum_ref.shape
    planes, lines, length = out_ref.shape[1:]
    half = length // 2
    even_in = spectrum_ref[: devices // 2].reshape(half, rows).T
    odd_in = spectrum_ref[devices // 2 :].reshape(half, rows).T
    even = product(split(even_in), pair(even_ref), NN)
    odd = product(split(odd_in), pair(odd_ref), NN)
    out_ref[0, :, :, :half] = ((even + odd) * norm).reshape(planes, lines, half)
    out_ref[0, :, :, half:] = ((even - odd) * norm).reshape(planes, lines, half)


def x_kernel(
    walls, rate_ref, square_y_ref, square_x_ref, even_ref, odd_ref, odd_turned_ref,
    received_ref, out_ref, sum_ref, difference_ref,
):
    devices, waves, rows = received_ref.shape
    groups = devices // walls
    half = even_ref.shape[1]
    lines = 2 * half // groups
    planes = rows // lines
    count = walls * planes
    lower = lax.broadcasted_iota(jnp.int32, (waves, 128), 1) < lines

    def paired(a, b):
        return (
            jnp.where(lower, a, pltpu.roll(b, lines, 1)),
            jnp.where(lower, pltpu.roll(a, lines, 1), b),
        )

    for w in range(walls):
        for p in range(planes // 2):
            lanes = slice(128 * p, 128 * (p + 1))
            top = (w * planes + 2 * p) * waves
            for j in range(groups // 4):
                first, second = w * groups + 2 * j, w * groups + 2 * j + groups // 2
                a, b = received_ref[first, :, lanes], received_ref[first + 1, :, lanes]
                c, d = received_ref[second, :, lanes], received_ref[second + 1, :, lanes]
                columns = slice(128 * j, 128 * (j + 1))
                for target, pieces in (
                    (sum_ref, paired(a + c, b + d)),
                    (difference_ref, paired(a - c, b - d)),
                ):
                    target[top : top + waves, columns] = pieces[0]
                    target[top + waves : top + 2 * waves, columns] = pieces[1]

    sum_ref[...] = product(split(sum_ref[...]), pair(even_ref), NN)
    difference_ref[...] = product(split(difference_ref[...]), pair(odd_ref), NN)

    rates = [rate_ref[z] for z in range(count)]
    damping_y = [jnp.exp(-rate * square_y_ref[...]) for rate in rates]
    for parity, ref in enumerate((sum_ref, difference_ref)):
        for j in range(half // 128):
            columns = slice(128 * j, 128 * (j + 1))
            square_x = square_x_ref[parity : parity + 1, columns]
            damping = [jnp.exp(-rate * square_x) * dy for rate, dy in zip(rates, damping_y)]
            field = [ref[z * waves : (z + 1) * waves, columns] for z in range(count)]
            for step in range(STEPS):
                updated = []
                for z in range(count):
                    around = field[z - 1] if z > 0 else None
                    if z + 1 < count:
                        around = field[z + 1] if around is None else around + field[z + 1]
                    value = (1.0 - 2.0 * rates[z]) * field[z]
                    if around is not None:
                        value = value + rates[z] * around
                    updated.append(damping[z] * value)
                field = updated
            for z in range(count):
                ref[z * waves : (z + 1) * waves, columns] = field[z]

    even = product(split(sum_ref[...]), pair(even_ref), NN)
    odd = product(split(difference_ref[...]), pair(odd_turned_ref), NN)
    sum_ref[...] = even + odd
    difference_ref[...] = even - odd

    for w in range(walls):
        for p in range(planes // 2):
            lanes = slice(128 * p, 128 * (p + 1))
            top = (w * planes + 2 * p) * waves
            for j in range(groups // 4):
                columns = slice(128 * j, 128 * (j + 1))
                first = w * groups + 2 * j
                for ref, target in ((sum_ref, first), (difference_ref, first + groups // 2)):
                    a, b = paired(
                        ref[top : top + waves, columns],
                        ref[top + waves : top + 2 * waves, columns],
                    )
                    out_ref[target, :, lanes] = a
                    out_ref[target + 1, :, lanes] = b


PARAMS = pltpu.CompilerParams(vmem_limit_bytes=VMEM_BYTES)
VMEM = pl.BlockSpec(memory_space=pltpu.VMEM)


def cost(terms, total):
    return pl.CostEstimate(flops=2 * terms, bytes_accessed=total, transcendentals=0)


def with_kernels(fields, rates, walls, square_y, square_x, ky, kx):
    scalars, planes, lines, length = fields.shape
    devices = walls * lax.axis_size("row")
    waves = length // devices
    rows = planes * lines
    even, odd, odd_turned = ky
    blocks = jax.ShapeDtypeStruct((devices, waves, rows), jnp.float32)
    block_bytes = 4 * rows * length
    work = 3 * rows * length * length // 2

    def scalar_block(s):
        return pl.BlockSpec((1, planes, lines, length), lambda i: (s, 0, 0, 0))

    def y_forward(s):
        return pl.pallas_call(
            y_forward_kernel,
            grid=(1,),
            in_specs=[scalar_block(s), pl.BlockSpec(even.shape, lambda i: (0, 0, 0)), pl.BlockSpec(odd.shape, lambda i: (0, 0, 0))],
            out_specs=pl.BlockSpec(blocks.shape, lambda i: (0, 0, 0)),
            out_shape=blocks,
            compiler_params=PARAMS,
            cost_estimate=cost(work, 2 * block_bytes + 4 * length * length // 2),
            name="y_forward",
        )(fields, even, odd_turned)

    def x_filter(received, rate):
        return pl.pallas_call(
            functools.partial(x_kernel, walls),
            in_specs=[pl.BlockSpec(memory_space=pltpu.SMEM)] + [VMEM] * 6,
            out_specs=VMEM,
            out_shape=blocks,
            scratch_shapes=[pltpu.VMEM((walls * planes * waves, kx[0].shape[1]), jnp.float32)] * 2,
            compiler_params=PARAMS,
            cost_estimate=cost(2 * work, 2 * block_bytes + 6 * length * length // 2),
            name="x_filter",
        )(rate, square_y, square_x, *kx, received)

    def y_inverse(s, spectrum, partial):
        norm = 1.0 / (length * lines * lax.axis_size("row"))
        extra = [] if partial is None else [partial]
        return pl.pallas_call(
            functools.partial(y_inverse_kernel, norm),
            grid=(1,),
            in_specs=[
                pl.BlockSpec(blocks.shape, lambda i: (0, 0, 0)),
                pl.BlockSpec(even.shape, lambda i: (0, 0, 0)),
                pl.BlockSpec(odd.shape, lambda i: (0, 0, 0)),
            ] + [pl.BlockSpec(memory_space=pl.ANY)] * len(extra),
            out_specs=scalar_block(s),
            out_shape=jax.ShapeDtypeStruct(fields.shape, jnp.float32),
            input_output_aliases={3: 0} if extra else {},
            compiler_params=PARAMS,
            cost_estimate=cost(work, 2 * block_bytes + 4 * length * length // 2),
            name="y_inverse",
        )(spectrum, even, odd_turned, *extra)

    exchanged = [exchange(y_forward(s)) for s in range(scalars)]
    returned = [exchange(x_filter(exchanged[s], rates[s])) for s in range(scalars)]
    result = None
    for s in range(scalars):
        result = y_inverse(s, returned[s], result)
    return result


def exchange(blocks):
    return lax.all_to_all(blocks, AXES, split_axis=0, concat_axis=0, tiled=True)


def with_arrays(fields, rates, walls, square_y, square_x, ky, kx):
    scalars, planes, lines, length = fields.shape
    groups = lax.axis_size("row")
    devices = walls * groups
    waves = length // devices
    count = walls * planes
    dot = functools.partial(jnp.matmul, precision=lax.Precision.HIGHEST)

    def whole(table):
        table = jnp.asarray(table)
        return table[0].astype(jnp.float32) + table[1].astype(jnp.float32)

    def forward(value, group):
        half = value.shape[-1] // 2
        a, b = value[..., :half], value[..., half:]
        return jnp.concatenate([dot(a + b, whole(group[0])), dot(a - b, whole(group[1]))], axis=-1)

    def inverse(value, group):
        half = value.shape[-1] // 2
        even, odd = dot(value[..., :half], whole(group[0])), dot(value[..., half:], whole(group[2]))
        return jnp.concatenate([even + odd, even - odd], axis=-1)

    results = []
    for s in range(scalars):
        spectral = forward(fields[s], ky).reshape(planes * lines, devices, waves)
        received = exchange(spectral.transpose(1, 2, 0))
        received = received.reshape(walls, groups, waves, planes, lines).transpose(0, 3, 2, 1, 4)
        field = forward(received.reshape(count, waves, groups * lines), kx)
        rate = rates[s][:, None, None]
        damping = jnp.exp(-rate * (square_y + square_x.reshape(1, -1)))
        for step in range(STEPS):
            padded = jnp.pad(field, ((1, 1), (0, 0), (0, 0)))
            field = damping * (field + rate * (padded[2:] + padded[:-2] - 2.0 * field))
        back = inverse(field, kx).reshape(walls, planes, waves, groups, lines).transpose(0, 3, 2, 1, 4)
        spectrum = exchange(back.reshape(devices, waves, planes * lines)).reshape(length, -1)
        results.append(inverse(spectrum.T, ky).reshape(planes, lines, length))
    return jnp.stack(results) * (1.0 / (length * groups * lines))


def signed_square(waves, length):
    signed = jnp.where(waves > length // 2, waves - length, waves)
    scaled = 2.0 * np.pi / length * signed.astype(jnp.float32)
    return scaled * scaled


def per_device(ky, kx, thermal_scalars, conductive_number):
    scalars, planes, lines, length = thermal_scalars.shape
    walls, groups = lax.axis_size("wall"), lax.axis_size("row")
    length_x = lines * groups
    devices = walls * groups
    waves = length // devices
    rates = lax.all_gather(conductive_number, "wall", axis=1, tiled=True)
    place = lax.axis_index(AXES) * waves + jnp.arange(waves, dtype=jnp.int32)
    order = 2 * (place % (length // 2)) + place // (length // 2)
    square_y = signed_square(order, length)[:, None]
    waves_x = jnp.stack([jnp.arange(0, length_x, 2), jnp.arange(1, length_x, 2)])
    square_x = signed_square(waves_x, length_x)
    aligned = lines == 64 and planes % 2 == 0 and waves % 8 == 0 and groups % 4 == 0
    run = with_kernels if aligned else with_arrays
    return run(thermal_scalars, rates, walls, square_y, square_x, ky, kx)


def solution(mesh):
    def run(thermal_scalars, conductive_number):
        ky = tables(thermal_scalars.shape[3])
        kx = tables(thermal_scalars.shape[2])
        return jax.shard_map(
            functools.partial(per_device, ky, kx),
            mesh=mesh,
            in_specs=(P(None, "wall", "row", None), P(None, "wall")),
            out_specs=P(None, "wall", "row", None),
            check_vma=False,
        )(thermal_scalars, conductive_number)

    return run
```

```python
import functools

import jax
import jax.numpy as jnp
import ml_dtypes
import numpy as np
from jax import lax
from jax.experimental import pallas as pl
from jax.experimental.pallas import tpu as pltpu
from jax.sharding import PartitionSpec as P

STEPS = 3
AXES = ("wall", "row")
WALLS, LEVELS, ROUND = 2, 4, 4
VMEM_BYTES = 60 * 1024 * 1024


def cas_table(length, offset, step):
    half = length // 2
    samples = np.arange(half, dtype=np.int64)
    waves = offset + step * np.arange(half, dtype=np.int64)
    angle = (samples[:, None] * waves[None, :] % length) * (2.0 * np.pi / length)
    return np.cos(angle) + np.sin(angle)


def split_table(table):
    high = table.astype(np.float32).astype(ml_dtypes.bfloat16)
    low = (table - high.astype(np.float64)).astype(np.float32).astype(ml_dtypes.bfloat16)
    return np.stack([high, low])


def tables(length):
    even = split_table(cas_table(length, 0, 2))
    odd = split_table(cas_table(length, 1, 2))
    return even, odd, np.ascontiguousarray(odd.transpose(0, 2, 1))


def split(value):
    high = value.astype(jnp.bfloat16)
    low = (value - high.astype(jnp.float32)).astype(jnp.bfloat16)
    return high, low


def product(a, b, dims):
    dot = functools.partial(
        lax.dot_general, dimension_numbers=(dims, ((), ())), preferred_element_type=jnp.float32
    )
    return dot(a[0], b[0]) + (dot(a[0], b[1]) + dot(a[1], b[0]))


NN = ((1,), (0,))
NT = ((1,), (1,))


def pair(ref):
    return ref[0], ref[1]


def y_forward_kernel(level_ref, field_ref, table_ref, *refs):
    out_refs, parts_ref = refs[:-1], refs[-1]
    planes, lines, length = field_ref.shape[1:]
    half = length // 2
    rows = planes * lines
    level = level_ref[0]
    lower = field_ref[0, :, :, :half].reshape(rows, half)
    upper = field_ref[0, :, :, half:].reshape(rows, half)
    parts_ref[0, 0], parts_ref[0, 1] = split(lower + upper)
    parts_ref[1, 0], parts_ref[1, 1] = split(lower - upper)
    for k in range(LEVELS):
        target = level ^ k
        parity = target // (LEVELS // 2)
        waves = product(
            (table_ref[target, 0], table_ref[target, 1]),
            (parts_ref[parity, 0], parts_ref[parity, 1]),
            NT,
        ).reshape(WALLS * ROUND, -1, rows)
        if len(out_refs) == 1:
            out_refs[0][:, k] = waves
        else:
            out_refs[k][...] = waves


def y_inverse_kernel(norm, pieces, level_ref, table_ref, *refs):
    spectrum_refs, out_ref, parts_ref = refs[:pieces], refs[-2], refs[-1]
    planes, lines, length = out_ref.shape[1:]
    half = length // 2
    level = level_ref[0]
    for k in range(LEVELS):
        source = spectrum_refs[0][:, k] if k == 0 or pieces == 1 else spectrum_refs[k][...]
        high, low = split(source.reshape(-1, source.shape[-1]).T)
        parts_ref[level ^ k, 0] = high
        parts_ref[level ^ k, 1] = low
    sums = []
    for parity in range(2):
        first = parity * (LEVELS // 2)
        levels = range(first, first + LEVELS // 2)
        left = [jnp.concatenate([parts_ref[t, i] for t in levels], axis=1) for i in range(2)]
        right = [jnp.concatenate([table_ref[t, i] for t in levels], axis=0) for i in range(2)]
        sums.append(product(left, right, NN))
    even, odd = sums
    out_ref[0, :, :, :half] = ((even + odd) * norm).reshape(planes, lines, half)
    out_ref[0, :, :, half:] = ((even - odd) * norm).reshape(planes, lines, half)


def x_kernel(
    scalar, separate, level_ref, rate_ref, square_y_ref, square_x_ref, even_ref, odd_ref,
    odd_turned_ref, *refs
):
    number = LEVELS if separate else 1
    in_refs, out_refs = refs[:number], refs[number : 2 * number]
    sum_ref, difference_ref = refs[2 * number : 2 * number + 2]
    level = level_ref[0]
    waves, rows = in_refs[0].shape[-2:]
    half = even_ref.shape[1]
    groups = LEVELS * ROUND
    lines = 2 * half // groups
    planes = rows // lines
    count = WALLS * planes
    lower = lax.broadcasted_iota(jnp.int32, (waves, 128), 1) < lines
    if separate:
        held_ref = refs[-1]
        for k in range(LEVELS):
            held_ref[level ^ k] = in_refs[0][:, 0] if k == 0 else in_refs[k][...]

    def load(w, r, lanes):
        place, height = w * ROUND + r % ROUND, r // ROUND
        if separate:
            return held_ref[height, place, :, lanes]
        return in_refs[0][place, height ^ level, :, lanes]

    def store(w, r, lanes, value):
        place, height = w * ROUND + r % ROUND, r // ROUND
        if separate:
            held_ref[height, place, :, lanes] = value
        else:
            out_refs[0][place, height ^ level, :, lanes] = value

    def paired(a, b):
        return (
            jnp.where(lower, a, pltpu.roll(b, lines, 1)),
            jnp.where(lower, pltpu.roll(a, lines, 1), b),
        )

    for w in range(WALLS):
        for p in range(planes // 2):
            lanes = slice(128 * p, 128 * (p + 1))
            top = (w * planes + 2 * p) * waves
            for j in range(groups // 4):
                first, second = 2 * j, 2 * j + groups // 2
                a, b = load(w, first, lanes), load(w, first + 1, lanes)
                c, d = load(w, second, lanes), load(w, second + 1, lanes)
                columns = slice(128 * j, 128 * (j + 1))
                for target, pieces in (
                    (sum_ref, paired(a + c, b + d)),
                    (difference_ref, paired(a - c, b - d)),
                ):
                    target[top : top + waves, columns] = pieces[0]
                    target[top + waves : top + 2 * waves, columns] = pieces[1]

    sum_ref[...] = product(split(sum_ref[...]), pair(even_ref), NN)
    difference_ref[...] = product(split(difference_ref[...]), pair(odd_ref), NN)

    rates = [rate_ref[scalar, z] for z in range(count)]
    damping_y = [jnp.exp(-rate * square_y_ref[...]) for rate in rates]
    for parity, ref in enumerate((sum_ref, difference_ref)):
        for j in range(half // 128):
            columns = slice(128 * j, 128 * (j + 1))
            square_x = square_x_ref[parity : parity + 1, columns]
            damping = [jnp.exp(-rate * square_x) * dy for rate, dy in zip(rates, damping_y)]
            field = [ref[z * waves : (z + 1) * waves, columns] for z in range(count)]
            for step in range(STEPS):
                updated = []
                for z in range(count):
                    value = (1.0 - 2.0 * rates[z]) * field[z]
                    if z == 0:
                        around = field[1]
                    elif z == count - 1:
                        around = field[z - 1]
                    else:
                        around = field[z - 1] + field[z + 1]
                    updated.append(damping[z] * (value + rates[z] * around))
                field = updated
            for z in range(count):
                ref[z * waves : (z + 1) * waves, columns] = field[z]

    even = product(split(sum_ref[...]), pair(even_ref), NN)
    odd = product(split(difference_ref[...]), pair(odd_turned_ref), NN)
    sum_ref[...] = even + odd
    difference_ref[...] = even - odd

    for w in range(WALLS):
        for p in range(planes // 2):
            lanes = slice(128 * p, 128 * (p + 1))
            top = (w * planes + 2 * p) * waves
            for j in range(groups // 4):
                columns = slice(128 * j, 128 * (j + 1))
                for ref, first in ((sum_ref, 2 * j), (difference_ref, 2 * j + groups // 2)):
                    a, b = paired(
                        ref[top : top + waves, columns],
                        ref[top + waves : top + 2 * waves, columns],
                    )
                    store(w, first, lanes, a)
                    store(w, first + 1, lanes, b)

    if separate:
        for k in range(LEVELS):
            out_refs[k][...] = held_ref[level ^ k]


PARAMS = pltpu.CompilerParams(vmem_limit_bytes=VMEM_BYTES)
SMEM = pl.BlockSpec(memory_space=pltpu.SMEM)


def cost(terms, total):
    return pl.CostEstimate(flops=2 * terms, bytes_accessed=total, transcendentals=0)


def full(array):
    return pl.BlockSpec(array.shape, lambda i, n=len(array.shape): (0,) * n)


def in_plane(blocks):
    groups = [
        [(w * LEVELS + t) * ROUND + g for w in range(WALLS) for g in range(ROUND)]
        for t in range(LEVELS)
    ]
    return lax.all_to_all(
        blocks, AXES, split_axis=0, concat_axis=0, tiled=True, axis_index_groups=groups
    )


def to_level(value, k):
    swap = [(t * ROUND + g, (t ^ k) * ROUND + g) for t in range(LEVELS) for g in range(ROUND)]
    return lax.ppermute(value, "row", swap)


def with_kernels(fields, own_rates, ky, kx):
    scalars, planes, lines, length = fields.shape
    length_x = lines * lax.axis_size("row")
    peers = WALLS * ROUND
    waves = length // (LEVELS * peers)
    rows = planes * lines
    wall, row = lax.axis_index("wall"), lax.axis_index("row")
    level = row // ROUND
    level_operand = jnp.reshape(level, (1,)).astype(jnp.int32)
    other_rates = lax.ppermute(own_rates, "wall", [(0, 1), (1, 0)])
    rates = jnp.concatenate(
        [jnp.where(wall == 0, own_rates, other_rates), jnp.where(wall == 0, other_rates, own_rates)],
        axis=1,
    )
    place = (level * peers + wall * ROUND + row % ROUND) * waves + jnp.arange(waves, dtype=jnp.int32)
    square_y = signed_square(wave_order(place, length), length)[:, None]
    square_x = signed_square(wave_order(jnp.arange(length_x), length_x), length_x).reshape(2, -1)

    half = length // 2
    y_table = np.concatenate([ky[0].transpose(0, 2, 1), ky[2]], axis=1)
    y_table = y_table.reshape(2, LEVELS, length // LEVELS, half).transpose(1, 0, 2, 3)
    joint = jax.ShapeDtypeStruct((peers, LEVELS, waves, rows), jnp.float32)
    single = jax.ShapeDtypeStruct((peers, waves, rows), jnp.float32)
    block_bytes = 4 * rows * length
    work = 3 * rows * length * length // 2

    def scalar_block(s):
        return pl.BlockSpec((1, planes, lines, length), lambda i: (s, 0, 0, 0))

    def y_forward(s, separate):
        out = [single] * LEVELS if separate else [joint]
        return pl.pallas_call(
            y_forward_kernel,
            grid=(1,),
            in_specs=[SMEM, scalar_block(s), full(y_table)],
            out_specs=[full(o) for o in out],
            out_shape=out,
            scratch_shapes=[pltpu.VMEM((2, 2, rows, half), jnp.bfloat16)],
            compiler_params=PARAMS,
            cost_estimate=cost(work, 2 * block_bytes + 2 * length * length),
            name="y_forward",
        )(level_operand, fields, y_table)

    def x_filter(s, received, separate):
        out = [single] * LEVELS if separate else [joint]
        scratch = [pltpu.VMEM((WALLS * planes * waves, length_x // 2), jnp.float32)] * 2
        if separate:
            scratch.append(pltpu.VMEM((LEVELS, peers, waves, rows), jnp.float32))
        operands = [square_y, square_x, *kx, *received]
        return pl.pallas_call(
            functools.partial(x_kernel, s, separate),
            grid=(1,),
            in_specs=[SMEM, SMEM] + [full(o) for o in operands],
            out_specs=[full(o) for o in out],
            out_shape=out,
            scratch_shapes=scratch,
            compiler_params=PARAMS,
            cost_estimate=cost(2 * work, 2 * block_bytes + 3 * length * length),
            name="x_filter",
        )(level_operand, rates, *operands)

    def y_inverse(s, spectrum, partial):
        norm = 1.0 / (length * length_x)
        extra = [] if partial is None else [partial]
        return pl.pallas_call(
            functools.partial(y_inverse_kernel, norm, len(spectrum)),
            grid=(1,),
            in_specs=[SMEM, full(y_table)]
            + [full(o) for o in spectrum]
            + [pl.BlockSpec(memory_space=pl.ANY)] * len(extra),
            out_specs=scalar_block(s),
            out_shape=jax.ShapeDtypeStruct(fields.shape, jnp.float32),
            input_output_aliases={2 + len(spectrum): 0} if extra else {},
            scratch_shapes=[pltpu.VMEM((LEVELS, 2, rows, length // LEVELS), jnp.bfloat16)],
            compiler_params=PARAMS,
            cost_estimate=cost(work, 2 * block_bytes + 2 * length * length),
            name="y_inverse",
        )(level_operand, y_table, *spectrum, *extra)

    def across(pieces):
        return [pieces[0]] + [to_level(pieces[k], k) for k in range(1, LEVELS)]

    def slices(array):
        return [array] + [array[:, k] for k in range(1, LEVELS)]

    first = across(y_forward(0, True))
    second = across(slices(in_plane(y_forward(1, False)[0])))
    first = in_plane(jnp.stack(first, axis=1))
    second = across(x_filter(1, second, True))
    first = across(slices(in_plane(x_filter(0, [first], False)[0])))
    second = in_plane(jnp.stack(second, axis=1))
    result = y_inverse(1, [second], None)
    return y_inverse(0, first, result)


def exchange(blocks):
    return lax.all_to_all(blocks, AXES, split_axis=0, concat_axis=0, tiled=True)


def with_arrays(fields, own_rates, ky, kx):
    scalars, planes, lines, length = fields.shape
    walls, groups = lax.axis_size("wall"), lax.axis_size("row")
    length_x = groups * lines
    devices = walls * groups
    waves = length // devices
    count = walls * planes
    rates = lax.all_gather(own_rates, "wall", axis=1, tiled=True)
    place = lax.axis_index(AXES) * waves + jnp.arange(waves, dtype=jnp.int32)
    square_y = signed_square(wave_order(place, length), length)[:, None]
    square_x = signed_square(wave_order(jnp.arange(length_x), length_x), length_x)
    dot = functools.partial(jnp.matmul, precision=lax.Precision.HIGHEST)

    def whole(table):
        table = jnp.asarray(table)
        return table[0].astype(jnp.float32) + table[1].astype(jnp.float32)

    def forward(value, group):
        half = value.shape[-1] // 2
        a, b = value[..., :half], value[..., half:]
        return jnp.concatenate([dot(a + b, whole(group[0])), dot(a - b, whole(group[1]))], axis=-1)

    def inverse(value, group):
        half = value.shape[-1] // 2
        even, odd = dot(value[..., :half], whole(group[0])), dot(value[..., half:], whole(group[2]))
        return jnp.concatenate([even + odd, even - odd], axis=-1)

    results = []
    for s in range(scalars):
        spectral = forward(fields[s], ky).reshape(planes * lines, devices, waves)
        received = exchange(spectral.transpose(1, 2, 0))
        received = received.reshape(walls, groups, waves, planes, lines).transpose(0, 3, 2, 1, 4)
        field = forward(received.reshape(count, waves, groups * lines), kx)
        rate = rates[s][:, None, None]
        damping = jnp.exp(-rate * (square_y + square_x.reshape(1, -1)))
        for step in range(STEPS):
            padded = jnp.pad(field, ((1, 1), (0, 0), (0, 0)))
            field = damping * (field + rate * (padded[2:] + padded[:-2] - 2.0 * field))
        back = inverse(field, kx).reshape(walls, planes, waves, groups, lines).transpose(0, 3, 2, 1, 4)
        spectrum = exchange(back.reshape(devices, waves, planes * lines)).reshape(length, -1)
        results.append(inverse(spectrum.T, ky).reshape(planes, lines, length))
    return jnp.stack(results) * (1.0 / (length * groups * lines))


def signed_square(waves, length):
    signed = jnp.where(waves > length // 2, waves - length, waves)
    scaled = 2.0 * np.pi / length * signed.astype(jnp.float32)
    return scaled * scaled


def wave_order(place, length):
    return 2 * (place % (length // 2)) + place // (length // 2)


def per_device(ky, kx, thermal_scalars, conductive_number):
    scalars, planes, lines, length = thermal_scalars.shape
    walls, groups = lax.axis_size("wall"), lax.axis_size("row")
    if (scalars, walls, groups, lines, planes % 2) == (2, WALLS, LEVELS * ROUND, 64, 0):
        return with_kernels(thermal_scalars, conductive_number, ky, kx)
    return with_arrays(thermal_scalars, conductive_number, ky, kx)


def solution(mesh):
    def run(thermal_scalars, conductive_number):
        ky = tables(thermal_scalars.shape[3])
        kx = tables(thermal_scalars.shape[2])
        return jax.shard_map(
            functools.partial(per_device, ky, kx),
            mesh=mesh,
            in_specs=(P(None, "wall", "row", None), P(None, "wall")),
            out_specs=P(None, "wall", "row", None),
            check_vma=False,
        )(thermal_scalars, conductive_number)

    return run
```

```python
import functools

import jax
import jax.numpy as jnp
import ml_dtypes
import numpy as np
from jax import lax
from jax.experimental import pallas as pl
from jax.experimental.pallas import tpu as pltpu
from jax.sharding import PartitionSpec as P

STEPS = 3
AXES = ("wall", "row")
VMEM_BYTES = 40 * 1024 * 1024


def cas_table(length, offset, step):
    half = length // 2
    samples = np.arange(half, dtype=np.int64)
    waves = offset + step * np.arange(half, dtype=np.int64)
    angle = (samples[:, None] * waves[None, :] % length) * (2.0 * np.pi / length)
    return np.cos(angle) + np.sin(angle)


def split_table(table):
    high = table.astype(np.float32).astype(ml_dtypes.bfloat16)
    low = (table - high.astype(np.float64)).astype(np.float32).astype(ml_dtypes.bfloat16)
    return np.stack([high, low])


def tables(length):
    even = split_table(cas_table(length, 0, 2))
    odd = split_table(cas_table(length, 1, 2))
    return even, odd, np.ascontiguousarray(odd.transpose(0, 2, 1))


def split(value):
    high = value.astype(jnp.bfloat16)
    low = (value - high.astype(jnp.float32)).astype(jnp.bfloat16)
    return high, low


def product(a, b, dims):
    dot = functools.partial(
        lax.dot_general, dimension_numbers=(dims, ((), ())), preferred_element_type=jnp.float32
    )
    return dot(a[0], b[0]) + (dot(a[0], b[1]) + dot(a[1], b[0]))


NN = ((1,), (0,))
NT = ((1,), (1,))


def pair(ref):
    return ref[0], ref[1]


def y_forward_kernel(field_ref, table_ref, out_ref):
    planes, lines, length = field_ref.shape[1:]
    half = length // 2
    rows = planes * lines
    lower = field_ref[0, :, :, :half].reshape(rows, half)
    upper = field_ref[0, :, :, half:].reshape(rows, half)
    folded = jnp.where(pl.program_id(1) == 0, lower + upper, lower - upper)
    waves = product((table_ref[0, 0], table_ref[0, 1]), split(folded), NT)
    out_ref[:, 0] = waves.reshape(out_ref.shape[0], -1, rows)


def y_inverse_kernel(norm, spectrum_ref, table_ref, out_ref):
    devices, _, waves, rows = spectrum_ref.shape
    planes, lines, length = out_ref.shape[1:]
    half = length // 2
    even, odd = (
        product(
            split(spectrum_ref[p * devices // 2 : (p + 1) * devices // 2, 0].reshape(half, rows).T),
            (table_ref[p, 0], table_ref[p, 1]),
            NN,
        )
        for p in range(2)
    )
    out_ref[0, :, :, :half] = ((even + odd) * norm).reshape(planes, lines, half)
    out_ref[0, :, :, half:] = ((even - odd) * norm).reshape(planes, lines, half)


def x_kernel(
    walls, rate_ref, square_y_ref, square_x_ref, even_ref, odd_ref, odd_turned_ref,
    received_ref, out_ref, sum_ref, difference_ref,
):
    devices, _, waves, rows = received_ref.shape
    groups = devices // walls
    scalar = pl.program_id(0)
    half = even_ref.shape[1]
    lines = 2 * half // groups
    planes = rows // lines
    count = walls * planes
    lower = lax.broadcasted_iota(jnp.int32, (waves, 128), 1) < lines

    def paired(a, b):
        return (
            jnp.where(lower, a, pltpu.roll(b, lines, 1)),
            jnp.where(lower, pltpu.roll(a, lines, 1), b),
        )

    for w in range(walls):
        for p in range(planes // 2):
            lanes = slice(128 * p, 128 * (p + 1))
            top = (w * planes + 2 * p) * waves
            for j in range(groups // 4):
                first, second = w * groups + 2 * j, w * groups + 2 * j + groups // 2
                a, b = received_ref[first, 0, :, lanes], received_ref[first + 1, 0, :, lanes]
                c, d = received_ref[second, 0, :, lanes], received_ref[second + 1, 0, :, lanes]
                columns = slice(128 * j, 128 * (j + 1))
                for target, pieces in (
                    (sum_ref, paired(a + c, b + d)),
                    (difference_ref, paired(a - c, b - d)),
                ):
                    target[top : top + waves, columns] = pieces[0]
                    target[top + waves : top + 2 * waves, columns] = pieces[1]

    sum_ref[...] = product(split(sum_ref[...]), pair(even_ref), NN)
    difference_ref[...] = product(split(difference_ref[...]), pair(odd_ref), NN)

    rates = [rate_ref[scalar, z] for z in range(count)]
    damping_y = [jnp.exp(-rate * square_y_ref[...]) for rate in rates]
    for parity, ref in enumerate((sum_ref, difference_ref)):
        for j in range(half // 128):
            columns = slice(128 * j, 128 * (j + 1))
            square_x = square_x_ref[parity : parity + 1, columns]
            damping = [jnp.exp(-rate * square_x) * dy for rate, dy in zip(rates, damping_y)]
            field = [ref[z * waves : (z + 1) * waves, columns] for z in range(count)]
            for step in range(STEPS):
                updated = []
                for z in range(count):
                    around = field[z - 1] if z > 0 else None
                    if z + 1 < count:
                        around = field[z + 1] if around is None else around + field[z + 1]
                    value = (1.0 - 2.0 * rates[z]) * field[z]
                    if around is not None:
                        value = value + rates[z] * around
                    updated.append(damping[z] * value)
                field = updated
            for z in range(count):
                ref[z * waves : (z + 1) * waves, columns] = field[z]

    even = product(split(sum_ref[...]), pair(even_ref), NN)
    odd = product(split(difference_ref[...]), pair(odd_turned_ref), NN)
    sum_ref[...] = even + odd
    difference_ref[...] = even - odd

    for w in range(walls):
        for p in range(planes // 2):
            lanes = slice(128 * p, 128 * (p + 1))
            top = (w * planes + 2 * p) * waves
            for j in range(groups // 4):
                columns = slice(128 * j, 128 * (j + 1))
                first = w * groups + 2 * j
                for ref, target in ((sum_ref, first), (difference_ref, first + groups // 2)):
                    a, b = paired(
                        ref[top : top + waves, columns],
                        ref[top + waves : top + 2 * waves, columns],
                    )
                    out_ref[target, 0, :, lanes] = a
                    out_ref[target + 1, 0, :, lanes] = b


PARAMS = pltpu.CompilerParams(vmem_limit_bytes=VMEM_BYTES)
VMEM = pl.BlockSpec(memory_space=pltpu.VMEM)


def cost(terms, total):
    return pl.CostEstimate(flops=2 * terms, bytes_accessed=total, transcendentals=0)


def with_kernels(fields, rates, walls, square_y, square_x, ky, kx):
    scalars, planes, lines, length = fields.shape
    groups = lax.axis_size("row")
    devices = walls * groups
    waves = length // devices
    rows = planes * lines
    half = length // 2
    y_table = np.stack([ky[0].transpose(0, 2, 1), ky[2]])
    blocks = jax.ShapeDtypeStruct((devices, scalars, waves, rows), jnp.float32)
    total = 8 * scalars * rows * length + 2 * length * length
    work = 3 * scalars * rows * length * half
    field_block = pl.BlockSpec((1, planes, lines, length), lambda s, *_: (s, 0, 0, 0))
    spectrum_block = pl.BlockSpec((devices, 1, waves, rows), lambda s: (0, s, 0, 0))

    spectrum = pl.pallas_call(
        y_forward_kernel,
        grid=(scalars, 2),
        in_specs=[field_block, pl.BlockSpec((1, 2, half, half), lambda s, p: (p, 0, 0, 0))],
        out_specs=pl.BlockSpec((devices // 2, 1, waves, rows), lambda s, p: (p, s, 0, 0)),
        out_shape=blocks,
        compiler_params=PARAMS,
        cost_estimate=cost(work, total),
        name="y_forward",
    )(fields, y_table)
    filtered = pl.pallas_call(
        functools.partial(x_kernel, walls),
        grid=(scalars,),
        in_specs=[pl.BlockSpec(memory_space=pltpu.SMEM)] + [VMEM] * 5 + [spectrum_block],
        out_specs=spectrum_block,
        out_shape=blocks,
        scratch_shapes=[pltpu.VMEM((walls * planes * waves, kx[0].shape[1]), jnp.float32)] * 2,
        compiler_params=PARAMS,
        cost_estimate=cost(2 * work, total),
        name="x_filter",
    )(rates, square_y, square_x, *kx, exchange(spectrum))
    return pl.pallas_call(
        functools.partial(y_inverse_kernel, 1.0 / (length * lines * groups)),
        grid=(scalars,),
        in_specs=[spectrum_block, VMEM],
        out_specs=field_block,
        out_shape=jax.ShapeDtypeStruct(fields.shape, jnp.float32),
        compiler_params=PARAMS,
        cost_estimate=cost(work, total),
        name="y_inverse",
    )(exchange(filtered), y_table)


def exchange(blocks):
    return lax.all_to_all(blocks, AXES, split_axis=0, concat_axis=0, tiled=True)


def with_arrays(fields, rates, walls, square_y, square_x, ky, kx):
    scalars, planes, lines, length = fields.shape
    groups = lax.axis_size("row")
    devices = walls * groups
    waves = length // devices
    count = walls * planes
    dot = functools.partial(jnp.matmul, precision=lax.Precision.HIGHEST)

    def whole(table):
        table = jnp.asarray(table)
        return table[0].astype(jnp.float32) + table[1].astype(jnp.float32)

    def forward(value, group):
        half = value.shape[-1] // 2
        a, b = value[..., :half], value[..., half:]
        return jnp.concatenate([dot(a + b, whole(group[0])), dot(a - b, whole(group[1]))], axis=-1)

    def inverse(value, group):
        half = value.shape[-1] // 2
        even, odd = dot(value[..., :half], whole(group[0])), dot(value[..., half:], whole(group[2]))
        return jnp.concatenate([even + odd, even - odd], axis=-1)

    results = []
    for s in range(scalars):
        spectral = forward(fields[s], ky).reshape(planes * lines, devices, waves)
        received = exchange(spectral.transpose(1, 2, 0))
        received = received.reshape(walls, groups, waves, planes, lines).transpose(0, 3, 2, 1, 4)
        field = forward(received.reshape(count, waves, groups * lines), kx)
        rate = rates[s][:, None, None]
        damping = jnp.exp(-rate * (square_y + square_x.reshape(1, -1)))
        for step in range(STEPS):
            padded = jnp.pad(field, ((1, 1), (0, 0), (0, 0)))
            field = damping * (field + rate * (padded[2:] + padded[:-2] - 2.0 * field))
        back = inverse(field, kx).reshape(walls, planes, waves, groups, lines).transpose(0, 3, 2, 1, 4)
        spectrum = exchange(back.reshape(devices, waves, planes * lines)).reshape(length, -1)
        results.append(inverse(spectrum.T, ky).reshape(planes, lines, length))
    return jnp.stack(results) * (1.0 / (length * groups * lines))


def signed_square(waves, length):
    signed = jnp.where(waves > length // 2, waves - length, waves)
    scaled = 2.0 * np.pi / length * signed.astype(jnp.float32)
    return scaled * scaled


def per_device(ky, kx, thermal_scalars, conductive_number):
    scalars, planes, lines, length = thermal_scalars.shape
    walls, groups = lax.axis_size("wall"), lax.axis_size("row")
    length_x = lines * groups
    devices = walls * groups
    waves = length // devices
    rates = lax.all_gather(conductive_number, "wall", axis=1, tiled=True)
    place = lax.axis_index(AXES) * waves + jnp.arange(waves, dtype=jnp.int32)
    order = 2 * (place % (length // 2)) + place // (length // 2)
    square_y = signed_square(order, length)[:, None]
    waves_x = jnp.stack([jnp.arange(0, length_x, 2), jnp.arange(1, length_x, 2)])
    square_x = signed_square(waves_x, length_x)
    aligned = lines == 64 and planes % 2 == 0 and waves % 8 == 0 and groups % 4 == 0
    run = with_kernels if aligned else with_arrays
    return run(thermal_scalars, rates, walls, square_y, square_x, ky, kx)


def solution(mesh):
    def run(thermal_scalars, conductive_number):
        ky = tables(thermal_scalars.shape[3])
        kx = tables(thermal_scalars.shape[2])
        return jax.shard_map(
            functools.partial(per_device, ky, kx),
            mesh=mesh,
            in_specs=(P(None, "wall", "row", None), P(None, "wall")),
            out_specs=P(None, "wall", "row", None),
            check_vma=False,
        )(thermal_scalars, conductive_number)

    return run
```

```python
import functools

import jax
import jax.numpy as jnp
import ml_dtypes
import numpy as np
from jax import lax
from jax.experimental import pallas as pl
from jax.experimental.pallas import tpu as pltpu
from jax.sharding import PartitionSpec as P

STEPS = 3
AXES = ("wall", "row")
LEVELS = 4
VMEM_BYTES = 40 * 1024 * 1024


def cas_table(length, offset, step):
    half = length // 2
    samples = np.arange(half, dtype=np.int64)
    waves = offset + step * np.arange(half, dtype=np.int64)
    angle = (samples[:, None] * waves[None, :] % length) * (2.0 * np.pi / length)
    return np.cos(angle) + np.sin(angle)


def split_table(table):
    high = table.astype(np.float32).astype(ml_dtypes.bfloat16)
    low = (table - high.astype(np.float64)).astype(np.float32).astype(ml_dtypes.bfloat16)
    return np.stack([high, low])


def table_of(length):
    return np.stack([split_table(cas_table(length, parity, 2).T) for parity in range(2)])


def split(value):
    high = value.astype(jnp.bfloat16)
    low = (value - high.astype(jnp.float32)).astype(jnp.bfloat16)
    return high, low


def product(a, b, dims):
    dot = functools.partial(
        lax.dot_general, dimension_numbers=(dims, ((), ())), preferred_element_type=jnp.float32
    )
    return dot(a[0], b[0]) + (dot(a[0], b[1]) + dot(a[1], b[0]))


NN = ((1,), (0,))
NT = ((1,), (1,))


def slot(w, r, groups):
    per_level = groups // LEVELS
    return (w * per_level + r % per_level) * LEVELS + r // per_level


def y_forward_kernel(field_ref, table_ref, out_ref):
    planes, lines, length = field_ref.shape[1:]
    half = length // 2
    rows = planes * lines
    lower = field_ref[0, :, :, :half].reshape(rows, half)
    upper = field_ref[0, :, :, half:].reshape(rows, half)
    folded = jnp.where(pl.program_id(1) == 0, lower + upper, lower - upper)
    waves = product((table_ref[0, 0], table_ref[0, 1]), split(folded), NT)
    out_ref[:, 0] = waves.reshape(out_ref.shape[0], -1, rows)


def y_inverse_kernel(norm, spectrum_ref, table_ref, out_ref):
    devices, _, waves, rows = spectrum_ref.shape
    planes, lines, length = out_ref.shape[1:]
    half = length // 2
    even, odd = (
        product(
            split(spectrum_ref[p * devices // 2 : (p + 1) * devices // 2, 0].reshape(half, rows).T),
            (table_ref[p, 0], table_ref[p, 1]),
            NN,
        )
        for p in range(2)
    )
    out_ref[0, :, :, :half] = ((even + odd) * norm).reshape(planes, lines, half)
    out_ref[0, :, :, half:] = ((even - odd) * norm).reshape(planes, lines, half)


def x_kernel(
    walls, rate_ref, square_y_ref, square_x_ref, table_ref, received_ref, out_ref, sum_ref,
    difference_ref,
):
    devices, _, waves, rows = received_ref.shape
    groups = devices // walls
    scalar = pl.program_id(0)
    half = table_ref.shape[3]
    even_pair, odd_pair = ((table_ref[p, 0], table_ref[p, 1]) for p in range(2))
    lines = 2 * half // groups
    planes = rows // lines
    count = walls * planes
    lower = lax.broadcasted_iota(jnp.int32, (waves, 128), 1) < lines

    def paired(a, b):
        return (
            jnp.where(lower, a, pltpu.roll(b, lines, 1)),
            jnp.where(lower, pltpu.roll(a, lines, 1), b),
        )

    for w in range(walls):
        for p in range(planes // 2):
            lanes = slice(128 * p, 128 * (p + 1))
            top = (w * planes + 2 * p) * waves
            for j in range(groups // 4):
                first, second = 2 * j, 2 * j + groups // 2
                a, b, c, d = (
                    received_ref[slot(w, r, groups), 0, :, lanes]
                    for r in (first, first + 1, second, second + 1)
                )
                columns = slice(128 * j, 128 * (j + 1))
                for target, pieces in (
                    (sum_ref, paired(a + c, b + d)),
                    (difference_ref, paired(a - c, b - d)),
                ):
                    target[top : top + waves, columns] = pieces[0]
                    target[top + waves : top + 2 * waves, columns] = pieces[1]

    sum_ref[...] = product(split(sum_ref[...]), even_pair, NT)
    difference_ref[...] = product(split(difference_ref[...]), odd_pair, NT)

    rates = [rate_ref[scalar, z] for z in range(count)]
    damping_y = [jnp.exp(-rate * square_y_ref[...]) for rate in rates]
    for parity, ref in enumerate((sum_ref, difference_ref)):
        for j in range(half // 128):
            columns = slice(128 * j, 128 * (j + 1))
            square_x = square_x_ref[parity : parity + 1, columns]
            damping = [jnp.exp(-rate * square_x) * dy for rate, dy in zip(rates, damping_y)]
            field = [ref[z * waves : (z + 1) * waves, columns] for z in range(count)]
            for step in range(STEPS):
                updated = []
                for z in range(count):
                    around = field[z - 1] if z > 0 else None
                    if z + 1 < count:
                        around = field[z + 1] if around is None else around + field[z + 1]
                    value = (1.0 - 2.0 * rates[z]) * field[z]
                    if around is not None:
                        value = value + rates[z] * around
                    updated.append(damping[z] * value)
                field = updated
            for z in range(count):
                ref[z * waves : (z + 1) * waves, columns] = field[z]

    even = product(split(sum_ref[...]), even_pair, NN)
    odd = product(split(difference_ref[...]), odd_pair, NN)
    sum_ref[...] = even + odd
    difference_ref[...] = even - odd

    for w in range(walls):
        for p in range(planes // 2):
            lanes = slice(128 * p, 128 * (p + 1))
            top = (w * planes + 2 * p) * waves
            for j in range(groups // 4):
                columns = slice(128 * j, 128 * (j + 1))
                for ref, r in ((sum_ref, 2 * j), (difference_ref, 2 * j + groups // 2)):
                    a, b = paired(
                        ref[top : top + waves, columns],
                        ref[top + waves : top + 2 * waves, columns],
                    )
                    out_ref[slot(w, r, groups), 0, :, lanes] = a
                    out_ref[slot(w, r + 1, groups), 0, :, lanes] = b


PARAMS = pltpu.CompilerParams(vmem_limit_bytes=VMEM_BYTES)
WIDE_PARAMS = pltpu.CompilerParams(vmem_limit_bytes=60 * 1024 * 1024)
VMEM = pl.BlockSpec(memory_space=pltpu.VMEM)


def cost(terms, total):
    return pl.CostEstimate(flops=2 * terms, bytes_accessed=total, transcendentals=0)


def with_kernels(fields, rates, walls, square_y, square_x, y_table, x_table):
    scalars, planes, lines, length = fields.shape
    groups = lax.axis_size("row")
    devices = walls * groups
    waves = length // devices
    rows = planes * lines
    half = length // 2
    blocks = jax.ShapeDtypeStruct((devices, scalars, waves, rows), jnp.float32)
    total = 8 * scalars * rows * length + 2 * length * length
    work = 3 * scalars * rows * length * half
    field_block = pl.BlockSpec((1, planes, lines, length), lambda s, *_: (s, 0, 0, 0))
    spectrum_block = pl.BlockSpec((devices, 1, waves, rows), lambda s: (0, s, 0, 0))

    spectrum = pl.pallas_call(
        y_forward_kernel,
        grid=(scalars, 2),
        in_specs=[field_block, pl.BlockSpec((1, 2, half, half), lambda s, p: (p, 0, 0, 0))],
        out_specs=pl.BlockSpec((devices // 2, 1, waves, rows), lambda s, p: (p, s, 0, 0)),
        out_shape=blocks,
        compiler_params=WIDE_PARAMS,
        cost_estimate=cost(work, total),
        name="y_forward",
    )(fields, y_table)
    filtered = pl.pallas_call(
        functools.partial(x_kernel, walls),
        grid=(scalars,),
        in_specs=[pl.BlockSpec(memory_space=pltpu.SMEM)] + [VMEM] * 3 + [spectrum_block],
        out_specs=spectrum_block,
        out_shape=blocks,
        scratch_shapes=[pltpu.VMEM((walls * planes * waves, x_table.shape[3]), jnp.float32)] * 2,
        compiler_params=PARAMS,
        cost_estimate=cost(2 * work, total),
        name="x_filter",
    )(rates, square_y, square_x, x_table, exchange(spectrum))
    return pl.pallas_call(
        functools.partial(y_inverse_kernel, 1.0 / (length * lines * groups)),
        grid=(scalars,),
        in_specs=[spectrum_block, VMEM],
        out_specs=field_block,
        out_shape=jax.ShapeDtypeStruct(fields.shape, jnp.float32),
        compiler_params=PARAMS,
        cost_estimate=cost(work, total),
        name="y_inverse",
    )(exchange(filtered), y_table)


def exchange(blocks):
    walls, groups = lax.axis_size("wall"), lax.axis_size("row")
    members = {slot(w, r, groups): w * groups + r for w in range(walls) for r in range(groups)}
    return lax.all_to_all(
        blocks, AXES, split_axis=0, concat_axis=0, tiled=True,
        axis_index_groups=[[members[i] for i in range(len(members))]],
    )


def with_arrays(fields, rates, walls, square_y, square_x, y_table, x_table):
    scalars, planes, lines, length = fields.shape
    groups = lax.axis_size("row")
    devices = walls * groups
    waves = length // devices
    count = walls * planes
    order = np.array([slot(w, r, groups) for w in range(walls) for r in range(groups)])
    dot = functools.partial(jnp.matmul, precision=lax.Precision.HIGHEST)

    def whole(table):
        table = jnp.asarray(table)
        return table[0].astype(jnp.float32) + table[1].astype(jnp.float32)

    def forward(value, table):
        half = value.shape[-1] // 2
        a, b = value[..., :half], value[..., half:]
        return jnp.concatenate([dot(a + b, whole(table[0]).T), dot(a - b, whole(table[1]).T)], axis=-1)

    def inverse(value, table):
        half = value.shape[-1] // 2
        even, odd = dot(value[..., :half], whole(table[0])), dot(value[..., half:], whole(table[1]))
        return jnp.concatenate([even + odd, even - odd], axis=-1)

    results = []
    for s in range(scalars):
        spectral = forward(fields[s], y_table).reshape(planes * lines, devices, waves)
        received = exchange(spectral.transpose(1, 2, 0))[order]
        received = received.reshape(walls, groups, waves, planes, lines).transpose(0, 3, 2, 1, 4)
        field = forward(received.reshape(count, waves, groups * lines), x_table)
        rate = rates[s][:, None, None]
        damping = jnp.exp(-rate * (square_y + square_x.reshape(1, -1)))
        for step in range(STEPS):
            padded = jnp.pad(field, ((1, 1), (0, 0), (0, 0)))
            field = damping * (field + rate * (padded[2:] + padded[:-2] - 2.0 * field))
        back = inverse(field, x_table).reshape(walls, planes, waves, groups, lines)
        back = back.transpose(0, 3, 2, 1, 4).reshape(devices, waves, planes * lines)
        spectrum = exchange(back[np.argsort(order)]).reshape(length, -1)
        results.append(inverse(spectrum.T, y_table).reshape(planes, lines, length))
    return jnp.stack(results) * (1.0 / (length * groups * lines))


def signed_square(waves, length):
    signed = jnp.where(waves > length // 2, waves - length, waves)
    scaled = 2.0 * np.pi / length * signed.astype(jnp.float32)
    return scaled * scaled


def per_device(y_table, x_table, thermal_scalars, conductive_number):
    scalars, planes, lines, length = thermal_scalars.shape
    walls, groups = lax.axis_size("wall"), lax.axis_size("row")
    length_x = lines * groups
    devices = walls * groups
    waves = length // devices
    rates = lax.all_gather(conductive_number, "wall", axis=1, tiled=True)
    own = slot(lax.axis_index("wall"), lax.axis_index("row"), groups)
    place = own * waves + jnp.arange(waves, dtype=jnp.int32)
    order = 2 * (place % (length // 2)) + place // (length // 2)
    square_y = signed_square(order, length)[:, None]
    waves_x = jnp.stack([jnp.arange(0, length_x, 2), jnp.arange(1, length_x, 2)])
    square_x = signed_square(waves_x, length_x)
    aligned = lines == 64 and planes % 2 == 0 and waves % 8 == 0 and groups % 4 == 0
    run = with_kernels if aligned else with_arrays
    return run(thermal_scalars, rates, walls, square_y, square_x, y_table, x_table)


def solution(mesh):
    def run(thermal_scalars, conductive_number):
        y_table = table_of(thermal_scalars.shape[3])
        x_table = table_of(thermal_scalars.shape[2])
        return jax.shard_map(
            functools.partial(per_device, y_table, x_table),
            mesh=mesh,
            in_specs=(P(None, "wall", "row", None), P(None, "wall")),
            out_specs=P(None, "wall", "row", None),
            check_vma=False,
        )(thermal_scalars, conductive_number)

    return run
```

```python
import functools

import jax
import jax.numpy as jnp
import ml_dtypes
import numpy as np
from jax import lax
from jax.experimental import pallas as pl
from jax.experimental.pallas import tpu as pltpu
from jax.sharding import PartitionSpec as P

STEPS = 3
AXES = ("wall", "row")
LEVELS = 4
PARTS = 4
VMEM_BYTES = 40 * 1024 * 1024


def cas_table(length, offset, step):
    half = length // 2
    samples = np.arange(half, dtype=np.int64)
    waves = offset + step * np.arange(half, dtype=np.int64)
    angle = (samples[:, None] * waves[None, :] % length) * (2.0 * np.pi / length)
    return np.cos(angle) + np.sin(angle)


def split_table(table):
    high = table.astype(np.float32).astype(ml_dtypes.bfloat16)
    low = (table - high.astype(np.float64)).astype(np.float32).astype(ml_dtypes.bfloat16)
    return np.stack([high, low])


def table_of(length):
    return np.stack([split_table(cas_table(length, parity, 2).T) for parity in range(2)])


def split(value):
    high = value.astype(jnp.bfloat16)
    low = (value - high.astype(jnp.float32)).astype(jnp.bfloat16)
    return high, low


def product(a, b, dims):
    left = jnp.concatenate([a[0], a[1], a[0]], axis=dims[0][0])
    right = jnp.concatenate([b[0], b[0], b[1]], axis=dims[1][0])
    return lax.dot_general(left, right, (dims, ((), ())), preferred_element_type=jnp.float32)


NN = ((1,), (0,))
NT = ((1,), (1,))


def slot(w, r, groups):
    per_level = groups // LEVELS
    return (w * per_level + r % per_level) * LEVELS + r // per_level


def y_forward_kernel(lower_ref, upper_ref, high_ref, low_ref, out_ref):
    planes, lines, half = lower_ref.shape[1:]
    rows = planes * lines
    lower = lower_ref[0].reshape(rows, half)
    upper = upper_ref[0].reshape(rows, half)
    folded = jnp.where(pl.program_id(1) == 0, lower + upper, lower - upper)
    waves = product((high_ref[0, 0], low_ref[0, 0]), split(folded), NT)
    out_ref[:, 0] = waves.reshape(out_ref.shape[0], -1, rows)


def y_inverse_kernel(norm, *refs):
    spectrum_refs, (table_ref, out_ref) = refs[:-2], refs[-2:]
    rows = spectrum_refs[0].shape[3]
    share = len(spectrum_refs) // 2
    planes, lines, length = out_ref.shape[1:]
    half = length // 2
    even, odd = (
        product(
            split(jnp.concatenate([ref[:, 0].reshape(-1, rows) for ref in spectrum_refs[p * share : (p + 1) * share]]).T),
            (table_ref[p, 0], table_ref[p, 1]),
            NN,
        )
        for p in range(2)
    )
    out_ref[0, :, :, :half] = ((even + odd) * norm).reshape(planes, lines, half)
    out_ref[0, :, :, half:] = ((even - odd) * norm).reshape(planes, lines, half)


def x_kernel(
    walls, rate_ref, square_y_ref, square_x_ref, table_ref, *refs
):
    received_refs, (out_ref, sum_ref, difference_ref) = refs[:-3], refs[-3:]
    devices, _, waves, rows = out_ref.shape
    groups = devices // walls
    part = devices // len(received_refs)
    scalar = pl.program_id(0)
    half = table_ref.shape[3]
    even_pair, odd_pair = ((table_ref[p, 0], table_ref[p, 1]) for p in range(2))
    lines = 2 * half // groups
    planes = rows // lines
    count = walls * planes
    lower = lax.broadcasted_iota(jnp.int32, (waves, 128), 1) < lines

    def paired(a, b):
        return (
            jnp.where(lower, a, pltpu.roll(b, lines, 1)),
            jnp.where(lower, pltpu.roll(a, lines, 1), b),
        )

    for w in range(walls):
        for p in range(planes // 2):
            lanes = slice(128 * p, 128 * (p + 1))
            top = (w * planes + 2 * p) * waves
            for j in range(groups // 4):
                first, second = 2 * j, 2 * j + groups // 2
                a, b, c, d = (
                    received_refs[i // part][i % part, 0, :, lanes]
                    for i in (slot(w, r, groups) for r in (first, first + 1, second, second + 1))
                )
                columns = slice(128 * j, 128 * (j + 1))
                for target, pieces in (
                    (sum_ref, paired(a + c, b + d)),
                    (difference_ref, paired(a - c, b - d)),
                ):
                    target[top : top + waves, columns] = pieces[0]
                    target[top + waves : top + 2 * waves, columns] = pieces[1]

    sum_ref[...] = product(split(sum_ref[...]), even_pair, NT)
    difference_ref[...] = product(split(difference_ref[...]), odd_pair, NT)

    rates = [rate_ref[scalar, z] for z in range(count)]
    damping_y = [jnp.exp(-rate * square_y_ref[...]) for rate in rates]
    for parity, ref in enumerate((sum_ref, difference_ref)):
        for j in range(half // 128):
            columns = slice(128 * j, 128 * (j + 1))
            square_x = square_x_ref[parity : parity + 1, columns]
            damping = [jnp.exp(-rate * square_x) * dy for rate, dy in zip(rates, damping_y)]
            field = [ref[z * waves : (z + 1) * waves, columns] for z in range(count)]
            for step in range(STEPS):
                updated = []
                for z in range(count):
                    around = field[z - 1] if z > 0 else None
                    if z + 1 < count:
                        around = field[z + 1] if around is None else around + field[z + 1]
                    value = (1.0 - 2.0 * rates[z]) * field[z]
                    if around is not None:
                        value = value + rates[z] * around
                    updated.append(damping[z] * value)
                field = updated
            for z in range(count):
                ref[z * waves : (z + 1) * waves, columns] = field[z]

    even = product(split(sum_ref[...]), even_pair, NN)
    odd = product(split(difference_ref[...]), odd_pair, NN)
    sum_ref[...] = even + odd
    difference_ref[...] = even - odd

    for w in range(walls):
        for p in range(planes // 2):
            lanes = slice(128 * p, 128 * (p + 1))
            top = (w * planes + 2 * p) * waves
            for j in range(groups // 4):
                columns = slice(128 * j, 128 * (j + 1))
                for ref, r in ((sum_ref, 2 * j), (difference_ref, 2 * j + groups // 2)):
                    a, b = paired(
                        ref[top : top + waves, columns],
                        ref[top + waves : top + 2 * waves, columns],
                    )
                    out_ref[slot(w, r, groups), 0, :, lanes] = a
                    out_ref[slot(w, r + 1, groups), 0, :, lanes] = b


PARAMS = pltpu.CompilerParams(vmem_limit_bytes=VMEM_BYTES)
WIDE_PARAMS = pltpu.CompilerParams(vmem_limit_bytes=60 * 1024 * 1024)
VMEM = pl.BlockSpec(memory_space=pltpu.VMEM)


def cost(terms, total):
    return pl.CostEstimate(flops=2 * terms, bytes_accessed=total, transcendentals=0)


def with_kernels(fields, rates, walls, square_y, square_x, y_table, x_table):
    scalars, planes, lines, length = fields.shape
    groups = lax.axis_size("row")
    devices = walls * groups
    waves = length // devices
    rows = planes * lines
    half = length // 2
    blocks = jax.ShapeDtypeStruct((devices, scalars, waves, rows), jnp.float32)
    total = 8 * scalars * rows * length + 2 * length * length
    work = 3 * scalars * rows * length * half
    field_block = pl.BlockSpec((1, planes, lines, length), lambda s: (s, 0, 0, 0))
    spectrum_block = pl.BlockSpec((devices, 1, waves, rows), lambda s: (0, s, 0, 0))

    part_blocks = [
        pl.BlockSpec((devices // PARTS, 1, waves, rows), lambda s, i=i: (i, s, 0, 0)) for i in range(PARTS)
    ]

    spectrum = pl.pallas_call(
        y_forward_kernel,
        grid=(scalars, 2),
        in_specs=[
            pl.BlockSpec((1, planes, lines, half), lambda s, p, i=i: (s, 0, 0, i)) for i in range(2)
        ] + [
            pl.BlockSpec((1, 1, half, half), lambda s, p, i=i: (p, i, 0, 0)) for i in range(2)
        ],
        out_specs=pl.BlockSpec((devices // 2, 1, waves, rows), lambda s, p: (p, s, 0, 0)),
        out_shape=blocks,
        compiler_params=WIDE_PARAMS,
        cost_estimate=cost(work, total),
        name="y_forward",
    )(fields, fields, y_table, y_table)
    received = exchange(spectrum)
    filtered = pl.pallas_call(
        functools.partial(x_kernel, walls),
        grid=(scalars,),
        in_specs=[pl.BlockSpec(memory_space=pltpu.SMEM)] + [VMEM] * 3 + part_blocks,
        out_specs=spectrum_block,
        out_shape=blocks,
        scratch_shapes=[pltpu.VMEM((walls * planes * waves, x_table.shape[3]), jnp.float32)] * 2,
        compiler_params=PARAMS,
        cost_estimate=cost(2 * work, total),
        name="x_filter",
    )(rates, square_y, square_x, x_table, *[received] * PARTS)
    returned = exchange(filtered)
    return pl.pallas_call(
        functools.partial(y_inverse_kernel, 1.0 / (length * lines * groups)),
        grid=(scalars,),
        in_specs=part_blocks + [VMEM],
        out_specs=field_block,
        out_shape=jax.ShapeDtypeStruct(fields.shape, jnp.float32),
        compiler_params=PARAMS,
        cost_estimate=cost(work, total),
        name="y_inverse",
    )(*[returned] * PARTS, y_table)


def exchange(blocks):
    walls, groups = lax.axis_size("wall"), lax.axis_size("row")
    members = {slot(w, r, groups): w * groups + r for w in range(walls) for r in range(groups)}
    return lax.all_to_all(
        blocks, AXES, split_axis=0, concat_axis=0, tiled=True,
        axis_index_groups=[[members[i] for i in range(len(members))]],
    )


def with_arrays(fields, rates, walls, square_y, square_x, y_table, x_table):
    scalars, planes, lines, length = fields.shape
    groups = lax.axis_size("row")
    devices = walls * groups
    waves = length // devices
    count = walls * planes
    order = np.array([slot(w, r, groups) for w in range(walls) for r in range(groups)])
    dot = functools.partial(jnp.matmul, precision=lax.Precision.HIGHEST)

    def whole(table):
        table = jnp.asarray(table)
        return table[0].astype(jnp.float32) + table[1].astype(jnp.float32)

    def forward(value, table):
        half = value.shape[-1] // 2
        a, b = value[..., :half], value[..., half:]
        return jnp.concatenate([dot(a + b, whole(table[0]).T), dot(a - b, whole(table[1]).T)], axis=-1)

    def inverse(value, table):
        half = value.shape[-1] // 2
        even, odd = dot(value[..., :half], whole(table[0])), dot(value[..., half:], whole(table[1]))
        return jnp.concatenate([even + odd, even - odd], axis=-1)

    results = []
    for s in range(scalars):
        spectral = forward(fields[s], y_table).reshape(planes * lines, devices, waves)
        received = exchange(spectral.transpose(1, 2, 0))[order]
        received = received.reshape(walls, groups, waves, planes, lines).transpose(0, 3, 2, 1, 4)
        field = forward(received.reshape(count, waves, groups * lines), x_table)
        rate = rates[s][:, None, None]
        damping = jnp.exp(-rate * (square_y + square_x.reshape(1, -1)))
        for step in range(STEPS):
            padded = jnp.pad(field, ((1, 1), (0, 0), (0, 0)))
            field = damping * (field + rate * (padded[2:] + padded[:-2] - 2.0 * field))
        back = inverse(field, x_table).reshape(walls, planes, waves, groups, lines)
        back = back.transpose(0, 3, 2, 1, 4).reshape(devices, waves, planes * lines)
        spectrum = exchange(back[np.argsort(order)]).reshape(length, -1)
        results.append(inverse(spectrum.T, y_table).reshape(planes, lines, length))
    return jnp.stack(results) * (1.0 / (length * groups * lines))


def signed_square(waves, length):
    signed = jnp.where(waves > length // 2, waves - length, waves)
    scaled = 2.0 * np.pi / length * signed.astype(jnp.float32)
    return scaled * scaled


def per_device(y_table, x_table, thermal_scalars, conductive_number):
    scalars, planes, lines, length = thermal_scalars.shape
    walls, groups = lax.axis_size("wall"), lax.axis_size("row")
    length_x = lines * groups
    devices = walls * groups
    waves = length // devices
    rates = lax.all_gather(conductive_number, "wall", axis=1, tiled=True)
    own = slot(lax.axis_index("wall"), lax.axis_index("row"), groups)
    place = own * waves + jnp.arange(waves, dtype=jnp.int32)
    order = 2 * (place % (length // 2)) + place // (length // 2)
    square_y = signed_square(order, length)[:, None]
    waves_x = jnp.stack([jnp.arange(0, length_x, 2), jnp.arange(1, length_x, 2)])
    square_x = signed_square(waves_x, length_x)
    aligned = lines == 64 and planes % 2 == 0 and waves % 8 == 0 and groups % 4 == 0
    run = with_kernels if aligned else with_arrays
    return run(thermal_scalars, rates, walls, square_y, square_x, y_table, x_table)


def solution(mesh):
    def run(thermal_scalars, conductive_number):
        y_table = table_of(thermal_scalars.shape[3])
        x_table = table_of(thermal_scalars.shape[2])
        return jax.shard_map(
            functools.partial(per_device, y_table, x_table),
            mesh=mesh,
            in_specs=(P(None, "wall", "row", None), P(None, "wall")),
            out_specs=P(None, "wall", "row", None),
            check_vma=False,
        )(thermal_scalars, conductive_number)

    return run
```

```python
import functools

import jax
import jax.numpy as jnp
import ml_dtypes
import numpy as np
from jax import lax
from jax.experimental import pallas as pl
from jax.experimental.pallas import tpu as pltpu
from jax.sharding import PartitionSpec as P

STEPS = 3
AXES = ("wall", "row")
LEVELS = 4
VMEM_BYTES = 40 * 1024 * 1024


def wave_order(place, length):
    quarter = length // 4
    even = jnp.where(place < quarter, 4 * place, 4 * (place - quarter) + 2)
    return jnp.where(place < 2 * quarter, even, 2 * (place - 2 * quarter) + 1)


def cas_table(length, first, step):
    size = length // step
    waves = first + step * np.arange(size, dtype=np.int64)
    samples = np.arange(size, dtype=np.int64)
    angle = (waves[:, None] * samples[None, :] % length) * (2.0 * np.pi / length)
    table = np.cos(angle) + np.sin(angle)
    high = table.astype(np.float32).astype(ml_dtypes.bfloat16)
    low = (table - high.astype(np.float64)).astype(np.float32).astype(ml_dtypes.bfloat16)
    return np.stack([high, low])


def tables_of(length):
    even = np.stack([cas_table(length, 0, 4), cas_table(length, 2, 4)])
    return even, cas_table(length, 1, 2)


def fold(q):
    low, high = q[0] + q[2], q[1] + q[3]
    return low + high, low - high, q[0] - q[2], q[1] - q[3]


def unfold(first, second, third, fourth):
    low, high = first + second, first - second
    return low + third, high + fourth, low - third, high - fourth


def split(value):
    high = value.astype(jnp.bfloat16)
    low = (value - high.astype(jnp.float32)).astype(jnp.bfloat16)
    return high, low


def product(a, b, dims):
    left = jnp.concatenate([a[0], a[1], a[0]], axis=dims[0][0])
    right = jnp.concatenate([b[0], b[0], b[1]], axis=dims[1][0])
    return lax.dot_general(left, right, (dims, ((), ())), preferred_element_type=jnp.float32)


NN = ((1,), (0,))
NT = ((1,), (1,))


def part_tables(even_ref, odd_ref):
    return [(even_ref[p, 0], even_ref[p, 1]) for p in range(2)] + [(odd_ref[0], odd_ref[1])]


def part_ranges(total):
    return (0, total // 4), (total // 4, total // 2), (total // 2, total)


def slot(w, r, groups):
    per_level = groups // LEVELS
    return (w * per_level + r % per_level) * LEVELS + r // per_level


def y_forward_kernel(
    field_hbm, even_hbm, odd_hbm, out_hbm, even_ref, odd_ref, field_ref, out_ref, in_sem, table_sem,
    out_sem,
):
    scalars, planes, lines, length = field_ref.shape
    rows = planes * lines
    quarter = length // 4
    loads = [
        pltpu.make_async_copy(field_hbm.at[s], field_ref.at[s], in_sem.at[s]) for s in range(scalars)
    ]
    even_load = pltpu.make_async_copy(even_hbm, even_ref, table_sem.at[0])
    odd_load = pltpu.make_async_copy(odd_hbm, odd_ref, table_sem.at[1])
    loads[0].start()
    even_load.start()
    odd_load.start()
    for load in loads[1:]:
        load.start()
    stores = []
    for s in range(scalars):
        loads[s].wait()
        lines_of = [
            field_ref[s, :, :, q * quarter : (q + 1) * quarter].reshape(rows, quarter) for q in range(4)
        ]
        first, second, third, fourth = fold(lines_of)
        parts = [first, second, jnp.concatenate([third, fourth], axis=1)]
        for p, (low, high) in enumerate(part_ranges(out_ref.shape[0])):
            if s == 0 and p == 0:
                even_load.wait()
            if s == 0 and p == 2:
                odd_load.wait()
            table = (odd_ref[0], odd_ref[1]) if p == 2 else (even_ref[p, 0], even_ref[p, 1])
            waves = product(table, split(parts[p]), NT)
            out_ref[low:high, s] = waves.reshape(high - low, -1, rows)
            store = pltpu.make_async_copy(
                out_ref.at[pl.ds(low, high - low), s],
                out_hbm.at[pl.ds(low, high - low), s],
                out_sem.at[s, p],
            )
            store.start()
            stores.append(store)
    for store in stores:
        store.wait()


def y_inverse_kernel(norm, even_ref, odd_ref, spectrum_ref, out_hbm, out_ref, out_sem):
    devices, scalars, waves, rows = spectrum_ref.shape
    planes, lines, length = out_ref.shape[1:]
    quarter = length // 4
    tables = part_tables(even_ref, odd_ref)
    stores = []
    for s in range(scalars):
        first, second, third = (
            product(split(spectrum_ref[low:high, s].reshape(-1, rows).T), table, NN)
            for table, (low, high) in zip(tables, part_ranges(devices))
        )
        quarters = unfold(first * norm, second * norm, third[:, :quarter] * norm, third[:, quarter:] * norm)
        for q, value in enumerate(quarters):
            out_ref[s, :, :, q * quarter : (q + 1) * quarter] = value.reshape(planes, lines, quarter)
        for z in range(planes):
            store = pltpu.make_async_copy(out_ref.at[s, z], out_hbm.at[s, z], out_sem.at[s, z])
            store.start()
            stores.append(store)
    for store in stores:
        store.wait()


def x_kernel(
    walls, rate_ref, square_y_ref, square_x_ref, even_ref, odd_ref, received_ref, out_ref, *line_refs
):
    devices, scalars, waves, rows = received_ref.shape
    groups = devices // walls
    length = line_refs[0].shape[1]
    quarter = length // 4
    lines = length // groups
    planes = rows // lines
    count = walls * planes
    lower = lax.broadcasted_iota(jnp.int32, (waves, 128), 1) < lines
    tables = part_tables(even_ref, odd_ref)
    ranges = part_ranges(length)

    def paired(a, b):
        return (
            jnp.where(lower, a, pltpu.roll(b, lines, 1)),
            jnp.where(lower, pltpu.roll(a, lines, 1), b),
        )

    def tiles():
        for w in range(walls):
            for p in range(planes // 2):
                yield w, slice(128 * p, 128 * (p + 1)), (w * planes + 2 * p) * waves

    def forward(s):
        line_ref = line_refs[s]
        for w, lanes, top in tiles():
            for i in range(groups // 8):
                left, right = (
                    fold([
                        received_ref[slot(w, groups // 4 * q + 2 * i + side, groups), s, :, lanes]
                        for q in range(4)
                    ])
                    for side in range(2)
                )
                for q in range(4):
                    a, b = paired(left[q], right[q])
                    columns = slice(quarter * q + 128 * i, quarter * q + 128 * (i + 1))
                    line_ref[top : top + waves, columns] = a
                    line_ref[top + waves : top + 2 * waves, columns] = b
        for table, (low, high) in zip(tables, ranges):
            line_ref[:, low:high] = product(split(line_ref[:, low:high]), table, NT)

    def diffuse(s):
        line_ref = line_refs[s]
        rates = [rate_ref[s, z] for z in range(count)]
        damping_y = [jnp.exp(-rate * square_y_ref[...]) for rate in rates]
        for j in range(length // 128):
            columns = slice(128 * j, 128 * (j + 1))
            square_x = square_x_ref[:, columns]
            damping = [jnp.exp(-rate * square_x) * dy for rate, dy in zip(rates, damping_y)]
            field = [line_ref[z * waves : (z + 1) * waves, columns] for z in range(count)]
            for step in range(STEPS):
                updated = []
                for z in range(count):
                    value = (1.0 - 2.0 * rates[z]) * field[z]
                    if z == 0:
                        around = field[1]
                    elif z == count - 1:
                        around = field[z - 1]
                    else:
                        around = field[z - 1] + field[z + 1]
                    updated.append(damping[z] * (value + rates[z] * around))
                field = updated
            for z in range(count):
                line_ref[z * waves : (z + 1) * waves, columns] = field[z]

    def inverse(s):
        line_ref = line_refs[s]
        first, second, third = (
            product(split(line_ref[:, low:high]), table, NN) for table, (low, high) in zip(tables, ranges)
        )
        quarters = unfold(first, second, third[:, :quarter], third[:, quarter:])
        for q, value in enumerate(quarters):
            line_ref[:, q * quarter : (q + 1) * quarter] = value
        for w, lanes, top in tiles():
            for j in range(groups // 2):
                columns = slice(128 * j, 128 * (j + 1))
                a, b = paired(
                    line_ref[top : top + waves, columns],
                    line_ref[top + waves : top + 2 * waves, columns],
                )
                out_ref[slot(w, 2 * j, groups), s, :, lanes] = a
                out_ref[slot(w, 2 * j + 1, groups), s, :, lanes] = b

    for phase in (forward, diffuse, inverse):
        for s in range(scalars):
            phase(s)


PARAMS = pltpu.CompilerParams(vmem_limit_bytes=VMEM_BYTES)
VMEM = pl.BlockSpec(memory_space=pltpu.VMEM)
ANY = pl.BlockSpec(memory_space=pl.ANY)


def cost(terms, total):
    return pl.CostEstimate(flops=2 * terms, bytes_accessed=total, transcendentals=0)


def with_kernels(fields, rates, walls, square_y, square_x, tables):
    scalars, planes, lines, length = fields.shape
    groups = lax.axis_size("row")
    devices = walls * groups
    waves = length // devices
    rows = planes * lines
    even, odd = tables
    blocks = jax.ShapeDtypeStruct((devices, scalars, waves, rows), jnp.float32)
    shapes = [jax.ShapeDtypeStruct(t.shape, jnp.bfloat16) for t in tables]
    total = 8 * scalars * rows * length
    work = 9 * scalars * rows * length * length // 8

    spectrum, even, odd = pl.pallas_call(
        y_forward_kernel,
        in_specs=[ANY] * 3,
        out_specs=[ANY, VMEM, VMEM],
        out_shape=[blocks, *shapes],
        scratch_shapes=[
            pltpu.VMEM(fields.shape, jnp.float32),
            pltpu.VMEM(blocks.shape, jnp.float32),
            pltpu.SemaphoreType.DMA((scalars,)),
            pltpu.SemaphoreType.DMA((2,)),
            pltpu.SemaphoreType.DMA((scalars, 3)),
        ],
        compiler_params=PARAMS,
        cost_estimate=cost(work, total),
        name="y_forward",
    )(fields, even, odd)
    filtered = pl.pallas_call(
        functools.partial(x_kernel, walls),
        in_specs=[pl.BlockSpec(memory_space=pltpu.SMEM)] + [VMEM] * 5,
        out_specs=VMEM,
        out_shape=blocks,
        scratch_shapes=[pltpu.VMEM((walls * planes * waves, lines * groups), jnp.float32)] * scalars,
        compiler_params=PARAMS,
        cost_estimate=cost(2 * work, total),
        name="x_filter",
    )(rates, square_y, square_x, even, odd, exchange(spectrum))
    return pl.pallas_call(
        functools.partial(y_inverse_kernel, 1.0 / (length * lines * groups)),
        in_specs=[VMEM] * 3,
        out_specs=ANY,
        out_shape=jax.ShapeDtypeStruct(fields.shape, jnp.float32),
        scratch_shapes=[
            pltpu.VMEM(fields.shape, jnp.float32),
            pltpu.SemaphoreType.DMA((scalars, planes)),
        ],
        compiler_params=PARAMS,
        cost_estimate=cost(work, total),
        name="y_inverse",
    )(even, odd, exchange(filtered))


def exchange(blocks):
    walls, groups = lax.axis_size("wall"), lax.axis_size("row")
    members = {slot(w, r, groups): w * groups + r for w in range(walls) for r in range(groups)}
    return lax.all_to_all(
        blocks, AXES, split_axis=0, concat_axis=0, tiled=True,
        axis_index_groups=[[members[i] for i in range(len(members))]],
    )


def with_arrays(fields, rates, walls, square_y, square_x, y_tables, x_tables):
    scalars, planes, lines, length = fields.shape
    groups = lax.axis_size("row")
    devices = walls * groups
    waves = length // devices
    count = walls * planes
    order = np.array([slot(w, r, groups) for w in range(walls) for r in range(groups)])
    dot = functools.partial(jnp.matmul, precision=lax.Precision.HIGHEST)

    def whole(tables):
        pairs = [jnp.asarray(t).astype(jnp.float32) for t in (*tables[0], tables[1])]
        return [t[0] + t[1] for t in pairs]

    def forward(value, tables):
        first, second, third, fourth = fold(jnp.split(value, 4, axis=-1))
        parts = (first, second, jnp.concatenate([third, fourth], axis=-1))
        return jnp.concatenate([dot(v, t.T) for v, t in zip(parts, whole(tables))], axis=-1)

    def inverse(value, tables):
        parts = jnp.split(value, [value.shape[-1] // 4, value.shape[-1] // 2], axis=-1)
        first, second, third = (dot(v, t) for v, t in zip(parts, whole(tables)))
        return jnp.concatenate(unfold(first, second, *jnp.split(third, 2, axis=-1)), axis=-1)

    results = []
    for s in range(scalars):
        spectral = forward(fields[s], y_tables).reshape(planes * lines, devices, waves)
        received = exchange(spectral.transpose(1, 2, 0))[order]
        received = received.reshape(walls, groups, waves, planes, lines).transpose(0, 3, 2, 1, 4)
        field = forward(received.reshape(count, waves, groups * lines), x_tables)
        rate = rates[s][:, None, None]
        damping = jnp.exp(-rate * (square_y + square_x))
        for step in range(STEPS):
            padded = jnp.pad(field, ((1, 1), (0, 0), (0, 0)))
            field = damping * (field + rate * (padded[2:] + padded[:-2] - 2.0 * field))
        back = inverse(field, x_tables).reshape(walls, planes, waves, groups, lines)
        back = back.transpose(0, 3, 2, 1, 4).reshape(devices, waves, planes * lines)
        spectrum = exchange(back[np.argsort(order)]).reshape(length, -1)
        results.append(inverse(spectrum.T, y_tables).reshape(planes, lines, length))
    return jnp.stack(results) * (1.0 / (length * groups * lines))


def signed_square(waves, length):
    signed = jnp.where(waves > length // 2, waves - length, waves)
    scaled = 2.0 * np.pi / length * signed.astype(jnp.float32)
    return scaled * scaled


def per_device(thermal_scalars, conductive_number):
    scalars, planes, lines, length = thermal_scalars.shape
    walls, groups = lax.axis_size("wall"), lax.axis_size("row")
    length_x = lines * groups
    waves = length // (walls * groups)
    rates = lax.all_gather(conductive_number, "wall", axis=1, tiled=True)
    own = slot(lax.axis_index("wall"), lax.axis_index("row"), groups)
    place = own * waves + jnp.arange(waves, dtype=jnp.int32)
    square_y = signed_square(wave_order(place, length), length)[:, None]
    square_x = signed_square(wave_order(jnp.arange(length_x), length_x), length_x)[None, :]
    fits = lines == 64 and planes % 2 == 0 and waves % 8 == 0 and groups % 8 == 0
    if fits and length == length_x and walls * groups % 4 == 0:
        return with_kernels(thermal_scalars, rates, walls, square_y, square_x, tables_of(length))
    return with_arrays(
        thermal_scalars, rates, walls, square_y, square_x, tables_of(length), tables_of(length_x)
    )


def solution(mesh):
    return jax.shard_map(
        per_device,
        mesh=mesh,
        in_specs=(P(None, "wall", "row", None), P(None, "wall")),
        out_specs=P(None, "wall", "row", None),
        check_vma=False,
    )
```

```python
import functools

import jax
import jax.numpy as jnp
import ml_dtypes
import numpy as np
from jax import lax
from jax.experimental import pallas as pl
from jax.experimental.pallas import tpu as pltpu
from jax.sharding import PartitionSpec as P

STEPS = 3
AXES = ("wall", "row")
LEVELS = 4
MIB = 1024 * 1024
TABLE_BYTES = 13 * MIB


def wave_order(place, length):
    quarter = length // 4
    even = jnp.where(place < quarter, 4 * place, 4 * (place - quarter) + 2)
    return jnp.where(place < 2 * quarter, even, 2 * (place - 2 * quarter) + 1)


def cas_table(length, first, step):
    size = length // step
    waves = first + step * np.arange(size, dtype=np.int64)
    samples = np.arange(size, dtype=np.int64)
    angle = (waves[:, None] * samples[None, :] % length) * (2.0 * np.pi / length)
    table = np.cos(angle) + np.sin(angle)
    high = table.astype(np.float32).astype(ml_dtypes.bfloat16)
    low = (table - high.astype(np.float64)).astype(np.float32).astype(ml_dtypes.bfloat16)
    return np.stack([high, low])


def tables_of(length):
    even = np.stack([cas_table(length, 0, 4), cas_table(length, 2, 4)])
    return even, cas_table(length, 1, 2)


def fold(q):
    low, high = q[0] + q[2], q[1] + q[3]
    return low + high, low - high, q[0] - q[2], q[1] - q[3]


def unfold(first, second, third, fourth):
    low, high = first + second, first - second
    return low + third, high + fourth, low - third, high - fourth


def split(value):
    high = value.astype(jnp.bfloat16)
    low = (value - high.astype(jnp.float32)).astype(jnp.bfloat16)
    return high, low


def product(a, b, dims):
    left = jnp.concatenate([a[0], a[1], a[0]], axis=dims[0][0])
    right = jnp.concatenate([b[0], b[0], b[1]], axis=dims[1][0])
    return lax.dot_general(left, right, (dims, ((), ())), preferred_element_type=jnp.float32)


NN = ((1,), (0,))
NT = ((1,), (1,))


def stacked(tables, rows):
    even, odd = tables
    top = np.concatenate([even[0], even[1]], axis=2)
    rest = np.zeros((2, rows - top.shape[1] - odd.shape[1], odd.shape[2]), odd.dtype)
    return np.concatenate([top, odd, rest], axis=1)


def part_tables(table_ref):
    quarter = table_ref.shape[2] // 2
    places = (
        (slice(0, quarter), slice(0, quarter)),
        (slice(0, quarter), slice(quarter, 2 * quarter)),
        (slice(quarter, 3 * quarter), slice(0, 2 * quarter)),
    )
    return [(table_ref[0, rows, columns], table_ref[1, rows, columns]) for rows, columns in places]


def table_loads(table_hbm, table_ref, sem):
    quarter = table_ref.shape[2] // 2
    return [
        pltpu.make_async_copy(table_hbm.at[:, rows], table_ref.at[:, rows], sem.at[i])
        for i, rows in enumerate((pl.ds(0, quarter), pl.ds(quarter, 2 * quarter)))
    ]


def part_ranges(total):
    return (0, total // 4), (total // 4, total // 2), (total // 2, total)


def slot(w, r, groups):
    per_level = groups // LEVELS
    return (w * per_level + r % per_level) * LEVELS + r // per_level


def y_forward_kernel(
    field_hbm, table_hbm, out_hbm, field_ref, table_ref, out_ref, in_sem, table_sem, out_sem
):
    scalars, planes, lines, length = field_ref.shape
    rows = planes * lines
    quarter = length // 4
    ranges = part_ranges(out_ref.shape[0])
    loads = [
        pltpu.make_async_copy(field_hbm.at[s], field_ref.at[s], in_sem.at[s]) for s in range(scalars)
    ]
    even_load, odd_load = table_loads(table_hbm, table_ref, table_sem)
    loads[0].start()
    even_load.start()
    odd_load.start()
    for load in loads[1:]:
        load.start()
    stores = []
    for s in range(scalars):
        loads[s].wait()
        first, second, third, fourth = fold([
            field_ref[s, :, :, q * quarter : (q + 1) * quarter].reshape(rows, quarter) for q in range(4)
        ])
        parts = [split(v) for v in (first, second, jnp.concatenate([third, fourth], axis=1))]
        for p in (0, 1, 2) if s == 0 else (2, 0, 1):
            if s == 0 and p == 0:
                even_load.wait()
            if s == 0 and p == 2:
                odd_load.wait()
            low, high = ranges[p]
            out_ref[low:high, s] = product(part_tables(table_ref)[p], parts[p], NT).reshape(high - low, -1, rows)
            store = pltpu.make_async_copy(
                out_ref.at[pl.ds(low, high - low), s],
                out_hbm.at[pl.ds(low, high - low), s],
                out_sem.at[s, p],
            )
            store.start()
            stores.append(store)
    for store in stores:
        store.wait()


def y_inverse_kernel(
    norm, spectrum_ref, table_hbm, out_hbm, table_ref, out_ref, table_sem, out_sem
):
    devices, scalars, waves, rows = spectrum_ref.shape
    planes, lines, length = out_ref.shape[1:]
    quarter = length // 4
    even_load, odd_load = table_loads(table_hbm, table_ref, table_sem)
    even_load.start()
    odd_load.start()
    turned = [
        [
            split((spectrum_ref[low:high, s].reshape(-1, rows) * norm).T)
            for low, high in part_ranges(devices)
        ]
        for s in range(scalars)
    ]
    even_load.wait()
    odd_load.wait()
    stores = []
    for s in range(scalars):
        first, second, third = (
            product(part, table, NN) for part, table in zip(turned[s], part_tables(table_ref))
        )
        for z in range(planes):
            own = slice(z * lines, (z + 1) * lines)
            quarters = unfold(first[own], second[own], third[own, :quarter], third[own, quarter:])
            for q, value in enumerate(quarters):
                out_ref[s, z, :, q * quarter : (q + 1) * quarter] = value
            store = pltpu.make_async_copy(out_ref.at[s, z], out_hbm.at[s, z], out_sem.at[s, z])
            store.start()
            stores.append(store)
    for store in stores:
        store.wait()


def x_kernel(
    walls, rate_ref, square_y_ref, square_x_ref, received_ref, table_hbm, out_ref, table_ref,
    table_sem, *line_refs
):
    even_load, odd_load = table_loads(table_hbm, table_ref, table_sem)
    even_load.start()
    odd_load.start()
    devices, scalars, waves, rows = received_ref.shape
    groups = devices // walls
    length = line_refs[0].shape[1]
    quarter = length // 4
    lines = length // groups
    planes = rows // lines
    count = walls * planes
    lower = lax.broadcasted_iota(jnp.int32, (waves, 128), 1) < lines
    ranges = part_ranges(length)

    def paired(a, b):
        return (
            jnp.where(lower, a, pltpu.roll(b, lines, 1)),
            jnp.where(lower, pltpu.roll(a, lines, 1), b),
        )

    def tiles():
        for w in range(walls):
            for p in range(planes // 2):
                yield w, slice(128 * p, 128 * (p + 1)), (w * planes + 2 * p) * waves

    def arrange(s):
        line_ref = line_refs[s]
        for w, lanes, top in tiles():
            for i in range(groups // 8):
                left, right = (
                    fold([
                        received_ref[slot(w, groups // 4 * q + 2 * i + side, groups), s, :, lanes]
                        for q in range(4)
                    ])
                    for side in range(2)
                )
                for q in range(4):
                    a, b = paired(left[q], right[q])
                    columns = slice(quarter * q + 128 * i, quarter * q + 128 * (i + 1))
                    line_ref[top : top + waves, columns] = a
                    line_ref[top + waves : top + 2 * waves, columns] = b

    def forward(s):
        line_ref = line_refs[s]
        for table, (low, high) in zip(part_tables(table_ref), ranges):
            line_ref[:, low:high] = product(split(line_ref[:, low:high]), table, NT)

    def diffuse(s):
        line_ref = line_refs[s]
        rates = [rate_ref[s, z] for z in range(count)]
        damping_y = [jnp.exp(-rate * square_y_ref[...]) for rate in rates]
        for j in range(length // 128):
            columns = slice(128 * j, 128 * (j + 1))
            square_x = square_x_ref[:, columns]
            damping = [jnp.exp(-rate * square_x) * dy for rate, dy in zip(rates, damping_y)]
            field = [line_ref[z * waves : (z + 1) * waves, columns] for z in range(count)]
            for step in range(STEPS):
                updated = []
                for z in range(count):
                    value = (1.0 - 2.0 * rates[z]) * field[z]
                    if z == 0:
                        around = field[1]
                    elif z == count - 1:
                        around = field[z - 1]
                    else:
                        around = field[z - 1] + field[z + 1]
                    updated.append(damping[z] * (value + rates[z] * around))
                field = updated
            for z in range(count):
                line_ref[z * waves : (z + 1) * waves, columns] = field[z]

    def inverse(s):
        line_ref = line_refs[s]
        first, second, third = (
            product(split(line_ref[:, low:high]), table, NN)
            for table, (low, high) in zip(part_tables(table_ref), ranges)
        )
        quarters = unfold(first, second, third[:, :quarter], third[:, quarter:])
        for q, value in enumerate(quarters):
            line_ref[:, q * quarter : (q + 1) * quarter] = value

    def send(s):
        line_ref = line_refs[s]
        for w, lanes, top in tiles():
            for j in range(groups // 2):
                columns = slice(128 * j, 128 * (j + 1))
                a, b = paired(
                    line_ref[top : top + waves, columns],
                    line_ref[top + waves : top + 2 * waves, columns],
                )
                out_ref[slot(w, 2 * j, groups), s, :, lanes] = a
                out_ref[slot(w, 2 * j + 1, groups), s, :, lanes] = b

    for s in range(scalars):
        arrange(s)
    even_load.wait()
    odd_load.wait()
    phases = (forward, diffuse, inverse, send)
    for time in range(len(phases) + scalars - 1):
        for s in reversed(range(scalars)):
            if 0 <= time - s < len(phases):
                phases[time - s](s)


def grant(mebibytes):
    return pltpu.CompilerParams(vmem_limit_bytes=mebibytes * MIB)


VMEM = pl.BlockSpec(memory_space=pltpu.VMEM)
ANY = pl.BlockSpec(memory_space=pl.ANY)


def cost(terms, total):
    return pl.CostEstimate(flops=2 * terms, bytes_accessed=total, transcendentals=0)


def with_kernels(fields, rates, walls, square_y, square_x, tables):
    scalars, planes, lines, length = fields.shape
    groups = lax.axis_size("row")
    devices = walls * groups
    waves = length // devices
    rows = planes * lines
    blocks = jax.ShapeDtypeStruct((devices, scalars, waves, rows), jnp.float32)
    total = 8 * scalars * rows * length
    work = 9 * scalars * rows * length * length // 8
    table = stacked(tables, TABLE_BYTES // (2 * length))
    table_scratch = pltpu.VMEM((2, 3 * length // 4, length // 2), jnp.bfloat16)

    spectrum = pl.pallas_call(
        y_forward_kernel,
        in_specs=[ANY] * 2,
        out_specs=ANY,
        out_shape=blocks,
        scratch_shapes=[
            pltpu.VMEM(fields.shape, jnp.float32),
            table_scratch,
            pltpu.VMEM(blocks.shape, jnp.float32),
            pltpu.SemaphoreType.DMA((scalars,)),
            pltpu.SemaphoreType.DMA((2,)),
            pltpu.SemaphoreType.DMA((scalars, 3)),
        ],
        compiler_params=grant(60),
        cost_estimate=cost(work, total),
        name="y_forward",
    )(fields, table)
    filtered = pl.pallas_call(
        functools.partial(x_kernel, walls),
        in_specs=[pl.BlockSpec(memory_space=pltpu.SMEM)] + [VMEM] * 3 + [ANY],
        out_specs=VMEM,
        out_shape=blocks,
        scratch_shapes=[
            table_scratch,
            pltpu.SemaphoreType.DMA((2,)),
            *[pltpu.VMEM((walls * planes * waves, lines * groups), jnp.float32)] * scalars,
        ],
        compiler_params=grant(48),
        cost_estimate=cost(2 * work, total),
        name="x_filter",
    )(rates, square_y, square_x, exchange(spectrum), table)
    return pl.pallas_call(
        functools.partial(y_inverse_kernel, 1.0 / (length * lines * groups)),
        in_specs=[VMEM, ANY],
        out_specs=ANY,
        out_shape=jax.ShapeDtypeStruct(fields.shape, jnp.float32),
        scratch_shapes=[
            table_scratch,
            pltpu.VMEM(fields.shape, jnp.float32),
            pltpu.SemaphoreType.DMA((2,)),
            pltpu.SemaphoreType.DMA((scalars, planes)),
        ],
        compiler_params=grant(48),
        cost_estimate=cost(work, total),
        name="y_inverse",
    )(exchange(filtered), table)


def exchange(blocks):
    walls, groups = lax.axis_size("wall"), lax.axis_size("row")
    members = {slot(w, r, groups): w * groups + r for w in range(walls) for r in range(groups)}
    return lax.all_to_all(
        blocks, AXES, split_axis=0, concat_axis=0, tiled=True,
        axis_index_groups=[[members[i] for i in range(len(members))]],
    )


def with_arrays(fields, rates, walls, square_y, square_x, y_tables, x_tables):
    scalars, planes, lines, length = fields.shape
    groups = lax.axis_size("row")
    devices = walls * groups
    waves = length // devices
    count = walls * planes
    order = np.array([slot(w, r, groups) for w in range(walls) for r in range(groups)])
    dot = functools.partial(jnp.matmul, precision=lax.Precision.HIGHEST)

    def whole(tables):
        pairs = [jnp.asarray(t).astype(jnp.float32) for t in (*tables[0], tables[1])]
        return [t[0] + t[1] for t in pairs]

    def forward(value, tables):
        first, second, third, fourth = fold(jnp.split(value, 4, axis=-1))
        parts = (first, second, jnp.concatenate([third, fourth], axis=-1))
        return jnp.concatenate([dot(v, t.T) for v, t in zip(parts, whole(tables))], axis=-1)

    def inverse(value, tables):
        parts = jnp.split(value, [value.shape[-1] // 4, value.shape[-1] // 2], axis=-1)
        first, second, third = (dot(v, t) for v, t in zip(parts, whole(tables)))
        return jnp.concatenate(unfold(first, second, *jnp.split(third, 2, axis=-1)), axis=-1)

    results = []
    for s in range(scalars):
        spectral = forward(fields[s], y_tables).reshape(planes * lines, devices, waves)
        received = exchange(spectral.transpose(1, 2, 0))[order]
        received = received.reshape(walls, groups, waves, planes, lines).transpose(0, 3, 2, 1, 4)
        field = forward(received.reshape(count, waves, groups * lines), x_tables)
        rate = rates[s][:, None, None]
        damping = jnp.exp(-rate * (square_y + square_x))
        for step in range(STEPS):
            padded = jnp.pad(field, ((1, 1), (0, 0), (0, 0)))
            field = damping * (field + rate * (padded[2:] + padded[:-2] - 2.0 * field))
        back = inverse(field, x_tables).reshape(walls, planes, waves, groups, lines)
        back = back.transpose(0, 3, 2, 1, 4).reshape(devices, waves, planes * lines)
        spectrum = exchange(back[np.argsort(order)]).reshape(length, -1)
        results.append(inverse(spectrum.T, y_tables).reshape(planes, lines, length))
    return jnp.stack(results) * (1.0 / (length * groups * lines))


def signed_square(waves, length):
    signed = jnp.where(waves > length // 2, waves - length, waves)
    scaled = 2.0 * np.pi / length * signed.astype(jnp.float32)
    return scaled * scaled


def per_device(thermal_scalars, conductive_number):
    scalars, planes, lines, length = thermal_scalars.shape
    walls, groups = lax.axis_size("wall"), lax.axis_size("row")
    length_x = lines * groups
    waves = length // (walls * groups)
    rates = lax.all_gather(conductive_number, "wall", axis=1, tiled=True)
    own = slot(lax.axis_index("wall"), lax.axis_index("row"), groups)
    place = own * waves + jnp.arange(waves, dtype=jnp.int32)
    square_y = signed_square(wave_order(place, length), length)[:, None]
    square_x = signed_square(wave_order(jnp.arange(length_x), length_x), length_x)[None, :]
    fits = lines == 64 and planes % 2 == 0 and waves % 8 == 0 and groups % 8 == 0
    if fits and length == length_x and walls * groups % 4 == 0:
        return with_kernels(thermal_scalars, rates, walls, square_y, square_x, tables_of(length))
    return with_arrays(
        thermal_scalars, rates, walls, square_y, square_x, tables_of(length), tables_of(length_x)
    )


def solution(mesh):
    return jax.shard_map(
        per_device,
        mesh=mesh,
        in_specs=(P(None, "wall", "row", None), P(None, "wall")),
        out_specs=P(None, "wall", "row", None),
        check_vma=False,
    )
```

```python
import functools

import jax
import jax.numpy as jnp
import ml_dtypes
import numpy as np
from jax import lax
from jax.experimental import pallas as pl
from jax.experimental.pallas import tpu as pltpu
from jax.sharding import PartitionSpec as P

STEPS = 3
AXES = ("wall", "row")
LEVELS = 4
MIB = 1024 * 1024
TABLE_BYTES = 13 * MIB


def wave_order(place, length):
    quarter = length // 4
    even = jnp.where(place < quarter, 4 * place, 4 * (place - quarter) + 2)
    return jnp.where(place < 2 * quarter, even, 2 * (place - 2 * quarter) + 1)


def cas_table(length, first, step):
    size = length // step
    waves = first + step * np.arange(size, dtype=np.int64)
    samples = np.arange(size, dtype=np.int64)
    angle = (waves[:, None] * samples[None, :] % length) * (2.0 * np.pi / length)
    table = np.cos(angle) + np.sin(angle)
    high = table.astype(np.float32).astype(ml_dtypes.bfloat16)
    low = (table - high.astype(np.float64)).astype(np.float32).astype(ml_dtypes.bfloat16)
    return np.stack([high, low])


def tables_of(length):
    even = np.stack([cas_table(length, 0, 4), cas_table(length, 2, 4)])
    return even, cas_table(length, 1, 2)


def fold(q):
    low, high = q[0] + q[2], q[1] + q[3]
    return low + high, low - high, q[0] - q[2], q[1] - q[3]


def unfold(first, second, third, fourth):
    low, high = first + second, first - second
    return low + third, high + fourth, low - third, high - fourth


def split(value):
    high = value.astype(jnp.bfloat16)
    low = (value - high.astype(jnp.float32)).astype(jnp.bfloat16)
    return high, low


def product(a, b, dims):
    left = jnp.concatenate([a[0], a[1], a[0]], axis=dims[0][0])
    right = jnp.concatenate([b[0], b[0], b[1]], axis=dims[1][0])
    return lax.dot_general(left, right, (dims, ((), ())), preferred_element_type=jnp.float32)


NN = ((1,), (0,))
NT = ((1,), (1,))


def stacked(tables, rows):
    even, odd = tables
    top = np.concatenate([even[0], even[1]], axis=2)
    rest = np.zeros((2, rows - top.shape[1] - odd.shape[1], odd.shape[2]), odd.dtype)
    return np.concatenate([top, odd, rest], axis=1)


def part_tables(table_ref):
    quarter = table_ref.shape[2] // 2
    places = (
        (slice(0, quarter), slice(0, quarter)),
        (slice(0, quarter), slice(quarter, 2 * quarter)),
        (slice(quarter, 3 * quarter), slice(0, 2 * quarter)),
    )
    return [(table_ref[0, rows, columns], table_ref[1, rows, columns]) for rows, columns in places]


def table_loads(table_hbm, table_ref, sem):
    quarter = table_ref.shape[2] // 2
    return [
        pltpu.make_async_copy(table_hbm.at[:, rows], table_ref.at[:, rows], sem.at[i])
        for i, rows in enumerate((pl.ds(0, quarter), pl.ds(quarter, 2 * quarter)))
    ]


def part_ranges(total):
    return (0, total // 4), (total // 4, total // 2), (total // 2, total)


def slot(w, r, groups):
    per_level = groups // LEVELS
    return (w * per_level + r % per_level) * LEVELS + r // per_level


def y_forward_kernel(
    field_hbm, table_hbm, out_hbm, field_ref, table_ref, out_ref, in_sem, table_sem, out_sem
):
    scalars, planes, lines, length = field_ref.shape
    rows = planes * lines
    quarter = length // 4
    ranges = part_ranges(out_ref.shape[0])
    loads = [
        pltpu.make_async_copy(field_hbm.at[s], field_ref.at[s], in_sem.at[s]) for s in range(scalars)
    ]
    even_load, odd_load = table_loads(table_hbm, table_ref, table_sem)
    loads[0].start()
    even_load.start()
    odd_load.start()
    for load in loads[1:]:
        load.start()
    stores = []
    for s in range(scalars):
        loads[s].wait()
        first, second, third, fourth = fold([
            field_ref[s, :, :, q * quarter : (q + 1) * quarter].reshape(rows, quarter) for q in range(4)
        ])
        parts = [split(v) for v in (first, second, jnp.concatenate([third, fourth], axis=1))]
        for p in (0, 1, 2) if s == 0 else (2, 0, 1):
            if s == 0 and p == 0:
                even_load.wait()
            if s == 0 and p == 2:
                odd_load.wait()
            low, high = ranges[p]
            out_ref[low:high, s] = product(part_tables(table_ref)[p], parts[p], NT).reshape(high - low, -1, rows)
            store = pltpu.make_async_copy(
                out_ref.at[pl.ds(low, high - low), s],
                out_hbm.at[pl.ds(low, high - low), s],
                out_sem.at[s, p],
            )
            store.start()
            stores.append(store)
    for store in stores:
        store.wait()


def hold_kernel(after_hbm, table_hbm, table_ref, sem):
    del after_hbm
    load = pltpu.make_async_copy(table_hbm.at[:, pl.ds(0, table_ref.shape[1])], table_ref, sem.at[0])
    load.start()
    load.wait()


def y_inverse_kernel(norm, table_ref, spectrum_ref, out_hbm, out_ref, out_sem):
    devices, scalars, waves, rows = spectrum_ref.shape
    planes, lines, length = out_ref.shape[1:]
    quarter = length // 4
    tables = part_tables(table_ref)
    stores = []
    for s in range(scalars):
        first, second, third = (
            product(split(spectrum_ref[low:high, s].reshape(-1, rows).T), table, NN)
            for table, (low, high) in zip(tables, part_ranges(devices))
        )
        quarters = unfold(first * norm, second * norm, third[:, :quarter] * norm, third[:, quarter:] * norm)
        for q, value in enumerate(quarters):
            out_ref[s, :, :, q * quarter : (q + 1) * quarter] = value.reshape(planes, lines, quarter)
        for z in range(planes):
            store = pltpu.make_async_copy(out_ref.at[s, z], out_hbm.at[s, z], out_sem.at[s, z])
            store.start()
            stores.append(store)
    for store in stores:
        store.wait()


def x_kernel(
    walls, rate_ref, square_y_ref, square_x_ref, table_ref, received_ref, out_ref, *line_refs
):
    devices, scalars, waves, rows = received_ref.shape
    groups = devices // walls
    length = line_refs[0].shape[1]
    quarter = length // 4
    lines = length // groups
    planes = rows // lines
    count = walls * planes
    lower = lax.broadcasted_iota(jnp.int32, (waves, 128), 1) < lines
    tables = part_tables(table_ref)
    ranges = part_ranges(length)

    def paired(a, b):
        return (
            jnp.where(lower, a, pltpu.roll(b, lines, 1)),
            jnp.where(lower, pltpu.roll(a, lines, 1), b),
        )

    def tiles():
        for w in range(walls):
            for p in range(planes // 2):
                yield w, slice(128 * p, 128 * (p + 1)), (w * planes + 2 * p) * waves

    def forward(s):
        line_ref = line_refs[s]
        for w, lanes, top in tiles():
            for i in range(groups // 8):
                left, right = (
                    fold([
                        received_ref[slot(w, groups // 4 * q + 2 * i + side, groups), s, :, lanes]
                        for q in range(4)
                    ])
                    for side in range(2)
                )
                for q in range(4):
                    a, b = paired(left[q], right[q])
                    columns = slice(quarter * q + 128 * i, quarter * q + 128 * (i + 1))
                    line_ref[top : top + waves, columns] = a
                    line_ref[top + waves : top + 2 * waves, columns] = b
        for table, (low, high) in zip(tables, ranges):
            line_ref[:, low:high] = product(split(line_ref[:, low:high]), table, NT)

    def diffuse(s):
        line_ref = line_refs[s]
        rates = [rate_ref[s, z] for z in range(count)]
        damping_y = [jnp.exp(-rate * square_y_ref[...]) for rate in rates]
        for j in range(length // 128):
            columns = slice(128 * j, 128 * (j + 1))
            square_x = square_x_ref[:, columns]
            damping = [jnp.exp(-rate * square_x) * dy for rate, dy in zip(rates, damping_y)]
            field = [line_ref[z * waves : (z + 1) * waves, columns] for z in range(count)]
            for step in range(STEPS):
                updated = []
                for z in range(count):
                    value = (1.0 - 2.0 * rates[z]) * field[z]
                    if z == 0:
                        around = field[1]
                    elif z == count - 1:
                        around = field[z - 1]
                    else:
                        around = field[z - 1] + field[z + 1]
                    updated.append(damping[z] * (value + rates[z] * around))
                field = updated
            for z in range(count):
                line_ref[z * waves : (z + 1) * waves, columns] = field[z]

    def inverse(s):
        line_ref = line_refs[s]
        first, second, third = (
            product(split(line_ref[:, low:high]), table, NN) for table, (low, high) in zip(tables, ranges)
        )
        quarters = unfold(first, second, third[:, :quarter], third[:, quarter:])
        for q, value in enumerate(quarters):
            line_ref[:, q * quarter : (q + 1) * quarter] = value
        for w, lanes, top in tiles():
            for j in range(groups // 2):
                columns = slice(128 * j, 128 * (j + 1))
                a, b = paired(
                    line_ref[top : top + waves, columns],
                    line_ref[top + waves : top + 2 * waves, columns],
                )
                out_ref[slot(w, 2 * j, groups), s, :, lanes] = a
                out_ref[slot(w, 2 * j + 1, groups), s, :, lanes] = b

    for phase in (forward, diffuse, inverse):
        for s in range(scalars):
            phase(s)


def grant(mebibytes):
    return pltpu.CompilerParams(vmem_limit_bytes=mebibytes * MIB)


VMEM = pl.BlockSpec(memory_space=pltpu.VMEM)
ANY = pl.BlockSpec(memory_space=pl.ANY)


def cost(terms, total):
    return pl.CostEstimate(flops=2 * terms, bytes_accessed=total, transcendentals=0)


def with_kernels(fields, rates, walls, square_y, square_x, tables):
    scalars, planes, lines, length = fields.shape
    groups = lax.axis_size("row")
    devices = walls * groups
    waves = length // devices
    rows = planes * lines
    blocks = jax.ShapeDtypeStruct((devices, scalars, waves, rows), jnp.float32)
    total = 8 * scalars * rows * length
    work = 9 * scalars * rows * length * length // 8
    table = stacked(tables, TABLE_BYTES // (2 * length))
    table_shape = (2, 3 * length // 4, length // 2)

    spectrum = pl.pallas_call(
        y_forward_kernel,
        in_specs=[ANY] * 2,
        out_specs=ANY,
        out_shape=blocks,
        scratch_shapes=[
            pltpu.VMEM(fields.shape, jnp.float32),
            pltpu.VMEM(table_shape, jnp.bfloat16),
            pltpu.VMEM(blocks.shape, jnp.float32),
            pltpu.SemaphoreType.DMA((scalars,)),
            pltpu.SemaphoreType.DMA((2,)),
            pltpu.SemaphoreType.DMA((scalars, 3)),
        ],
        compiler_params=grant(60),
        cost_estimate=cost(work, total),
        name="y_forward",
    )(fields, table)
    held = pl.pallas_call(
        hold_kernel,
        in_specs=[ANY] * 2,
        out_specs=VMEM,
        out_shape=jax.ShapeDtypeStruct(table_shape, jnp.bfloat16),
        scratch_shapes=[pltpu.SemaphoreType.DMA((1,))],
        compiler_params=grant(48),
        cost_estimate=cost(0, 2 * MIB),
        name="hold",
    )(spectrum[0, 0, :8, :128], table)
    filtered = pl.pallas_call(
        functools.partial(x_kernel, walls),
        in_specs=[pl.BlockSpec(memory_space=pltpu.SMEM)] + [VMEM] * 4,
        out_specs=VMEM,
        out_shape=blocks,
        scratch_shapes=[pltpu.VMEM((walls * planes * waves, lines * groups), jnp.float32)] * scalars,
        compiler_params=grant(40),
        cost_estimate=cost(2 * work, total),
        name="x_filter",
    )(rates, square_y, square_x, held, exchange(spectrum))
    return pl.pallas_call(
        functools.partial(y_inverse_kernel, 1.0 / (length * lines * groups)),
        in_specs=[VMEM] * 2,
        out_specs=ANY,
        out_shape=jax.ShapeDtypeStruct(fields.shape, jnp.float32),
        scratch_shapes=[
            pltpu.VMEM(fields.shape, jnp.float32),
            pltpu.SemaphoreType.DMA((scalars, planes)),
        ],
        compiler_params=grant(40),
        cost_estimate=cost(work, total),
        name="y_inverse",
    )(held, exchange(filtered))


def exchange(blocks):
    walls, groups = lax.axis_size("wall"), lax.axis_size("row")
    members = {slot(w, r, groups): w * groups + r for w in range(walls) for r in range(groups)}
    return lax.all_to_all(
        blocks, AXES, split_axis=0, concat_axis=0, tiled=True,
        axis_index_groups=[[members[i] for i in range(len(members))]],
    )


def with_arrays(fields, rates, walls, square_y, square_x, y_tables, x_tables):
    scalars, planes, lines, length = fields.shape
    groups = lax.axis_size("row")
    devices = walls * groups
    waves = length // devices
    count = walls * planes
    order = np.array([slot(w, r, groups) for w in range(walls) for r in range(groups)])
    dot = functools.partial(jnp.matmul, precision=lax.Precision.HIGHEST)

    def whole(tables):
        pairs = [jnp.asarray(t).astype(jnp.float32) for t in (*tables[0], tables[1])]
        return [t[0] + t[1] for t in pairs]

    def forward(value, tables):
        first, second, third, fourth = fold(jnp.split(value, 4, axis=-1))
        parts = (first, second, jnp.concatenate([third, fourth], axis=-1))
        return jnp.concatenate([dot(v, t.T) for v, t in zip(parts, whole(tables))], axis=-1)

    def inverse(value, tables):
        parts = jnp.split(value, [value.shape[-1] // 4, value.shape[-1] // 2], axis=-1)
        first, second, third = (dot(v, t) for v, t in zip(parts, whole(tables)))
        return jnp.concatenate(unfold(first, second, *jnp.split(third, 2, axis=-1)), axis=-1)

    results = []
    for s in range(scalars):
        spectral = forward(fields[s], y_tables).reshape(planes * lines, devices, waves)
        received = exchange(spectral.transpose(1, 2, 0))[order]
        received = received.reshape(walls, groups, waves, planes, lines).transpose(0, 3, 2, 1, 4)
        field = forward(received.reshape(count, waves, groups * lines), x_tables)
        rate = rates[s][:, None, None]
        damping = jnp.exp(-rate * (square_y + square_x))
        for step in range(STEPS):
            padded = jnp.pad(field, ((1, 1), (0, 0), (0, 0)))
            field = damping * (field + rate * (padded[2:] + padded[:-2] - 2.0 * field))
        back = inverse(field, x_tables).reshape(walls, planes, waves, groups, lines)
        back = back.transpose(0, 3, 2, 1, 4).reshape(devices, waves, planes * lines)
        spectrum = exchange(back[np.argsort(order)]).reshape(length, -1)
        results.append(inverse(spectrum.T, y_tables).reshape(planes, lines, length))
    return jnp.stack(results) * (1.0 / (length * groups * lines))


def signed_square(waves, length):
    signed = jnp.where(waves > length // 2, waves - length, waves)
    scaled = 2.0 * np.pi / length * signed.astype(jnp.float32)
    return scaled * scaled


def per_device(thermal_scalars, conductive_number):
    scalars, planes, lines, length = thermal_scalars.shape
    walls, groups = lax.axis_size("wall"), lax.axis_size("row")
    length_x = lines * groups
    waves = length // (walls * groups)
    rates = lax.all_gather(conductive_number, "wall", axis=1, tiled=True)
    own = slot(lax.axis_index("wall"), lax.axis_index("row"), groups)
    place = own * waves + jnp.arange(waves, dtype=jnp.int32)
    square_y = signed_square(wave_order(place, length), length)[:, None]
    square_x = signed_square(wave_order(jnp.arange(length_x), length_x), length_x)[None, :]
    fits = lines == 64 and planes % 2 == 0 and waves % 8 == 0 and groups % 8 == 0
    if fits and length == length_x and walls * groups % 4 == 0:
        return with_kernels(thermal_scalars, rates, walls, square_y, square_x, tables_of(length))
    return with_arrays(
        thermal_scalars, rates, walls, square_y, square_x, tables_of(length), tables_of(length_x)
    )


def solution(mesh):
    return jax.shard_map(
        per_device,
        mesh=mesh,
        in_specs=(P(None, "wall", "row", None), P(None, "wall")),
        out_specs=P(None, "wall", "row", None),
        check_vma=False,
    )
```

```python
import functools

import jax
import jax.numpy as jnp
import ml_dtypes
import numpy as np
from jax import lax
from jax.experimental import pallas as pl
from jax.experimental.pallas import tpu as pltpu
from jax.sharding import PartitionSpec as P

STEPS = 3
HEIGHT = 16
AXES = ("wall", "row")
LEVELS = 4
MIB = 1024 * 1024
TABLE_BYTES = 13 * MIB


def wave_order(place, length):
    quarter = length // 4
    even = jnp.where(place < quarter, 4 * place, 4 * (place - quarter) + 2)
    return jnp.where(place < 2 * quarter, even, 2 * (place - 2 * quarter) + 1)


def cas_table(length, first, step):
    size = length // step
    waves = first + step * np.arange(size, dtype=np.int64)
    samples = np.arange(size, dtype=np.int64)
    angle = (waves[:, None] * samples[None, :] % length) * (2.0 * np.pi / length)
    table = np.cos(angle) + np.sin(angle)
    high = table.astype(np.float32).astype(ml_dtypes.bfloat16)
    low = (table - high.astype(np.float64)).astype(np.float32).astype(ml_dtypes.bfloat16)
    return np.stack([high, low])


def tables_of(length):
    even = np.stack([cas_table(length, 0, 4), cas_table(length, 2, 4)])
    return even, cas_table(length, 1, 2)


def fold(q):
    low, high = q[0] + q[2], q[1] + q[3]
    return low + high, low - high, q[0] - q[2], q[1] - q[3]


def unfold(first, second, third, fourth):
    low, high = first + second, first - second
    return low + third, high + fourth, low - third, high - fourth


def split(value):
    high = value.astype(jnp.bfloat16)
    low = (value - high.astype(jnp.float32)).astype(jnp.bfloat16)
    return high, low


def product(a, b, dims):
    left = jnp.concatenate([a[0], a[1], a[0]], axis=dims[0][0])
    right = jnp.concatenate([b[0], b[0], b[1]], axis=dims[1][0])
    return lax.dot_general(left, right, (dims, ((), ())), preferred_element_type=jnp.float32)


NN = ((1,), (0,))
NT = ((1,), (1,))


def stacked(tables, rows):
    even, odd = tables
    top = np.concatenate([even[0], even[1]], axis=2)
    rest = np.zeros((2, rows - top.shape[1] - odd.shape[1], odd.shape[2]), odd.dtype)
    return np.concatenate([top, odd, rest], axis=1)


def part_tables(table_ref):
    quarter = table_ref.shape[2] // 2
    places = (
        (slice(0, quarter), slice(0, quarter)),
        (slice(0, quarter), slice(quarter, 2 * quarter)),
        (slice(quarter, 3 * quarter), slice(0, 2 * quarter)),
    )
    return [(table_ref[0, rows, columns], table_ref[1, rows, columns]) for rows, columns in places]


def table_loads(table_hbm, table_ref, sem):
    quarter = table_ref.shape[2] // 2
    return [
        pltpu.make_async_copy(table_hbm.at[:, rows], table_ref.at[:, rows], sem.at[i])
        for i, rows in enumerate((pl.ds(0, quarter), pl.ds(quarter, 2 * quarter)))
    ]


def part_ranges(total):
    return (0, total // 4), (total // 4, total // 2), (total // 2, total)


def slot(w, r, groups):
    per_level = groups // LEVELS
    return (w * per_level + r % per_level) * LEVELS + r // per_level


def y_forward_kernel(
    field_hbm, table_hbm, out_hbm, field_ref, table_ref, out_ref, in_sem, table_sem, out_sem
):
    scalars, planes, lines, length = field_ref.shape
    rows = planes * lines
    quarter = length // 4
    ranges = part_ranges(out_ref.shape[0])
    halves = [pl.ds(0, planes // 2), pl.ds(planes // 2, planes // 2)]
    loads = [
        [
            pltpu.make_async_copy(field_hbm.at[s, h], field_ref.at[s, h], in_sem.at[s, i])
            for i, h in enumerate(halves)
        ]
        for s in range(scalars)
    ]
    even_load, odd_load = table_loads(table_hbm, table_ref, table_sem)
    for load in (*loads[0], even_load, odd_load, *sum(loads[1:], [])):
        load.start()
    stores = []
    for s in range(scalars):
        pieces = []
        for load, h in zip(loads[s], halves):
            load.wait()
            first, second, third, fourth = fold([
                field_ref[s, h, :, q * quarter : (q + 1) * quarter].reshape(rows // 2, quarter)
                for q in range(4)
            ])
            folded = (first, second, jnp.concatenate([third, fourth], axis=1))
            pieces.append([split(value) for value in folded])
        parts = [
            tuple(jnp.concatenate([piece[p][i] for piece in pieces]) for i in range(2)) for p in range(3)
        ]
        for p in (0, 1, 2) if s == 0 else (2, 0, 1):
            if s == 0 and p == 0:
                even_load.wait()
            if s == 0 and p == 2:
                odd_load.wait()
            low, high = ranges[p]
            out_ref[low:high, s] = product(part_tables(table_ref)[p], parts[p], NT).reshape(high - low, -1, rows)
            store = pltpu.make_async_copy(
                out_ref.at[pl.ds(low, high - low), s],
                out_hbm.at[pl.ds(low, high - low), s],
                out_sem.at[s, p],
            )
            store.start()
            stores.append(store)
    for store in stores:
        store.wait()


def hold_kernel(after_hbm, table_hbm, table_ref, sem):
    del after_hbm
    load = pltpu.make_async_copy(table_hbm.at[:, pl.ds(0, table_ref.shape[1])], table_ref, sem.at[0])
    load.start()
    load.wait()


def y_inverse_kernel(norm, table_ref, spectrum_ref, out_hbm, out_ref, out_sem):
    devices, scalars, waves, rows = spectrum_ref.shape
    planes, lines, length = out_ref.shape[1:]
    quarter = length // 4
    tables = part_tables(table_ref)
    stores = []
    for s in range(scalars):
        first, second, third = (
            product(split(spectrum_ref[low:high, s].reshape(-1, rows).T), table, NN)
            for table, (low, high) in zip(tables, part_ranges(devices))
        )
        quarters = unfold(first * norm, second * norm, third[:, :quarter] * norm, third[:, quarter:] * norm)
        for q, value in enumerate(quarters):
            out_ref[s, :, :, q * quarter : (q + 1) * quarter] = value.reshape(planes, lines, quarter)
        for z in range(planes):
            store = pltpu.make_async_copy(out_ref.at[s, z], out_hbm.at[s, z], out_sem.at[s, z])
            store.start()
            stores.append(store)
    for store in stores:
        store.wait()


def x_kernel(
    walls, rate_ref, square_y_ref, square_x_ref, table_ref, received_hbm, out_ref, received_ref, sem,
    *line_refs
):
    devices, scalars, waves, rows = received_ref.shape
    groups = devices // walls
    length = line_refs[0].shape[1]
    quarter = length // 4
    lines = length // groups
    planes = rows // lines
    count = walls * planes
    lower = lax.broadcasted_iota(jnp.int32, (waves, 128), 1) < lines
    loads = [
        [
            pltpu.make_async_copy(
                received_hbm.at[pl.ds(w * groups, groups), s],
                received_ref.at[pl.ds(w * groups, groups), s],
                sem.at[s, w],
            )
            for w in range(walls)
        ]
        for s in range(scalars)
    ]
    for load in sum(loads, []):
        load.start()
    tables = part_tables(table_ref)
    ranges = part_ranges(length)

    def paired(a, b):
        return (
            jnp.where(lower, a, pltpu.roll(b, lines, 1)),
            jnp.where(lower, pltpu.roll(a, lines, 1), b),
        )

    def tiles():
        for w in range(walls):
            for p in range(planes // 2):
                yield w, slice(128 * p, 128 * (p + 1)), (w * planes + 2 * p) * waves

    def forward(s):
        line_ref = line_refs[s]
        for w, lanes, top in tiles():
            if lanes.start == 0:
                loads[s][w].wait()
            for i in range(groups // 8):
                left, right = (
                    fold([
                        received_ref[slot(w, groups // 4 * q + 2 * i + side, groups), s, :, lanes]
                        for q in range(4)
                    ])
                    for side in range(2)
                )
                for q in range(4):
                    a, b = paired(left[q], right[q])
                    columns = slice(quarter * q + 128 * i, quarter * q + 128 * (i + 1))
                    line_ref[top : top + waves, columns] = a
                    line_ref[top + waves : top + 2 * waves, columns] = b
        for table, (low, high) in zip(tables, ranges):
            line_ref[:, low:high] = product(split(line_ref[:, low:high]), table, NT)

    def diffuse(s):
        line_ref = line_refs[s]
        rates = [rate_ref[s, z] for z in range(count)]
        damping_x = [jnp.exp(-rate * square_x_ref[...]) for rate in rates]
        for i in range(waves // HEIGHT):
            square_y = square_y_ref[HEIGHT * i : HEIGHT * (i + 1)]
            damping_y = [jnp.exp(-rate * square_y) for rate in rates]
            starts = [z * waves + HEIGHT * i for z in range(count)]
            for j in range(length // 128):
                columns = slice(128 * j, 128 * (j + 1))
                damping = [dx[:, columns] * dy for dx, dy in zip(damping_x, damping_y)]
                own = [d * (1.0 - 2.0 * rate) for d, rate in zip(damping, rates)]
                around = [d * rate for d, rate in zip(damping, rates)]
                field = [line_ref[top : top + HEIGHT, columns] for top in starts]
                for step in range(STEPS):
                    sums = [
                        field[1],
                        *[field[z - 1] + field[z + 1] for z in range(1, count - 1)],
                        field[count - 2],
                    ]
                    field = [own[z] * field[z] + around[z] * sums[z] for z in range(count)]
                for top, value in zip(starts, field):
                    line_ref[top : top + HEIGHT, columns] = value

    def inverse(s):
        line_ref = line_refs[s]
        first, second, third = (
            product(split(line_ref[:, low:high]), table, NN) for table, (low, high) in zip(tables, ranges)
        )
        quarters = unfold(first, second, third[:, :quarter], third[:, quarter:])
        for q, value in enumerate(quarters):
            line_ref[:, q * quarter : (q + 1) * quarter] = value
        for w, lanes, top in tiles():
            for j in range(groups // 2):
                columns = slice(128 * j, 128 * (j + 1))
                a, b = paired(
                    line_ref[top : top + waves, columns],
                    line_ref[top + waves : top + 2 * waves, columns],
                )
                out_ref[slot(w, 2 * j, groups), s, :, lanes] = a
                out_ref[slot(w, 2 * j + 1, groups), s, :, lanes] = b

    for phase in (forward, diffuse, inverse):
        for s in range(scalars):
            phase(s)


def grant(mebibytes):
    return pltpu.CompilerParams(vmem_limit_bytes=mebibytes * MIB)


VMEM = pl.BlockSpec(memory_space=pltpu.VMEM)
ANY = pl.BlockSpec(memory_space=pl.ANY)


def cost(terms, total):
    return pl.CostEstimate(flops=2 * terms, bytes_accessed=total, transcendentals=0)


def with_kernels(fields, rates, walls, square_y, square_x, tables):
    scalars, planes, lines, length = fields.shape
    groups = lax.axis_size("row")
    devices = walls * groups
    waves = length // devices
    rows = planes * lines
    blocks = jax.ShapeDtypeStruct((devices, scalars, waves, rows), jnp.float32)
    total = 8 * scalars * rows * length
    work = 9 * scalars * rows * length * length // 8
    table = stacked(tables, TABLE_BYTES // (2 * length))
    table_shape = (2, 3 * length // 4, length // 2)

    spectrum = pl.pallas_call(
        y_forward_kernel,
        in_specs=[ANY] * 2,
        out_specs=ANY,
        out_shape=blocks,
        scratch_shapes=[
            pltpu.VMEM(fields.shape, jnp.float32),
            pltpu.VMEM(table_shape, jnp.bfloat16),
            pltpu.VMEM(blocks.shape, jnp.float32),
            pltpu.SemaphoreType.DMA((scalars, 2)),
            pltpu.SemaphoreType.DMA((2,)),
            pltpu.SemaphoreType.DMA((scalars, 3)),
        ],
        compiler_params=grant(60),
        cost_estimate=cost(work, total),
        name="y_forward",
    )(fields, table)
    held = pl.pallas_call(
        hold_kernel,
        in_specs=[ANY] * 2,
        out_specs=VMEM,
        out_shape=jax.ShapeDtypeStruct(table_shape, jnp.bfloat16),
        scratch_shapes=[pltpu.SemaphoreType.DMA((1,))],
        compiler_params=grant(48),
        cost_estimate=cost(0, 2 * MIB),
        name="hold",
    )(spectrum[0, 0, :8, :128], table)
    filtered = pl.pallas_call(
        functools.partial(x_kernel, walls),
        in_specs=[pl.BlockSpec(memory_space=pltpu.SMEM)] + [VMEM] * 3 + [ANY],
        out_specs=VMEM,
        out_shape=blocks,
        scratch_shapes=[
            pltpu.VMEM(blocks.shape, jnp.float32),
            pltpu.SemaphoreType.DMA((scalars, walls)),
            *[pltpu.VMEM((walls * planes * waves, lines * groups), jnp.float32)] * scalars,
        ],
        compiler_params=grant(40),
        cost_estimate=cost(2 * work, total),
        name="x_filter",
    )(rates, square_y, square_x, held, exchange(spectrum))
    return pl.pallas_call(
        functools.partial(y_inverse_kernel, 1.0 / (length * lines * groups)),
        in_specs=[VMEM] * 2,
        out_specs=ANY,
        out_shape=jax.ShapeDtypeStruct(fields.shape, jnp.float32),
        scratch_shapes=[
            pltpu.VMEM(fields.shape, jnp.float32),
            pltpu.SemaphoreType.DMA((scalars, planes)),
        ],
        compiler_params=grant(40),
        cost_estimate=cost(work, total),
        name="y_inverse",
    )(held, exchange(filtered))


def exchange(blocks):
    walls, groups = lax.axis_size("wall"), lax.axis_size("row")
    members = {slot(w, r, groups): w * groups + r for w in range(walls) for r in range(groups)}
    return lax.all_to_all(
        blocks, AXES, split_axis=0, concat_axis=0, tiled=True,
        axis_index_groups=[[members[i] for i in range(len(members))]],
    )


def with_arrays(fields, rates, walls, square_y, square_x, y_tables, x_tables):
    scalars, planes, lines, length = fields.shape
    groups = lax.axis_size("row")
    devices = walls * groups
    waves = length // devices
    count = walls * planes
    order = np.array([slot(w, r, groups) for w in range(walls) for r in range(groups)])
    dot = functools.partial(jnp.matmul, precision=lax.Precision.HIGHEST)

    def whole(tables):
        pairs = [jnp.asarray(t).astype(jnp.float32) for t in (*tables[0], tables[1])]
        return [t[0] + t[1] for t in pairs]

    def forward(value, tables):
        first, second, third, fourth = fold(jnp.split(value, 4, axis=-1))
        parts = (first, second, jnp.concatenate([third, fourth], axis=-1))
        return jnp.concatenate([dot(v, t.T) for v, t in zip(parts, whole(tables))], axis=-1)

    def inverse(value, tables):
        parts = jnp.split(value, [value.shape[-1] // 4, value.shape[-1] // 2], axis=-1)
        first, second, third = (dot(v, t) for v, t in zip(parts, whole(tables)))
        return jnp.concatenate(unfold(first, second, *jnp.split(third, 2, axis=-1)), axis=-1)

    results = []
    for s in range(scalars):
        spectral = forward(fields[s], y_tables).reshape(planes * lines, devices, waves)
        received = exchange(spectral.transpose(1, 2, 0))[order]
        received = received.reshape(walls, groups, waves, planes, lines).transpose(0, 3, 2, 1, 4)
        field = forward(received.reshape(count, waves, groups * lines), x_tables)
        rate = rates[s][:, None, None]
        damping = jnp.exp(-rate * (square_y + square_x))
        for step in range(STEPS):
            padded = jnp.pad(field, ((1, 1), (0, 0), (0, 0)))
            field = damping * (field + rate * (padded[2:] + padded[:-2] - 2.0 * field))
        back = inverse(field, x_tables).reshape(walls, planes, waves, groups, lines)
        back = back.transpose(0, 3, 2, 1, 4).reshape(devices, waves, planes * lines)
        spectrum = exchange(back[np.argsort(order)]).reshape(length, -1)
        results.append(inverse(spectrum.T, y_tables).reshape(planes, lines, length))
    return jnp.stack(results) * (1.0 / (length * groups * lines))


def signed_square(waves, length):
    signed = jnp.where(waves > length // 2, waves - length, waves)
    scaled = 2.0 * np.pi / length * signed.astype(jnp.float32)
    return scaled * scaled


def per_device(thermal_scalars, conductive_number):
    scalars, planes, lines, length = thermal_scalars.shape
    walls, groups = lax.axis_size("wall"), lax.axis_size("row")
    length_x = lines * groups
    waves = length // (walls * groups)
    rates = lax.all_gather(conductive_number, "wall", axis=1, tiled=True)
    own = slot(lax.axis_index("wall"), lax.axis_index("row"), groups)
    place = own * waves + jnp.arange(waves, dtype=jnp.int32)
    square_y = signed_square(wave_order(place, length), length)[:, None]
    square_x = signed_square(wave_order(jnp.arange(length_x), length_x), length_x)[None, :]
    fits = lines == 64 and planes % 2 == 0 and waves % HEIGHT == 0 and groups % 8 == 0
    if fits and length == length_x and walls * groups % 4 == 0:
        return with_kernels(thermal_scalars, rates, walls, square_y, square_x, tables_of(length))
    return with_arrays(
        thermal_scalars, rates, walls, square_y, square_x, tables_of(length), tables_of(length_x)
    )


def solution(mesh):
    return jax.shard_map(
        per_device,
        mesh=mesh,
        in_specs=(P(None, "wall", "row", None), P(None, "wall")),
        out_specs=P(None, "wall", "row", None),
        check_vma=False,
    )
```

```python
import functools

import jax
import jax.numpy as jnp
import ml_dtypes
import numpy as np
from jax import lax
from jax.experimental import pallas as pl
from jax.experimental.pallas import tpu as pltpu
from jax.sharding import PartitionSpec as P

STEPS = 3
AXES = ("wall", "row")
LEVELS = 4
MIB = 1024 * 1024
TABLE_BYTES = 21 * MIB


def wave_order(place, length):
    quarter = length // 4
    even = jnp.where(place < quarter, 4 * place, 4 * (place - quarter) + 2)
    return jnp.where(place < 2 * quarter, even, 2 * (place - 2 * quarter) + 1)


def cas_table(length, first, step):
    size = length // step
    waves = first + step * np.arange(size, dtype=np.int64)
    samples = np.arange(size, dtype=np.int64)
    angle = (waves[:, None] * samples[None, :] % length) * (2.0 * np.pi / length)
    table = np.cos(angle) + np.sin(angle)
    high = table.astype(np.float32).astype(ml_dtypes.bfloat16)
    low = (table - high.astype(np.float64)).astype(np.float32).astype(ml_dtypes.bfloat16)
    return np.stack([high, low])


def tables_of(length):
    even = np.stack([cas_table(length, 0, 4), cas_table(length, 2, 4)])
    return even, cas_table(length, 1, 2)


def fold(q):
    low, high = q[0] + q[2], q[1] + q[3]
    return low + high, low - high, q[0] - q[2], q[1] - q[3]


def unfold(first, second, third, fourth):
    low, high = first + second, first - second
    return low + third, high + fourth, low - third, high - fourth


def split(value):
    high = value.astype(jnp.bfloat16)
    low = (value - high.astype(jnp.float32)).astype(jnp.bfloat16)
    return high, low


def product(a, b, dims):
    left = jnp.concatenate([a[0], a[1], a[0]], axis=dims[0][0])
    right = jnp.concatenate([b[0], b[0], b[1]], axis=dims[1][0])
    return lax.dot_general(left, right, (dims, ((), ())), preferred_element_type=jnp.float32)


NN = ((1,), (0,))
NT = ((1,), (1,))


def stacked(tables, rows):
    even, odd = tables
    top = np.concatenate([even[0], even[1]], axis=2)
    rest = np.zeros((2, rows - top.shape[1] - odd.shape[1], odd.shape[2]), odd.dtype)
    return np.concatenate([top, odd, rest], axis=1)


def part_tables(table_ref):
    quarter = table_ref.shape[2] // 2
    places = (
        (slice(0, quarter), slice(0, quarter)),
        (slice(0, quarter), slice(quarter, 2 * quarter)),
        (slice(quarter, 3 * quarter), slice(0, 2 * quarter)),
    )
    return [(table_ref[0, rows, columns], table_ref[1, rows, columns]) for rows, columns in places]


def table_loads(table_hbm, table_ref, sem):
    quarter = table_ref.shape[2] // 2
    return [
        pltpu.make_async_copy(table_hbm.at[:, rows], table_ref.at[:, rows], sem.at[i])
        for i, rows in enumerate((pl.ds(0, quarter), pl.ds(quarter, 2 * quarter)))
    ]


def part_ranges(total):
    return (0, total // 4), (total // 4, total // 2), (total // 2, total)


def slot(w, r, groups):
    per_level = groups // LEVELS
    return (w * per_level + r % per_level) * LEVELS + r // per_level


def y_forward_kernel(
    field_hbm, table_hbm, out_hbm, field_ref, table_ref, out_ref, in_sem, table_sem, out_sem
):
    scalars, planes, lines, length = field_ref.shape
    rows = planes * lines
    quarter = length // 4
    ranges = part_ranges(out_ref.shape[0])
    loads = [
        pltpu.make_async_copy(field_hbm.at[s], field_ref.at[s], in_sem.at[s]) for s in range(scalars)
    ]
    even_load, odd_load = table_loads(table_hbm, table_ref, table_sem)
    loads[0].start()
    even_load.start()
    odd_load.start()
    for load in loads[1:]:
        load.start()
    stores = []
    for s in range(scalars):
        loads[s].wait()
        first, second, third, fourth = fold([
            field_ref[s, :, :, q * quarter : (q + 1) * quarter].reshape(rows, quarter) for q in range(4)
        ])
        parts = [split(v) for v in (first, second, jnp.concatenate([third, fourth], axis=1))]
        for p in (0, 1, 2) if s == 0 else (2, 0, 1):
            if s == 0 and p == 0:
                even_load.wait()
            if s == 0 and p == 2:
                odd_load.wait()
            low, high = ranges[p]
            out_ref[low:high, s] = product(part_tables(table_ref)[p], parts[p], NT).reshape(high - low, -1, rows)
            store = pltpu.make_async_copy(
                out_ref.at[pl.ds(low, high - low), s],
                out_hbm.at[pl.ds(low, high - low), s],
                out_sem.at[s, p],
            )
            store.start()
            stores.append(store)
    for store in stores:
        store.wait()


def hold_kernel(after_hbm, table_hbm, table_ref, sem):
    del after_hbm
    load = pltpu.make_async_copy(table_hbm.at[:, pl.ds(0, table_ref.shape[1])], table_ref, sem.at[0])
    load.start()
    load.wait()


def y_inverse_kernel(norm, table_ref, spectrum_ref, out_hbm, out_ref, out_sem):
    devices, scalars, waves, rows = spectrum_ref.shape
    planes, lines, length = out_ref.shape[1:]
    quarter = length // 4
    tables = part_tables(table_ref)
    stores = []
    for s in range(scalars):
        first, second, third = (
            product(split(spectrum_ref[low:high, s].reshape(-1, rows).T), table, NN)
            for table, (low, high) in zip(tables, part_ranges(devices))
        )
        quarters = unfold(first * norm, second * norm, third[:, :quarter] * norm, third[:, quarter:] * norm)
        for q, value in enumerate(quarters):
            out_ref[s, :, :, q * quarter : (q + 1) * quarter] = value.reshape(planes, lines, quarter)
        for z in range(planes):
            store = pltpu.make_async_copy(out_ref.at[s, z], out_hbm.at[s, z], out_sem.at[s, z])
            store.start()
            stores.append(store)
    for store in stores:
        store.wait()


def x_kernel(
    walls, rate_ref, square_y_ref, square_x_ref, table_ref, received_ref, out_ref, *line_refs
):
    devices, scalars, waves, rows = received_ref.shape
    groups = devices // walls
    length = line_refs[0].shape[1]
    quarter = length // 4
    lines = length // groups
    planes = rows // lines
    count = walls * planes
    lower = lax.broadcasted_iota(jnp.int32, (waves, 128), 1) < lines
    tables = part_tables(table_ref)
    ranges = part_ranges(length)

    def paired(a, b):
        return (
            jnp.where(lower, a, pltpu.roll(b, lines, 1)),
            jnp.where(lower, pltpu.roll(a, lines, 1), b),
        )

    def tiles():
        for w in range(walls):
            for p in range(planes // 2):
                yield w, slice(128 * p, 128 * (p + 1)), (w * planes + 2 * p) * waves

    def forward(s):
        line_ref = line_refs[s]
        for w, lanes, top in tiles():
            for i in range(groups // 8):
                left, right = (
                    fold([
                        received_ref[slot(w, groups // 4 * q + 2 * i + side, groups), s, :, lanes]
                        for q in range(4)
                    ])
                    for side in range(2)
                )
                for q in range(4):
                    a, b = paired(left[q], right[q])
                    columns = slice(quarter * q + 128 * i, quarter * q + 128 * (i + 1))
                    line_ref[top : top + waves, columns] = a
                    line_ref[top + waves : top + 2 * waves, columns] = b
        for table, (low, high) in zip(tables, ranges):
            line_ref[:, low:high] = product(split(line_ref[:, low:high]), table, NT)

    def diffuse(s):
        line_ref = line_refs[s]
        rates = [rate_ref[s, z] for z in range(count)]
        damping_y = [jnp.exp(-rate * square_y_ref[...]) for rate in rates]
        for j in range(length // 128):
            columns = slice(128 * j, 128 * (j + 1))
            square_x = square_x_ref[:, columns]
            damping = [jnp.exp(-rate * square_x) * dy for rate, dy in zip(rates, damping_y)]
            field = [line_ref[z * waves : (z + 1) * waves, columns] for z in range(count)]
            for step in range(STEPS):
                updated = []
                for z in range(count):
                    value = (1.0 - 2.0 * rates[z]) * field[z]
                    if z == 0:
                        around = field[1]
                    elif z == count - 1:
                        around = field[z - 1]
                    else:
                        around = field[z - 1] + field[z + 1]
                    updated.append(damping[z] * (value + rates[z] * around))
                field = updated
            for z in range(count):
                line_ref[z * waves : (z + 1) * waves, columns] = field[z]

    def inverse(s):
        line_ref = line_refs[s]
        first, second, third = (
            product(split(line_ref[:, low:high]), table, NN) for table, (low, high) in zip(tables, ranges)
        )
        quarters = unfold(first, second, third[:, :quarter], third[:, quarter:])
        for q, value in enumerate(quarters):
            line_ref[:, q * quarter : (q + 1) * quarter] = value
        for w, lanes, top in tiles():
            for j in range(groups // 2):
                columns = slice(128 * j, 128 * (j + 1))
                a, b = paired(
                    line_ref[top : top + waves, columns],
                    line_ref[top + waves : top + 2 * waves, columns],
                )
                out_ref[slot(w, 2 * j, groups), s, :, lanes] = a
                out_ref[slot(w, 2 * j + 1, groups), s, :, lanes] = b

    for phase in (forward, diffuse, inverse):
        for s in range(scalars):
            phase(s)


def grant(mebibytes):
    return pltpu.CompilerParams(vmem_limit_bytes=mebibytes * MIB)


VMEM = pl.BlockSpec(memory_space=pltpu.VMEM)
ANY = pl.BlockSpec(memory_space=pl.ANY)


def cost(terms, total):
    return pl.CostEstimate(flops=2 * terms, bytes_accessed=total, transcendentals=0)


def with_kernels(fields, rates, walls, square_y, square_x, tables):
    scalars, planes, lines, length = fields.shape
    groups = lax.axis_size("row")
    devices = walls * groups
    waves = length // devices
    rows = planes * lines
    blocks = jax.ShapeDtypeStruct((devices, scalars, waves, rows), jnp.float32)
    total = 8 * scalars * rows * length
    work = 9 * scalars * rows * length * length // 8
    table = stacked(tables, TABLE_BYTES // (2 * length))
    table_shape = (2, 3 * length // 4, length // 2)

    spectrum = pl.pallas_call(
        y_forward_kernel,
        in_specs=[ANY] * 2,
        out_specs=ANY,
        out_shape=blocks,
        scratch_shapes=[
            pltpu.VMEM(fields.shape, jnp.float32),
            pltpu.VMEM(table_shape, jnp.bfloat16),
            pltpu.VMEM(blocks.shape, jnp.float32),
            pltpu.SemaphoreType.DMA((scalars,)),
            pltpu.SemaphoreType.DMA((2,)),
            pltpu.SemaphoreType.DMA((scalars, 3)),
        ],
        compiler_params=grant(60),
        cost_estimate=cost(work, total),
        name="y_forward",
    )(fields, table)
    held = pl.pallas_call(
        hold_kernel,
        in_specs=[ANY] * 2,
        out_specs=VMEM,
        out_shape=jax.ShapeDtypeStruct(table_shape, jnp.bfloat16),
        scratch_shapes=[pltpu.SemaphoreType.DMA((1,))],
        compiler_params=grant(40),
        cost_estimate=cost(0, 2 * MIB),
        name="hold",
    )(spectrum[0, 0, :8, :128], table)
    filtered = pl.pallas_call(
        functools.partial(x_kernel, walls),
        in_specs=[pl.BlockSpec(memory_space=pltpu.SMEM)] + [VMEM] * 4,
        out_specs=VMEM,
        out_shape=blocks,
        scratch_shapes=[pltpu.VMEM((walls * planes * waves, lines * groups), jnp.float32)] * scalars,
        compiler_params=grant(40),
        cost_estimate=cost(2 * work, total),
        name="x_filter",
    )(rates, square_y, square_x, held, exchange(spectrum))
    return pl.pallas_call(
        functools.partial(y_inverse_kernel, 1.0 / (length * lines * groups)),
        in_specs=[VMEM] * 2,
        out_specs=ANY,
        out_shape=jax.ShapeDtypeStruct(fields.shape, jnp.float32),
        scratch_shapes=[
            pltpu.VMEM(fields.shape, jnp.float32),
            pltpu.SemaphoreType.DMA((scalars, planes)),
        ],
        compiler_params=grant(40),
        cost_estimate=cost(work, total),
        name="y_inverse",
    )(held, exchange(filtered))


def exchange(blocks):
    walls, groups = lax.axis_size("wall"), lax.axis_size("row")
    members = {slot(w, r, groups): w * groups + r for w in range(walls) for r in range(groups)}
    return lax.all_to_all(
        blocks, AXES, split_axis=0, concat_axis=0, tiled=True,
        axis_index_groups=[[members[i] for i in range(len(members))]],
    )


def with_arrays(fields, rates, walls, square_y, square_x, y_tables, x_tables):
    scalars, planes, lines, length = fields.shape
    groups = lax.axis_size("row")
    devices = walls * groups
    waves = length // devices
    count = walls * planes
    order = np.array([slot(w, r, groups) for w in range(walls) for r in range(groups)])
    dot = functools.partial(jnp.matmul, precision=lax.Precision.HIGHEST)

    def whole(tables):
        pairs = [jnp.asarray(t).astype(jnp.float32) for t in (*tables[0], tables[1])]
        return [t[0] + t[1] for t in pairs]

    def forward(value, tables):
        first, second, third, fourth = fold(jnp.split(value, 4, axis=-1))
        parts = (first, second, jnp.concatenate([third, fourth], axis=-1))
        return jnp.concatenate([dot(v, t.T) for v, t in zip(parts, whole(tables))], axis=-1)

    def inverse(value, tables):
        parts = jnp.split(value, [value.shape[-1] // 4, value.shape[-1] // 2], axis=-1)
        first, second, third = (dot(v, t) for v, t in zip(parts, whole(tables)))
        return jnp.concatenate(unfold(first, second, *jnp.split(third, 2, axis=-1)), axis=-1)

    results = []
    for s in range(scalars):
        spectral = forward(fields[s], y_tables).reshape(planes * lines, devices, waves)
        received = exchange(spectral.transpose(1, 2, 0))[order]
        received = received.reshape(walls, groups, waves, planes, lines).transpose(0, 3, 2, 1, 4)
        field = forward(received.reshape(count, waves, groups * lines), x_tables)
        rate = rates[s][:, None, None]
        damping = jnp.exp(-rate * (square_y + square_x))
        for step in range(STEPS):
            padded = jnp.pad(field, ((1, 1), (0, 0), (0, 0)))
            field = damping * (field + rate * (padded[2:] + padded[:-2] - 2.0 * field))
        back = inverse(field, x_tables).reshape(walls, planes, waves, groups, lines)
        back = back.transpose(0, 3, 2, 1, 4).reshape(devices, waves, planes * lines)
        spectrum = exchange(back[np.argsort(order)]).reshape(length, -1)
        results.append(inverse(spectrum.T, y_tables).reshape(planes, lines, length))
    return jnp.stack(results) * (1.0 / (length * groups * lines))


def signed_square(waves, length):
    signed = jnp.where(waves > length // 2, waves - length, waves)
    scaled = 2.0 * np.pi / length * signed.astype(jnp.float32)
    return scaled * scaled


def per_device(thermal_scalars, conductive_number):
    scalars, planes, lines, length = thermal_scalars.shape
    walls, groups = lax.axis_size("wall"), lax.axis_size("row")
    length_x = lines * groups
    waves = length // (walls * groups)
    rates = lax.all_gather(conductive_number, "wall", axis=1, tiled=True)
    own = slot(lax.axis_index("wall"), lax.axis_index("row"), groups)
    place = own * waves + jnp.arange(waves, dtype=jnp.int32)
    square_y = signed_square(wave_order(place, length), length)[:, None]
    square_x = signed_square(wave_order(jnp.arange(length_x), length_x), length_x)[None, :]
    fits = lines == 64 and planes % 2 == 0 and waves % 8 == 0 and groups % 8 == 0
    if fits and length == length_x and walls * groups % 4 == 0:
        return with_kernels(thermal_scalars, rates, walls, square_y, square_x, tables_of(length))
    return with_arrays(
        thermal_scalars, rates, walls, square_y, square_x, tables_of(length), tables_of(length_x)
    )


def solution(mesh):
    return jax.shard_map(
        per_device,
        mesh=mesh,
        in_specs=(P(None, "wall", "row", None), P(None, "wall")),
        out_specs=P(None, "wall", "row", None),
        check_vma=False,
    )
```

```python
import functools

import jax
import jax.numpy as jnp
import ml_dtypes
import numpy as np
from jax import lax
from jax.experimental import pallas as pl
from jax.experimental.pallas import tpu as pltpu
from jax.sharding import PartitionSpec as P

STEPS = 3
AXES = ("wall", "row")
LEVELS = 4
MIB = 1024 * 1024


def wave_order(place, length):
    quarter = length // 4
    even = jnp.where(place < quarter, 4 * place, 4 * (place - quarter) + 2)
    return jnp.where(place < 2 * quarter, even, 2 * (place - 2 * quarter) + 1)


def cas_table(length, first, step):
    size = length // step
    waves = first + step * np.arange(size, dtype=np.int64)
    samples = np.arange(size, dtype=np.int64)
    angle = (waves[:, None] * samples[None, :] % length) * (2.0 * np.pi / length)
    table = np.cos(angle) + np.sin(angle)
    high = table.astype(np.float32).astype(ml_dtypes.bfloat16)
    low = (table - high.astype(np.float64)).astype(np.float32).astype(ml_dtypes.bfloat16)
    return np.stack([high, low])


def tables_of(length):
    even = np.stack([cas_table(length, 0, 4), cas_table(length, 2, 4)])
    return even, cas_table(length, 1, 2)


def fold(q):
    low, high = q[0] + q[2], q[1] + q[3]
    return low + high, low - high, q[0] - q[2], q[1] - q[3]


def unfold(first, second, third, fourth):
    low, high = first + second, first - second
    return low + third, high + fourth, low - third, high - fourth


def split(value):
    high = value.astype(jnp.bfloat16)
    low = (value - high.astype(jnp.float32)).astype(jnp.bfloat16)
    return high, low


def product(a, b, dims):
    left = jnp.concatenate([a[0], a[1], a[0]], axis=dims[0][0])
    right = jnp.concatenate([b[0], b[0], b[1]], axis=dims[1][0])
    return lax.dot_general(left, right, (dims, ((), ())), preferred_element_type=jnp.float32)


NN = ((1,), (0,))
NT = ((1,), (1,))


def stacked(tables):
    even, odd = tables
    return np.concatenate([np.concatenate([even[0], even[1]], axis=2), odd], axis=1)


def part_tables(table_ref):
    quarter = table_ref.shape[2] // 2
    places = (
        (slice(0, quarter), slice(0, quarter)),
        (slice(0, quarter), slice(quarter, 2 * quarter)),
        (slice(quarter, 3 * quarter), slice(0, 2 * quarter)),
    )
    return [(table_ref[0, rows, columns], table_ref[1, rows, columns]) for rows, columns in places]


def table_loads(table_hbm, table_ref, sem):
    quarter = table_ref.shape[2] // 2
    return [
        pltpu.make_async_copy(table_hbm.at[:, rows], table_ref.at[:, rows], sem.at[i])
        for i, rows in enumerate((pl.ds(0, quarter), pl.ds(quarter, 2 * quarter)))
    ]


def part_ranges(total):
    return (0, total // 4), (total // 4, total // 2), (total // 2, total)


def slot(w, r, groups):
    per_level = groups // LEVELS
    return (w * per_level + r % per_level) * LEVELS + r // per_level


def y_forward_kernel(
    field_hbm, table_hbm, out_hbm, table_ref, field_ref, out_ref, in_sem, table_sem, out_sem
):
    scalars, planes, lines, length = field_ref.shape
    rows = planes * lines
    quarter = length // 4
    ranges = part_ranges(out_ref.shape[0])
    loads = [
        pltpu.make_async_copy(field_hbm.at[s], field_ref.at[s], in_sem.at[s]) for s in range(scalars)
    ]
    even_load, odd_load = table_loads(table_hbm, table_ref, table_sem)
    loads[0].start()
    even_load.start()
    odd_load.start()
    for load in loads[1:]:
        load.start()
    stores = []
    for s in range(scalars):
        loads[s].wait()
        first, second, third, fourth = fold([
            field_ref[s, :, :, q * quarter : (q + 1) * quarter].reshape(rows, quarter) for q in range(4)
        ])
        parts = [split(v) for v in (first, second, jnp.concatenate([third, fourth], axis=1))]
        for p in (0, 1, 2) if s == 0 else (2, 0, 1):
            if s == 0 and p == 0:
                even_load.wait()
            if s == 0 and p == 2:
                odd_load.wait()
            low, high = ranges[p]
            out_ref[low:high, s] = product(part_tables(table_ref)[p], parts[p], NT).reshape(high - low, -1, rows)
            store = pltpu.make_async_copy(
                out_ref.at[pl.ds(low, high - low), s],
                out_hbm.at[pl.ds(low, high - low), s],
                out_sem.at[s, p],
            )
            store.start()
            stores.append(store)
    for store in stores:
        store.wait()


def y_inverse_kernel(norm, table_ref, spectrum_ref, out_hbm, out_ref, out_sem):
    devices, scalars, waves, rows = spectrum_ref.shape
    planes, lines, length = out_ref.shape[1:]
    quarter = length // 4
    tables = part_tables(table_ref)
    stores = []
    for s in range(scalars):
        first, second, third = (
            product(split(spectrum_ref[low:high, s].reshape(-1, rows).T), table, NN)
            for table, (low, high) in zip(tables, part_ranges(devices))
        )
        quarters = unfold(first * norm, second * norm, third[:, :quarter] * norm, third[:, quarter:] * norm)
        for q, value in enumerate(quarters):
            out_ref[s, :, :, q * quarter : (q + 1) * quarter] = value.reshape(planes, lines, quarter)
        for z in range(planes):
            store = pltpu.make_async_copy(out_ref.at[s, z], out_hbm.at[s, z], out_sem.at[s, z])
            store.start()
            stores.append(store)
    for store in stores:
        store.wait()


def x_kernel(
    walls, rate_ref, square_y_ref, square_x_ref, table_ref, received_ref, out_ref, *line_refs
):
    devices, scalars, waves, rows = received_ref.shape
    groups = devices // walls
    length = line_refs[0].shape[1]
    quarter = length // 4
    lines = length // groups
    planes = rows // lines
    count = walls * planes
    lower = lax.broadcasted_iota(jnp.int32, (waves, 128), 1) < lines
    tables = part_tables(table_ref)
    ranges = part_ranges(length)

    def paired(a, b):
        return (
            jnp.where(lower, a, pltpu.roll(b, lines, 1)),
            jnp.where(lower, pltpu.roll(a, lines, 1), b),
        )

    def tiles():
        for w in range(walls):
            for p in range(planes // 2):
                yield w, slice(128 * p, 128 * (p + 1)), (w * planes + 2 * p) * waves

    def forward(s):
        line_ref = line_refs[s]
        for w, lanes, top in tiles():
            for i in range(groups // 8):
                left, right = (
                    fold([
                        received_ref[slot(w, groups // 4 * q + 2 * i + side, groups), s, :, lanes]
                        for q in range(4)
                    ])
                    for side in range(2)
                )
                for q in range(4):
                    a, b = paired(left[q], right[q])
                    columns = slice(quarter * q + 128 * i, quarter * q + 128 * (i + 1))
                    line_ref[top : top + waves, columns] = a
                    line_ref[top + waves : top + 2 * waves, columns] = b
        for table, (low, high) in zip(tables, ranges):
            line_ref[:, low:high] = product(split(line_ref[:, low:high]), table, NT)

    def diffuse(s):
        line_ref = line_refs[s]
        rates = [rate_ref[s, z] for z in range(count)]
        damping_y = [jnp.exp(-rate * square_y_ref[...]) for rate in rates]
        for j in range(length // 128):
            columns = slice(128 * j, 128 * (j + 1))
            square_x = square_x_ref[:, columns]
            damping = [jnp.exp(-rate * square_x) * dy for rate, dy in zip(rates, damping_y)]
            field = [line_ref[z * waves : (z + 1) * waves, columns] for z in range(count)]
            for step in range(STEPS):
                updated = []
                for z in range(count):
                    value = (1.0 - 2.0 * rates[z]) * field[z]
                    if z == 0:
                        around = field[1]
                    elif z == count - 1:
                        around = field[z - 1]
                    else:
                        around = field[z - 1] + field[z + 1]
                    updated.append(damping[z] * (value + rates[z] * around))
                field = updated
            for z in range(count):
                line_ref[z * waves : (z + 1) * waves, columns] = field[z]

    def inverse(s):
        line_ref = line_refs[s]
        first, second, third = (
            product(split(line_ref[:, low:high]), table, NN) for table, (low, high) in zip(tables, ranges)
        )
        quarters = unfold(first, second, third[:, :quarter], third[:, quarter:])
        for q, value in enumerate(quarters):
            line_ref[:, q * quarter : (q + 1) * quarter] = value
        for w, lanes, top in tiles():
            for j in range(groups // 2):
                columns = slice(128 * j, 128 * (j + 1))
                a, b = paired(
                    line_ref[top : top + waves, columns],
                    line_ref[top + waves : top + 2 * waves, columns],
                )
                out_ref[slot(w, 2 * j, groups), s, :, lanes] = a
                out_ref[slot(w, 2 * j + 1, groups), s, :, lanes] = b

    for phase in (forward, diffuse, inverse):
        for s in range(scalars):
            phase(s)


def grant(mebibytes):
    return pltpu.CompilerParams(vmem_limit_bytes=int(mebibytes * MIB))


VMEM = pl.BlockSpec(memory_space=pltpu.VMEM)
ANY = pl.BlockSpec(memory_space=pl.ANY)


def cost(terms, total):
    return pl.CostEstimate(flops=2 * terms, bytes_accessed=total, transcendentals=0)


def with_kernels(fields, rates, walls, square_y, square_x, tables):
    scalars, planes, lines, length = fields.shape
    groups = lax.axis_size("row")
    devices = walls * groups
    waves = length // devices
    rows = planes * lines
    blocks = jax.ShapeDtypeStruct((devices, scalars, waves, rows), jnp.float32)
    total = 8 * scalars * rows * length
    work = 9 * scalars * rows * length * length // 8
    table = stacked(tables)

    spectrum, table = pl.pallas_call(
        y_forward_kernel,
        in_specs=[ANY] * 2,
        out_specs=[ANY, VMEM],
        out_shape=[blocks, jax.ShapeDtypeStruct(table.shape, jnp.bfloat16)],
        scratch_shapes=[
            pltpu.VMEM(fields.shape, jnp.float32),
            pltpu.VMEM(blocks.shape, jnp.float32),
            pltpu.SemaphoreType.DMA((scalars,)),
            pltpu.SemaphoreType.DMA((2,)),
            pltpu.SemaphoreType.DMA((scalars, 3)),
        ],
        compiler_params=grant(51.5),
        cost_estimate=cost(work, total),
        name="y_forward",
    )(fields, table)
    filtered = pl.pallas_call(
        functools.partial(x_kernel, walls),
        in_specs=[pl.BlockSpec(memory_space=pltpu.SMEM)] + [VMEM] * 4,
        out_specs=VMEM,
        out_shape=blocks,
        scratch_shapes=[pltpu.VMEM((walls * planes * waves, lines * groups), jnp.float32)] * scalars,
        compiler_params=grant(40),
        cost_estimate=cost(2 * work, total),
        name="x_filter",
    )(rates, square_y, square_x, table, exchange(spectrum))
    return pl.pallas_call(
        functools.partial(y_inverse_kernel, 1.0 / (length * lines * groups)),
        in_specs=[VMEM] * 2,
        out_specs=ANY,
        out_shape=jax.ShapeDtypeStruct(fields.shape, jnp.float32),
        scratch_shapes=[
            pltpu.VMEM(fields.shape, jnp.float32),
            pltpu.SemaphoreType.DMA((scalars, planes)),
        ],
        compiler_params=grant(40),
        cost_estimate=cost(work, total),
        name="y_inverse",
    )(table, exchange(filtered))


def exchange(blocks):
    walls, groups = lax.axis_size("wall"), lax.axis_size("row")
    members = {slot(w, r, groups): w * groups + r for w in range(walls) for r in range(groups)}
    return lax.all_to_all(
        blocks, AXES, split_axis=0, concat_axis=0, tiled=True,
        axis_index_groups=[[members[i] for i in range(len(members))]],
    )


def with_arrays(fields, rates, walls, square_y, square_x, y_tables, x_tables):
    scalars, planes, lines, length = fields.shape
    groups = lax.axis_size("row")
    devices = walls * groups
    waves = length // devices
    count = walls * planes
    order = np.array([slot(w, r, groups) for w in range(walls) for r in range(groups)])
    dot = functools.partial(jnp.matmul, precision=lax.Precision.HIGHEST)

    def whole(tables):
        pairs = [jnp.asarray(t).astype(jnp.float32) for t in (*tables[0], tables[1])]
        return [t[0] + t[1] for t in pairs]

    def forward(value, tables):
        first, second, third, fourth = fold(jnp.split(value, 4, axis=-1))
        parts = (first, second, jnp.concatenate([third, fourth], axis=-1))
        return jnp.concatenate([dot(v, t.T) for v, t in zip(parts, whole(tables))], axis=-1)

    def inverse(value, tables):
        parts = jnp.split(value, [value.shape[-1] // 4, value.shape[-1] // 2], axis=-1)
        first, second, third = (dot(v, t) for v, t in zip(parts, whole(tables)))
        return jnp.concatenate(unfold(first, second, *jnp.split(third, 2, axis=-1)), axis=-1)

    results = []
    for s in range(scalars):
        spectral = forward(fields[s], y_tables).reshape(planes * lines, devices, waves)
        received = exchange(spectral.transpose(1, 2, 0))[order]
        received = received.reshape(walls, groups, waves, planes, lines).transpose(0, 3, 2, 1, 4)
        field = forward(received.reshape(count, waves, groups * lines), x_tables)
        rate = rates[s][:, None, None]
        damping = jnp.exp(-rate * (square_y + square_x))
        for step in range(STEPS):
            padded = jnp.pad(field, ((1, 1), (0, 0), (0, 0)))
            field = damping * (field + rate * (padded[2:] + padded[:-2] - 2.0 * field))
        back = inverse(field, x_tables).reshape(walls, planes, waves, groups, lines)
        back = back.transpose(0, 3, 2, 1, 4).reshape(devices, waves, planes * lines)
        spectrum = exchange(back[np.argsort(order)]).reshape(length, -1)
        results.append(inverse(spectrum.T, y_tables).reshape(planes, lines, length))
    return jnp.stack(results) * (1.0 / (length * groups * lines))


def signed_square(waves, length):
    signed = jnp.where(waves > length // 2, waves - length, waves)
    scaled = 2.0 * np.pi / length * signed.astype(jnp.float32)
    return scaled * scaled


def per_device(thermal_scalars, conductive_number):
    scalars, planes, lines, length = thermal_scalars.shape
    walls, groups = lax.axis_size("wall"), lax.axis_size("row")
    length_x = lines * groups
    waves = length // (walls * groups)
    rates = lax.all_gather(conductive_number, "wall", axis=1, tiled=True)
    own = slot(lax.axis_index("wall"), lax.axis_index("row"), groups)
    place = own * waves + jnp.arange(waves, dtype=jnp.int32)
    square_y = signed_square(wave_order(place, length), length)[:, None]
    square_x = signed_square(wave_order(jnp.arange(length_x), length_x), length_x)[None, :]
    fits = lines == 64 and planes % 2 == 0 and waves % 8 == 0 and groups % 8 == 0
    if fits and length == length_x and walls * groups % 4 == 0:
        return with_kernels(thermal_scalars, rates, walls, square_y, square_x, tables_of(length))
    return with_arrays(
        thermal_scalars, rates, walls, square_y, square_x, tables_of(length), tables_of(length_x)
    )


def solution(mesh):
    return jax.shard_map(
        per_device,
        mesh=mesh,
        in_specs=(P(None, "wall", "row", None), P(None, "wall")),
        out_specs=P(None, "wall", "row", None),
        check_vma=False,
    )
```

```python
import functools

import jax
import jax.numpy as jnp
import ml_dtypes
import numpy as np
from jax import lax
from jax.experimental import pallas as pl
from jax.experimental.pallas import tpu as pltpu
from jax.sharding import PartitionSpec as P

STEPS = 3
AXES = ("wall", "row")
LEVELS = 4
MIB = 1024 * 1024
TABLE_BYTES = 13 * MIB


def wave_order(place, length):
    quarter = length // 4
    even = jnp.where(place < quarter, 4 * place, 4 * (place - quarter) + 2)
    return jnp.where(place < 2 * quarter, even, 2 * (place - 2 * quarter) + 1)


def cas_table(length, first, step):
    size = length // step
    waves = first + step * np.arange(size, dtype=np.int64)
    samples = np.arange(size, dtype=np.int64)
    angle = (waves[:, None] * samples[None, :] % length) * (2.0 * np.pi / length)
    table = np.cos(angle) + np.sin(angle)
    high = table.astype(np.float32).astype(ml_dtypes.bfloat16)
    low = (table - high.astype(np.float64)).astype(np.float32).astype(ml_dtypes.bfloat16)
    return np.stack([high, low])


def tables_of(length):
    even = np.stack([cas_table(length, 0, 4), cas_table(length, 2, 4)])
    return even, cas_table(length, 1, 2)


def fold(q):
    low, high = q[0] + q[2], q[1] + q[3]
    return low + high, low - high, q[0] - q[2], q[1] - q[3]


def unfold(first, second, third, fourth):
    low, high = first + second, first - second
    return low + third, high + fourth, low - third, high - fourth


def split(value):
    high = value.astype(jnp.bfloat16)
    low = (value - high.astype(jnp.float32)).astype(jnp.bfloat16)
    return high, low


def product(a, b, dims):
    left = jnp.concatenate([a[0], a[1], a[0]], axis=dims[0][0])
    right = jnp.concatenate([b[0], b[0], b[1]], axis=dims[1][0])
    return lax.dot_general(left, right, (dims, ((), ())), preferred_element_type=jnp.float32)


NN = ((1,), (0,))
NT = ((1,), (1,))


def stacked(tables, rows):
    even, odd = tables
    top = np.concatenate([even[0], even[1]], axis=2)
    rest = np.zeros((2, rows - top.shape[1] - odd.shape[1], odd.shape[2]), odd.dtype)
    return np.concatenate([top, odd, rest], axis=1)


def part_tables(even_ref, odd_ref):
    quarter = even_ref.shape[1]
    columns = (slice(0, quarter), slice(quarter, 2 * quarter))
    return [(even_ref[0, :, c], even_ref[1, :, c]) for c in columns] + [(odd_ref[0], odd_ref[1])]


def even_copy(table_hbm, even_ref, sem):
    rows = pl.ds(0, even_ref.shape[1])
    return pltpu.make_async_copy(table_hbm.at[:, rows], even_ref, sem)


def odd_copy(table_hbm, odd_ref, sem):
    rows = pl.ds(odd_ref.shape[1] // 2, odd_ref.shape[1])
    return pltpu.make_async_copy(table_hbm.at[:, rows], odd_ref, sem)


def part_ranges(total):
    return (0, total // 4), (total // 4, total // 2), (total // 2, total)


def slot(w, r, groups):
    per_level = groups // LEVELS
    return (w * per_level + r % per_level) * LEVELS + r // per_level


def y_forward_kernel(
    field_hbm, table_hbm, out_hbm, odd_ref, field_ref, even_ref, out_ref, in_sem, table_sem, out_sem
):
    scalars, planes, lines, length = field_ref.shape
    rows = planes * lines
    quarter = length // 4
    ranges = part_ranges(out_ref.shape[0])
    loads = [
        pltpu.make_async_copy(field_hbm.at[s], field_ref.at[s], in_sem.at[s]) for s in range(scalars)
    ]
    even_load = even_copy(table_hbm, even_ref, table_sem.at[0])
    odd_load = odd_copy(table_hbm, odd_ref, table_sem.at[1])
    loads[0].start()
    even_load.start()
    odd_load.start()
    for load in loads[1:]:
        load.start()
    stores = []
    for s in range(scalars):
        loads[s].wait()
        first, second, third, fourth = fold([
            field_ref[s, :, :, q * quarter : (q + 1) * quarter].reshape(rows, quarter) for q in range(4)
        ])
        parts = [split(v) for v in (first, second, jnp.concatenate([third, fourth], axis=1))]
        for p in (0, 1, 2) if s == 0 else (2, 0, 1):
            if s == 0 and p == 0:
                even_load.wait()
            if s == 0 and p == 2:
                odd_load.wait()
            low, high = ranges[p]
            out_ref[low:high, s] = product(part_tables(even_ref, odd_ref)[p], parts[p], NT).reshape(high - low, -1, rows)
            store = pltpu.make_async_copy(
                out_ref.at[pl.ds(low, high - low), s],
                out_hbm.at[pl.ds(low, high - low), s],
                out_sem.at[s, p],
            )
            store.start()
            stores.append(store)
    for store in stores:
        store.wait()


def y_inverse_kernel(
    norm, odd_ref, spectrum_ref, table_hbm, out_hbm, even_ref, out_ref, table_sem, out_sem
):
    even_load = even_copy(table_hbm, even_ref, table_sem.at[0])
    even_load.start()
    devices, scalars, waves, rows = spectrum_ref.shape
    planes, lines, length = out_ref.shape[1:]
    quarter = length // 4
    ranges = part_ranges(devices)
    stores = []
    for s in range(scalars):
        parts = {}
        for p in (2, 0, 1):
            low, high = ranges[p]
            turned = split(spectrum_ref[low:high, s].reshape(-1, rows).T)
            if s == 0 and p == 0:
                even_load.wait()
            parts[p] = product(turned, part_tables(even_ref, odd_ref)[p], NN)
        first, second, third = (parts[p] for p in range(3))
        quarters = unfold(first * norm, second * norm, third[:, :quarter] * norm, third[:, quarter:] * norm)
        for q, value in enumerate(quarters):
            out_ref[s, :, :, q * quarter : (q + 1) * quarter] = value.reshape(planes, lines, quarter)
        for z in range(planes):
            store = pltpu.make_async_copy(out_ref.at[s, z], out_hbm.at[s, z], out_sem.at[s, z])
            store.start()
            stores.append(store)
    for store in stores:
        store.wait()


def x_kernel(
    walls, rate_ref, square_y_ref, square_x_ref, odd_ref, received_ref, table_hbm, out_ref, even_ref,
    table_sem, *line_refs
):
    even_load = even_copy(table_hbm, even_ref, table_sem.at[0])
    even_load.start()
    devices, scalars, waves, rows = received_ref.shape
    groups = devices // walls
    length = line_refs[0].shape[1]
    quarter = length // 4
    lines = length // groups
    planes = rows // lines
    count = walls * planes
    lower = lax.broadcasted_iota(jnp.int32, (waves, 128), 1) < lines
    ranges = part_ranges(length)

    def paired(a, b):
        return (
            jnp.where(lower, a, pltpu.roll(b, lines, 1)),
            jnp.where(lower, pltpu.roll(a, lines, 1), b),
        )

    def tiles():
        for w in range(walls):
            for p in range(planes // 2):
                yield w, slice(128 * p, 128 * (p + 1)), (w * planes + 2 * p) * waves

    def forward(s):
        line_ref = line_refs[s]
        for w, lanes, top in tiles():
            for i in range(groups // 8):
                left, right = (
                    fold([
                        received_ref[slot(w, groups // 4 * q + 2 * i + side, groups), s, :, lanes]
                        for q in range(4)
                    ])
                    for side in range(2)
                )
                for q in range(4):
                    a, b = paired(left[q], right[q])
                    columns = slice(quarter * q + 128 * i, quarter * q + 128 * (i + 1))
                    line_ref[top : top + waves, columns] = a
                    line_ref[top + waves : top + 2 * waves, columns] = b
        for p in (2, 0, 1):
            low, high = ranges[p]
            if s == 0 and p == 0:
                even_load.wait()
            table = part_tables(even_ref, odd_ref)[p]
            line_ref[:, low:high] = product(split(line_ref[:, low:high]), table, NT)

    def diffuse(s):
        line_ref = line_refs[s]
        rates = [rate_ref[s, z] for z in range(count)]
        damping_y = [jnp.exp(-rate * square_y_ref[...]) for rate in rates]
        for j in range(length // 128):
            columns = slice(128 * j, 128 * (j + 1))
            square_x = square_x_ref[:, columns]
            damping = [jnp.exp(-rate * square_x) * dy for rate, dy in zip(rates, damping_y)]
            field = [line_ref[z * waves : (z + 1) * waves, columns] for z in range(count)]
            for step in range(STEPS):
                updated = []
                for z in range(count):
                    value = (1.0 - 2.0 * rates[z]) * field[z]
                    if z == 0:
                        around = field[1]
                    elif z == count - 1:
                        around = field[z - 1]
                    else:
                        around = field[z - 1] + field[z + 1]
                    updated.append(damping[z] * (value + rates[z] * around))
                field = updated
            for z in range(count):
                line_ref[z * waves : (z + 1) * waves, columns] = field[z]

    def inverse(s):
        line_ref = line_refs[s]
        first, second, third = (
            product(split(line_ref[:, low:high]), table, NN)
            for table, (low, high) in zip(part_tables(even_ref, odd_ref), ranges)
        )
        quarters = unfold(first, second, third[:, :quarter], third[:, quarter:])
        for q, value in enumerate(quarters):
            line_ref[:, q * quarter : (q + 1) * quarter] = value
        for w, lanes, top in tiles():
            for j in range(groups // 2):
                columns = slice(128 * j, 128 * (j + 1))
                a, b = paired(
                    line_ref[top : top + waves, columns],
                    line_ref[top + waves : top + 2 * waves, columns],
                )
                out_ref[slot(w, 2 * j, groups), s, :, lanes] = a
                out_ref[slot(w, 2 * j + 1, groups), s, :, lanes] = b

    for phase in (forward, diffuse, inverse):
        for s in range(scalars):
            phase(s)


def grant(mebibytes):
    return pltpu.CompilerParams(vmem_limit_bytes=int(mebibytes * MIB))


VMEM = pl.BlockSpec(memory_space=pltpu.VMEM)
ANY = pl.BlockSpec(memory_space=pl.ANY)


def cost(terms, total):
    return pl.CostEstimate(flops=2 * terms, bytes_accessed=total, transcendentals=0)


def with_kernels(fields, rates, walls, square_y, square_x, tables):
    scalars, planes, lines, length = fields.shape
    groups = lax.axis_size("row")
    devices = walls * groups
    waves = length // devices
    rows = planes * lines
    blocks = jax.ShapeDtypeStruct((devices, scalars, waves, rows), jnp.float32)
    total = 8 * scalars * rows * length
    work = 9 * scalars * rows * length * length // 8
    table = stacked(tables, TABLE_BYTES // (2 * length))
    even_scratch = pltpu.VMEM((2, length // 4, length // 2), jnp.bfloat16)
    odd_shape = jax.ShapeDtypeStruct((2, length // 2, length // 2), jnp.bfloat16)

    spectrum, odd = pl.pallas_call(
        y_forward_kernel,
        in_specs=[ANY] * 2,
        out_specs=[ANY, VMEM],
        out_shape=[blocks, odd_shape],
        scratch_shapes=[
            pltpu.VMEM(fields.shape, jnp.float32),
            even_scratch,
            pltpu.VMEM(blocks.shape, jnp.float32),
            pltpu.SemaphoreType.DMA((scalars,)),
            pltpu.SemaphoreType.DMA((2,)),
            pltpu.SemaphoreType.DMA((scalars, 3)),
        ],
        compiler_params=grant(52),
        cost_estimate=cost(work, total),
        name="y_forward",
    )(fields, table)
    filtered = pl.pallas_call(
        functools.partial(x_kernel, walls),
        in_specs=[pl.BlockSpec(memory_space=pltpu.SMEM)] + [VMEM] * 4 + [ANY],
        out_specs=VMEM,
        out_shape=blocks,
        scratch_shapes=[
            even_scratch,
            pltpu.SemaphoreType.DMA((1,)),
            *[pltpu.VMEM((walls * planes * waves, lines * groups), jnp.float32)] * scalars,
        ],
        compiler_params=grant(48),
        cost_estimate=cost(2 * work, total),
        name="x_filter",
    )(rates, square_y, square_x, odd, exchange(spectrum), table)
    return pl.pallas_call(
        functools.partial(y_inverse_kernel, 1.0 / (length * lines * groups)),
        in_specs=[VMEM] * 2 + [ANY],
        out_specs=ANY,
        out_shape=jax.ShapeDtypeStruct(fields.shape, jnp.float32),
        scratch_shapes=[
            even_scratch,
            pltpu.VMEM(fields.shape, jnp.float32),
            pltpu.SemaphoreType.DMA((1,)),
            pltpu.SemaphoreType.DMA((scalars, planes)),
        ],
        compiler_params=grant(48),
        cost_estimate=cost(work, total),
        name="y_inverse",
    )(odd, exchange(filtered), table)


def exchange(blocks):
    walls, groups = lax.axis_size("wall"), lax.axis_size("row")
    members = {slot(w, r, groups): w * groups + r for w in range(walls) for r in range(groups)}
    return lax.all_to_all(
        blocks, AXES, split_axis=0, concat_axis=0, tiled=True,
        axis_index_groups=[[members[i] for i in range(len(members))]],
    )


def with_arrays(fields, rates, walls, square_y, square_x, y_tables, x_tables):
    scalars, planes, lines, length = fields.shape
    groups = lax.axis_size("row")
    devices = walls * groups
    waves = length // devices
    count = walls * planes
    order = np.array([slot(w, r, groups) for w in range(walls) for r in range(groups)])
    dot = functools.partial(jnp.matmul, precision=lax.Precision.HIGHEST)

    def whole(tables):
        pairs = [jnp.asarray(t).astype(jnp.float32) for t in (*tables[0], tables[1])]
        return [t[0] + t[1] for t in pairs]

    def forward(value, tables):
        first, second, third, fourth = fold(jnp.split(value, 4, axis=-1))
        parts = (first, second, jnp.concatenate([third, fourth], axis=-1))
        return jnp.concatenate([dot(v, t.T) for v, t in zip(parts, whole(tables))], axis=-1)

    def inverse(value, tables):
        parts = jnp.split(value, [value.shape[-1] // 4, value.shape[-1] // 2], axis=-1)
        first, second, third = (dot(v, t) for v, t in zip(parts, whole(tables)))
        return jnp.concatenate(unfold(first, second, *jnp.split(third, 2, axis=-1)), axis=-1)

    results = []
    for s in range(scalars):
        spectral = forward(fields[s], y_tables).reshape(planes * lines, devices, waves)
        received = exchange(spectral.transpose(1, 2, 0))[order]
        received = received.reshape(walls, groups, waves, planes, lines).transpose(0, 3, 2, 1, 4)
        field = forward(received.reshape(count, waves, groups * lines), x_tables)
        rate = rates[s][:, None, None]
        damping = jnp.exp(-rate * (square_y + square_x))
        for step in range(STEPS):
            padded = jnp.pad(field, ((1, 1), (0, 0), (0, 0)))
            field = damping * (field + rate * (padded[2:] + padded[:-2] - 2.0 * field))
        back = inverse(field, x_tables).reshape(walls, planes, waves, groups, lines)
        back = back.transpose(0, 3, 2, 1, 4).reshape(devices, waves, planes * lines)
        spectrum = exchange(back[np.argsort(order)]).reshape(length, -1)
        results.append(inverse(spectrum.T, y_tables).reshape(planes, lines, length))
    return jnp.stack(results) * (1.0 / (length * groups * lines))


def signed_square(waves, length):
    signed = jnp.where(waves > length // 2, waves - length, waves)
    scaled = 2.0 * np.pi / length * signed.astype(jnp.float32)
    return scaled * scaled


def per_device(thermal_scalars, conductive_number):
    scalars, planes, lines, length = thermal_scalars.shape
    walls, groups = lax.axis_size("wall"), lax.axis_size("row")
    length_x = lines * groups
    waves = length // (walls * groups)
    rates = lax.all_gather(conductive_number, "wall", axis=1, tiled=True)
    own = slot(lax.axis_index("wall"), lax.axis_index("row"), groups)
    place = own * waves + jnp.arange(waves, dtype=jnp.int32)
    square_y = signed_square(wave_order(place, length), length)[:, None]
    square_x = signed_square(wave_order(jnp.arange(length_x), length_x), length_x)[None, :]
    fits = lines == 64 and planes % 2 == 0 and waves % 8 == 0 and groups % 8 == 0
    if fits and length == length_x and walls * groups % 4 == 0:
        return with_kernels(thermal_scalars, rates, walls, square_y, square_x, tables_of(length))
    return with_arrays(
        thermal_scalars, rates, walls, square_y, square_x, tables_of(length), tables_of(length_x)
    )


def solution(mesh):
    return jax.shard_map(
        per_device,
        mesh=mesh,
        in_specs=(P(None, "wall", "row", None), P(None, "wall")),
        out_specs=P(None, "wall", "row", None),
        check_vma=False,
    )
```

```python
import functools

import jax
import jax.numpy as jnp
import ml_dtypes
import numpy as np
from jax import lax
from jax.experimental import pallas as pl
from jax.experimental.pallas import tpu as pltpu
from jax.sharding import PartitionSpec as P

STEPS = 3
AXES = ("wall", "row")
LEVELS = 4
MIB = 1024 * 1024
TABLE_BYTES = 13 * MIB


def wave_order(place, length):
    quarter = length // 4
    even = jnp.where(place < quarter, 4 * place, 4 * (place - quarter) + 2)
    return jnp.where(place < 2 * quarter, even, 2 * (place - 2 * quarter) + 1)


def cas_table(length, first, step):
    size = length // step
    waves = first + step * np.arange(size, dtype=np.int64)
    samples = np.arange(size, dtype=np.int64)
    angle = (waves[:, None] * samples[None, :] % length) * (2.0 * np.pi / length)
    table = np.cos(angle) + np.sin(angle)
    high = table.astype(np.float32).astype(ml_dtypes.bfloat16)
    low = (table - high.astype(np.float64)).astype(np.float32).astype(ml_dtypes.bfloat16)
    return np.stack([high, low])


def tables_of(length):
    even = np.stack([cas_table(length, 0, 4), cas_table(length, 2, 4)])
    return even, cas_table(length, 1, 2)


def fold(q):
    low, high = q[0] + q[2], q[1] + q[3]
    return low + high, low - high, q[0] - q[2], q[1] - q[3]


def unfold(first, second, third, fourth):
    low, high = first + second, first - second
    return low + third, high + fourth, low - third, high - fourth


def split(value):
    high = value.astype(jnp.bfloat16)
    low = (value - high.astype(jnp.float32)).astype(jnp.bfloat16)
    return high, low


def product(a, b, dims):
    left = jnp.concatenate([a[0], a[1], a[0]], axis=dims[0][0])
    right = jnp.concatenate([b[0], b[0], b[1]], axis=dims[1][0])
    return lax.dot_general(left, right, (dims, ((), ())), preferred_element_type=jnp.float32)


NN = ((1,), (0,))
NT = ((1,), (1,))


def stacked(tables, rows):
    even, odd = tables
    top = np.concatenate([even[0], even[1]], axis=2)
    rest = np.zeros((2, rows - top.shape[1] - odd.shape[1], odd.shape[2]), odd.dtype)
    return np.concatenate([top, odd, rest], axis=1)


def part_tables(even_ref, odd_ref):
    quarter = even_ref.shape[1]
    columns = (slice(0, quarter), slice(quarter, 2 * quarter))
    return [(even_ref[0, :, c], even_ref[1, :, c]) for c in columns] + [(odd_ref[0], odd_ref[1])]


def even_copy(table_hbm, even_ref, sem):
    rows = pl.ds(0, even_ref.shape[1])
    return pltpu.make_async_copy(table_hbm.at[:, rows], even_ref, sem)


def odd_copy(table_hbm, odd_ref, sem):
    rows = pl.ds(odd_ref.shape[1] // 2, odd_ref.shape[1])
    return pltpu.make_async_copy(table_hbm.at[:, rows], odd_ref, sem)


def part_ranges(total):
    return (0, total // 4), (total // 4, total // 2), (total // 2, total)


def slot(w, r, groups):
    per_level = groups // LEVELS
    return (w * per_level + r % per_level) * LEVELS + r // per_level


def y_forward_kernel(
    field_hbm, table_hbm, out_hbm, odd_ref, field_ref, even_ref, out_ref, in_sem, table_sem, out_sem
):
    scalars, planes, lines, length = field_ref.shape
    rows = planes * lines
    quarter = length // 4
    ranges = part_ranges(out_ref.shape[0])
    loads = [
        pltpu.make_async_copy(field_hbm.at[s], field_ref.at[s], in_sem.at[s]) for s in range(scalars)
    ]
    even_load = even_copy(table_hbm, even_ref, table_sem.at[0])
    odd_load = odd_copy(table_hbm, odd_ref, table_sem.at[1])
    loads[0].start()
    even_load.start()
    odd_load.start()
    for load in loads[1:]:
        load.start()
    stores = []
    for s in range(scalars):
        loads[s].wait()
        first, second, third, fourth = fold([
            field_ref[s, :, :, q * quarter : (q + 1) * quarter].reshape(rows, quarter) for q in range(4)
        ])
        parts = [split(v) for v in (first, second, jnp.concatenate([third, fourth], axis=1))]
        for p in (0, 1, 2) if s == 0 else (2, 0, 1):
            if s == 0 and p == 0:
                even_load.wait()
            if s == 0 and p == 2:
                odd_load.wait()
            low, high = ranges[p]
            out_ref[low:high, s] = product(part_tables(even_ref, odd_ref)[p], parts[p], NT).reshape(high - low, -1, rows)
            store = pltpu.make_async_copy(
                out_ref.at[pl.ds(low, high - low), s],
                out_hbm.at[pl.ds(low, high - low), s],
                out_sem.at[s, p],
            )
            store.start()
            stores.append(store)
    for store in stores:
        store.wait()


def y_inverse_kernel(
    norm, odd_ref, spectrum_ref, table_hbm, out_hbm, even_ref, out_ref, table_sem, out_sem
):
    even_load = even_copy(table_hbm, even_ref, table_sem.at[0])
    even_load.start()
    devices, scalars, waves, rows = spectrum_ref.shape
    planes, lines, length = out_ref.shape[1:]
    quarter = length // 4
    ranges = part_ranges(devices)
    stores = []
    for s in range(scalars):
        parts = {}
        for p in (2, 0, 1):
            low, high = ranges[p]
            turned = split(spectrum_ref[low:high, s].reshape(-1, rows).T)
            if s == 0 and p == 0:
                even_load.wait()
            parts[p] = product(turned, part_tables(even_ref, odd_ref)[p], NN)
        first, second, third = (parts[p] for p in range(3))
        quarters = unfold(first * norm, second * norm, third[:, :quarter] * norm, third[:, quarter:] * norm)
        for q, value in enumerate(quarters):
            out_ref[s, :, :, q * quarter : (q + 1) * quarter] = value.reshape(planes, lines, quarter)
        for z in range(planes):
            store = pltpu.make_async_copy(out_ref.at[s, z], out_hbm.at[s, z], out_sem.at[s, z])
            store.start()
            stores.append(store)
    for store in stores:
        store.wait()


def x_kernel(
    walls, rate_ref, square_y_ref, square_x_ref, odd_ref, received_ref, table_hbm, out_ref, even_ref,
    table_sem, *line_refs
):
    even_load = even_copy(table_hbm, even_ref, table_sem.at[0])
    even_load.start()
    devices, scalars, waves, rows = received_ref.shape
    groups = devices // walls
    length = line_refs[0].shape[1]
    quarter = length // 4
    lines = length // groups
    planes = rows // lines
    count = walls * planes
    lower = lax.broadcasted_iota(jnp.int32, (waves, 128), 1) < lines
    ranges = part_ranges(length)

    def paired(a, b):
        return (
            jnp.where(lower, a, pltpu.roll(b, lines, 1)),
            jnp.where(lower, pltpu.roll(a, lines, 1), b),
        )

    def tiles():
        for w in range(walls):
            for p in range(planes // 2):
                yield w, slice(128 * p, 128 * (p + 1)), (w * planes + 2 * p) * waves

    def forward(s):
        line_ref = line_refs[s]
        for w, lanes, top in tiles():
            for i in range(groups // 8):
                left, right = (
                    fold([
                        received_ref[slot(w, groups // 4 * q + 2 * i + side, groups), s, :, lanes]
                        for q in range(4)
                    ])
                    for side in range(2)
                )
                for q in range(4):
                    a, b = paired(left[q], right[q])
                    columns = slice(quarter * q + 128 * i, quarter * q + 128 * (i + 1))
                    line_ref[top : top + waves, columns] = a
                    line_ref[top + waves : top + 2 * waves, columns] = b
        if s == 0:
            even_load.wait()
        for table, (low, high) in zip(part_tables(even_ref, odd_ref), ranges):
            line_ref[:, low:high] = product(split(line_ref[:, low:high]), table, NT)

    def diffuse(s):
        line_ref = line_refs[s]
        rates = [rate_ref[s, z] for z in range(count)]
        damping_y = [jnp.exp(-rate * square_y_ref[...]) for rate in rates]
        for j in range(length // 128):
            columns = slice(128 * j, 128 * (j + 1))
            square_x = square_x_ref[:, columns]
            damping = [jnp.exp(-rate * square_x) * dy for rate, dy in zip(rates, damping_y)]
            field = [line_ref[z * waves : (z + 1) * waves, columns] for z in range(count)]
            for step in range(STEPS):
                updated = []
                for z in range(count):
                    value = (1.0 - 2.0 * rates[z]) * field[z]
                    if z == 0:
                        around = field[1]
                    elif z == count - 1:
                        around = field[z - 1]
                    else:
                        around = field[z - 1] + field[z + 1]
                    updated.append(damping[z] * (value + rates[z] * around))
                field = updated
            for z in range(count):
                line_ref[z * waves : (z + 1) * waves, columns] = field[z]

    def inverse(s):
        line_ref = line_refs[s]
        first, second, third = (
            product(split(line_ref[:, low:high]), table, NN)
            for table, (low, high) in zip(part_tables(even_ref, odd_ref), ranges)
        )
        quarters = unfold(first, second, third[:, :quarter], third[:, quarter:])
        for q, value in enumerate(quarters):
            line_ref[:, q * quarter : (q + 1) * quarter] = value
        for w, lanes, top in tiles():
            for j in range(groups // 2):
                columns = slice(128 * j, 128 * (j + 1))
                a, b = paired(
                    line_ref[top : top + waves, columns],
                    line_ref[top + waves : top + 2 * waves, columns],
                )
                out_ref[slot(w, 2 * j, groups), s, :, lanes] = a
                out_ref[slot(w, 2 * j + 1, groups), s, :, lanes] = b

    for phase in (forward, diffuse, inverse):
        for s in range(scalars):
            phase(s)


def grant(mebibytes):
    return pltpu.CompilerParams(vmem_limit_bytes=int(mebibytes * MIB))


VMEM = pl.BlockSpec(memory_space=pltpu.VMEM)
ANY = pl.BlockSpec(memory_space=pl.ANY)


def cost(terms, total):
    return pl.CostEstimate(flops=2 * terms, bytes_accessed=total, transcendentals=0)


def with_kernels(fields, rates, walls, square_y, square_x, tables):
    scalars, planes, lines, length = fields.shape
    groups = lax.axis_size("row")
    devices = walls * groups
    waves = length // devices
    rows = planes * lines
    blocks = jax.ShapeDtypeStruct((devices, scalars, waves, rows), jnp.float32)
    total = 8 * scalars * rows * length
    work = 9 * scalars * rows * length * length // 8
    table = stacked(tables, TABLE_BYTES // (2 * length))
    even_scratch = pltpu.VMEM((2, length // 4, length // 2), jnp.bfloat16)
    odd_shape = jax.ShapeDtypeStruct((2, length // 2, length // 2), jnp.bfloat16)

    spectrum, odd = pl.pallas_call(
        y_forward_kernel,
        in_specs=[ANY] * 2,
        out_specs=[ANY, VMEM],
        out_shape=[blocks, odd_shape],
        scratch_shapes=[
            pltpu.VMEM(fields.shape, jnp.float32),
            even_scratch,
            pltpu.VMEM(blocks.shape, jnp.float32),
            pltpu.SemaphoreType.DMA((scalars,)),
            pltpu.SemaphoreType.DMA((2,)),
            pltpu.SemaphoreType.DMA((scalars, 3)),
        ],
        compiler_params=grant(52),
        cost_estimate=cost(work, total),
        name="y_forward",
    )(fields, table)
    filtered = pl.pallas_call(
        functools.partial(x_kernel, walls),
        in_specs=[pl.BlockSpec(memory_space=pltpu.SMEM)] + [VMEM] * 4 + [ANY],
        out_specs=VMEM,
        out_shape=blocks,
        scratch_shapes=[
            even_scratch,
            pltpu.SemaphoreType.DMA((1,)),
            *[pltpu.VMEM((walls * planes * waves, lines * groups), jnp.float32)] * scalars,
        ],
        compiler_params=grant(48),
        cost_estimate=cost(2 * work, total),
        name="x_filter",
    )(rates, square_y, square_x, odd, exchange(spectrum), table)
    return pl.pallas_call(
        functools.partial(y_inverse_kernel, 1.0 / (length * lines * groups)),
        in_specs=[VMEM] * 2 + [ANY],
        out_specs=ANY,
        out_shape=jax.ShapeDtypeStruct(fields.shape, jnp.float32),
        scratch_shapes=[
            even_scratch,
            pltpu.VMEM(fields.shape, jnp.float32),
            pltpu.SemaphoreType.DMA((1,)),
            pltpu.SemaphoreType.DMA((scalars, planes)),
        ],
        compiler_params=grant(48),
        cost_estimate=cost(work, total),
        name="y_inverse",
    )(odd, exchange(filtered), table)


def exchange(blocks):
    walls, groups = lax.axis_size("wall"), lax.axis_size("row")
    members = {slot(w, r, groups): w * groups + r for w in range(walls) for r in range(groups)}
    return lax.all_to_all(
        blocks, AXES, split_axis=0, concat_axis=0, tiled=True,
        axis_index_groups=[[members[i] for i in range(len(members))]],
    )


def with_arrays(fields, rates, walls, square_y, square_x, y_tables, x_tables):
    scalars, planes, lines, length = fields.shape
    groups = lax.axis_size("row")
    devices = walls * groups
    waves = length // devices
    count = walls * planes
    order = np.array([slot(w, r, groups) for w in range(walls) for r in range(groups)])
    dot = functools.partial(jnp.matmul, precision=lax.Precision.HIGHEST)

    def whole(tables):
        pairs = [jnp.asarray(t).astype(jnp.float32) for t in (*tables[0], tables[1])]
        return [t[0] + t[1] for t in pairs]

    def forward(value, tables):
        first, second, third, fourth = fold(jnp.split(value, 4, axis=-1))
        parts = (first, second, jnp.concatenate([third, fourth], axis=-1))
        return jnp.concatenate([dot(v, t.T) for v, t in zip(parts, whole(tables))], axis=-1)

    def inverse(value, tables):
        parts = jnp.split(value, [value.shape[-1] // 4, value.shape[-1] // 2], axis=-1)
        first, second, third = (dot(v, t) for v, t in zip(parts, whole(tables)))
        return jnp.concatenate(unfold(first, second, *jnp.split(third, 2, axis=-1)), axis=-1)

    results = []
    for s in range(scalars):
        spectral = forward(fields[s], y_tables).reshape(planes * lines, devices, waves)
        received = exchange(spectral.transpose(1, 2, 0))[order]
        received = received.reshape(walls, groups, waves, planes, lines).transpose(0, 3, 2, 1, 4)
        field = forward(received.reshape(count, waves, groups * lines), x_tables)
        rate = rates[s][:, None, None]
        damping = jnp.exp(-rate * (square_y + square_x))
        for step in range(STEPS):
            padded = jnp.pad(field, ((1, 1), (0, 0), (0, 0)))
            field = damping * (field + rate * (padded[2:] + padded[:-2] - 2.0 * field))
        back = inverse(field, x_tables).reshape(walls, planes, waves, groups, lines)
        back = back.transpose(0, 3, 2, 1, 4).reshape(devices, waves, planes * lines)
        spectrum = exchange(back[np.argsort(order)]).reshape(length, -1)
        results.append(inverse(spectrum.T, y_tables).reshape(planes, lines, length))
    return jnp.stack(results) * (1.0 / (length * groups * lines))


def signed_square(waves, length):
    signed = jnp.where(waves > length // 2, waves - length, waves)
    scaled = 2.0 * np.pi / length * signed.astype(jnp.float32)
    return scaled * scaled


def per_device(thermal_scalars, conductive_number):
    scalars, planes, lines, length = thermal_scalars.shape
    walls, groups = lax.axis_size("wall"), lax.axis_size("row")
    length_x = lines * groups
    waves = length // (walls * groups)
    rates = lax.all_gather(conductive_number, "wall", axis=1, tiled=True)
    own = slot(lax.axis_index("wall"), lax.axis_index("row"), groups)
    place = own * waves + jnp.arange(waves, dtype=jnp.int32)
    square_y = signed_square(wave_order(place, length), length)[:, None]
    square_x = signed_square(wave_order(jnp.arange(length_x), length_x), length_x)[None, :]
    fits = lines == 64 and planes % 2 == 0 and waves % 8 == 0 and groups % 8 == 0
    if fits and length == length_x and walls * groups % 4 == 0:
        return with_kernels(thermal_scalars, rates, walls, square_y, square_x, tables_of(length))
    return with_arrays(
        thermal_scalars, rates, walls, square_y, square_x, tables_of(length), tables_of(length_x)
    )


def solution(mesh):
    return jax.shard_map(
        per_device,
        mesh=mesh,
        in_specs=(P(None, "wall", "row", None), P(None, "wall")),
        out_specs=P(None, "wall", "row", None),
        check_vma=False,
    )
```

```python
import functools

import jax
import jax.numpy as jnp
import ml_dtypes
import numpy as np
from jax import lax
from jax.experimental import pallas as pl
from jax.experimental.pallas import tpu as pltpu
from jax.sharding import PartitionSpec as P

STEPS = 3
AXES = ("wall", "row")
LEVELS = 4
MIB = 1024 * 1024
TABLE_BYTES = 13 * MIB


def wave_order(place, length):
    quarter = length // 4
    even = jnp.where(place < quarter, 4 * place, 4 * (place - quarter) + 2)
    return jnp.where(place < 2 * quarter, even, 2 * (place - 2 * quarter) + 1)


def cas_table(length, first, step):
    size = length // step
    waves = first + step * np.arange(size, dtype=np.int64)
    samples = np.arange(size, dtype=np.int64)
    angle = (waves[:, None] * samples[None, :] % length) * (2.0 * np.pi / length)
    table = np.cos(angle) + np.sin(angle)
    high = table.astype(np.float32).astype(ml_dtypes.bfloat16)
    low = (table - high.astype(np.float64)).astype(np.float32).astype(ml_dtypes.bfloat16)
    return np.stack([high, low])


def tables_of(length):
    even = np.stack([cas_table(length, 0, 4), cas_table(length, 2, 4)])
    return even, cas_table(length, 1, 2)


def fold(q):
    low, high = q[0] + q[2], q[1] + q[3]
    return low + high, low - high, q[0] - q[2], q[1] - q[3]


def unfold(first, second, third, fourth):
    low, high = first + second, first - second
    return low + third, high + fourth, low - third, high - fourth


def split(value):
    high = value.astype(jnp.bfloat16)
    low = (value - high.astype(jnp.float32)).astype(jnp.bfloat16)
    return high, low


def product(a, b, dims):
    left = jnp.concatenate([a[0], a[1], a[0]], axis=dims[0][0])
    right = jnp.concatenate([b[0], b[0], b[1]], axis=dims[1][0])
    return lax.dot_general(left, right, (dims, ((), ())), preferred_element_type=jnp.float32)


NN = ((1,), (0,))
NT = ((1,), (1,))


def stacked(tables, rows):
    even, odd = tables
    top = np.concatenate([even[0], even[1]], axis=2)
    rest = np.zeros((2, rows - top.shape[1] - odd.shape[1], odd.shape[2]), odd.dtype)
    return np.concatenate([top, odd, rest], axis=1)


def part_tables(even_ref, odd_ref):
    quarter = even_ref.shape[1]
    columns = (slice(0, quarter), slice(quarter, 2 * quarter))
    return [(even_ref[0, :, c], even_ref[1, :, c]) for c in columns] + [(odd_ref[0], odd_ref[1])]


def even_copy(table_hbm, even_ref, sem):
    rows = pl.ds(0, even_ref.shape[1])
    return pltpu.make_async_copy(table_hbm.at[:, rows], even_ref, sem)


def odd_copy(table_hbm, odd_ref, sem):
    rows = pl.ds(odd_ref.shape[1] // 2, odd_ref.shape[1])
    return pltpu.make_async_copy(table_hbm.at[:, rows], odd_ref, sem)


def part_ranges(total):
    return (0, total // 4), (total // 4, total // 2), (total // 2, total)


def slot(w, r, groups):
    per_level = groups // LEVELS
    return (w * per_level + r % per_level) * LEVELS + r // per_level


def y_forward_kernel(
    field_hbm, table_hbm, out_hbm, odd_ref, field_ref, even_ref, out_ref, in_sem, table_sem, out_sem
):
    scalars, planes, lines, length = field_ref.shape
    rows = planes * lines
    quarter = length // 4
    ranges = part_ranges(out_ref.shape[0])
    loads = [
        pltpu.make_async_copy(field_hbm.at[s], field_ref.at[s], in_sem.at[s]) for s in range(scalars)
    ]
    even_load = even_copy(table_hbm, even_ref, table_sem.at[0])
    odd_load = odd_copy(table_hbm, odd_ref, table_sem.at[1])
    loads[0].start()
    even_load.start()
    odd_load.start()
    for load in loads[1:]:
        load.start()
    stores = []
    for s in range(scalars):
        loads[s].wait()
        first, second, third, fourth = fold([
            field_ref[s, :, :, q * quarter : (q + 1) * quarter].reshape(rows, quarter) for q in range(4)
        ])
        parts = [split(v) for v in (first, second, jnp.concatenate([third, fourth], axis=1))]
        for p in (0, 1, 2) if s == 0 else (2, 0, 1):
            if s == 0 and p == 0:
                even_load.wait()
            if s == 0 and p == 2:
                odd_load.wait()
            low, high = ranges[p]
            out_ref[low:high, s] = product(part_tables(even_ref, odd_ref)[p], parts[p], NT).reshape(high - low, -1, rows)
            store = pltpu.make_async_copy(
                out_ref.at[pl.ds(low, high - low), s],
                out_hbm.at[pl.ds(low, high - low), s],
                out_sem.at[s, p],
            )
            store.start()
            stores.append(store)
    for store in stores:
        store.wait()


def y_inverse_kernel(norm, even_ref, odd_ref, spectrum_ref, out_hbm, out_ref, out_sem):
    devices, scalars, waves, rows = spectrum_ref.shape
    planes, lines, length = out_ref.shape[1:]
    quarter = length // 4
    ranges = part_ranges(devices)
    stores = []
    for s in range(scalars):
        first, second, third = (
            product(split(spectrum_ref[low:high, s].reshape(-1, rows).T), table, NN)
            for table, (low, high) in zip(part_tables(even_ref, odd_ref), ranges)
        )
        quarters = unfold(first * norm, second * norm, third[:, :quarter] * norm, third[:, quarter:] * norm)
        for q, value in enumerate(quarters):
            out_ref[s, :, :, q * quarter : (q + 1) * quarter] = value.reshape(planes, lines, quarter)
        for z in range(planes):
            store = pltpu.make_async_copy(out_ref.at[s, z], out_hbm.at[s, z], out_sem.at[s, z])
            store.start()
            stores.append(store)
    for store in stores:
        store.wait()


def x_kernel(
    walls, rate_ref, square_y_ref, square_x_ref, odd_ref, received_ref, table_hbm, out_ref, even_ref,
    table_sem, *line_refs
):
    even_load = even_copy(table_hbm, even_ref, table_sem.at[0])
    even_load.start()
    devices, scalars, waves, rows = received_ref.shape
    groups = devices // walls
    length = line_refs[0].shape[1]
    quarter = length // 4
    lines = length // groups
    planes = rows // lines
    count = walls * planes
    lower = lax.broadcasted_iota(jnp.int32, (waves, 128), 1) < lines
    ranges = part_ranges(length)

    def paired(a, b):
        return (
            jnp.where(lower, a, pltpu.roll(b, lines, 1)),
            jnp.where(lower, pltpu.roll(a, lines, 1), b),
        )

    def tiles():
        for w in range(walls):
            for p in range(planes // 2):
                yield w, slice(128 * p, 128 * (p + 1)), (w * planes + 2 * p) * waves

    def forward(s):
        line_ref = line_refs[s]
        for w, lanes, top in tiles():
            for i in range(groups // 8):
                left, right = (
                    fold([
                        received_ref[slot(w, groups // 4 * q + 2 * i + side, groups), s, :, lanes]
                        for q in range(4)
                    ])
                    for side in range(2)
                )
                for q in range(4):
                    a, b = paired(left[q], right[q])
                    columns = slice(quarter * q + 128 * i, quarter * q + 128 * (i + 1))
                    line_ref[top : top + waves, columns] = a
                    line_ref[top + waves : top + 2 * waves, columns] = b
        for p in (2, 0, 1):
            low, high = ranges[p]
            if s == 0 and p == 0:
                even_load.wait()
            table = part_tables(even_ref, odd_ref)[p]
            line_ref[:, low:high] = product(split(line_ref[:, low:high]), table, NT)

    def diffuse(s):
        line_ref = line_refs[s]
        rates = [rate_ref[s, z] for z in range(count)]
        damping_y = [jnp.exp(-rate * square_y_ref[...]) for rate in rates]
        for j in range(length // 128):
            columns = slice(128 * j, 128 * (j + 1))
            square_x = square_x_ref[:, columns]
            damping = [jnp.exp(-rate * square_x) * dy for rate, dy in zip(rates, damping_y)]
            field = [line_ref[z * waves : (z + 1) * waves, columns] for z in range(count)]
            for step in range(STEPS):
                updated = []
                for z in range(count):
                    value = (1.0 - 2.0 * rates[z]) * field[z]
                    if z == 0:
                        around = field[1]
                    elif z == count - 1:
                        around = field[z - 1]
                    else:
                        around = field[z - 1] + field[z + 1]
                    updated.append(damping[z] * (value + rates[z] * around))
                field = updated
            for z in range(count):
                line_ref[z * waves : (z + 1) * waves, columns] = field[z]

    def inverse(s):
        line_ref = line_refs[s]
        first, second, third = (
            product(split(line_ref[:, low:high]), table, NN)
            for table, (low, high) in zip(part_tables(even_ref, odd_ref), ranges)
        )
        quarters = unfold(first, second, third[:, :quarter], third[:, quarter:])
        for q, value in enumerate(quarters):
            line_ref[:, q * quarter : (q + 1) * quarter] = value
        for w, lanes, top in tiles():
            for j in range(groups // 2):
                columns = slice(128 * j, 128 * (j + 1))
                a, b = paired(
                    line_ref[top : top + waves, columns],
                    line_ref[top + waves : top + 2 * waves, columns],
                )
                out_ref[slot(w, 2 * j, groups), s, :, lanes] = a
                out_ref[slot(w, 2 * j + 1, groups), s, :, lanes] = b

    for phase in (forward, diffuse, inverse):
        for s in range(scalars):
            phase(s)


def grant(mebibytes):
    return pltpu.CompilerParams(vmem_limit_bytes=int(mebibytes * MIB))


VMEM = pl.BlockSpec(memory_space=pltpu.VMEM)
ANY = pl.BlockSpec(memory_space=pl.ANY)


def cost(terms, total):
    return pl.CostEstimate(flops=2 * terms, bytes_accessed=total, transcendentals=0)


def with_kernels(fields, rates, walls, square_y, square_x, tables):
    scalars, planes, lines, length = fields.shape
    groups = lax.axis_size("row")
    devices = walls * groups
    waves = length // devices
    rows = planes * lines
    blocks = jax.ShapeDtypeStruct((devices, scalars, waves, rows), jnp.float32)
    total = 8 * scalars * rows * length
    work = 9 * scalars * rows * length * length // 8
    table = stacked(tables, TABLE_BYTES // (2 * length))
    even_scratch = pltpu.VMEM((2, length // 4, length // 2), jnp.bfloat16)
    odd_shape = jax.ShapeDtypeStruct((2, length // 2, length // 2), jnp.bfloat16)

    spectrum, odd = pl.pallas_call(
        y_forward_kernel,
        in_specs=[ANY] * 2,
        out_specs=[ANY, VMEM],
        out_shape=[blocks, odd_shape],
        scratch_shapes=[
            pltpu.VMEM(fields.shape, jnp.float32),
            even_scratch,
            pltpu.VMEM(blocks.shape, jnp.float32),
            pltpu.SemaphoreType.DMA((scalars,)),
            pltpu.SemaphoreType.DMA((2,)),
            pltpu.SemaphoreType.DMA((scalars, 3)),
        ],
        compiler_params=grant(52),
        cost_estimate=cost(work, total),
        name="y_forward",
    )(fields, table)
    filtered, even = pl.pallas_call(
        functools.partial(x_kernel, walls),
        in_specs=[pl.BlockSpec(memory_space=pltpu.SMEM)] + [VMEM] * 4 + [ANY],
        out_specs=[VMEM] * 2,
        out_shape=[blocks, jax.ShapeDtypeStruct(even_scratch.shape, jnp.bfloat16)],
        scratch_shapes=[
            pltpu.SemaphoreType.DMA((1,)),
            *[pltpu.VMEM((walls * planes * waves, lines * groups), jnp.float32)] * scalars,
        ],
        compiler_params=grant(46),
        cost_estimate=cost(2 * work, total),
        name="x_filter",
    )(rates, square_y, square_x, odd, exchange(spectrum), table)
    return pl.pallas_call(
        functools.partial(y_inverse_kernel, 1.0 / (length * lines * groups)),
        in_specs=[VMEM] * 3,
        out_specs=ANY,
        out_shape=jax.ShapeDtypeStruct(fields.shape, jnp.float32),
        scratch_shapes=[
            pltpu.VMEM(fields.shape, jnp.float32),
            pltpu.SemaphoreType.DMA((scalars, planes)),
        ],
        compiler_params=grant(48),
        cost_estimate=cost(work, total),
        name="y_inverse",
    )(even, odd, exchange(filtered))


def exchange(blocks):
    walls, groups = lax.axis_size("wall"), lax.axis_size("row")
    members = {slot(w, r, groups): w * groups + r for w in range(walls) for r in range(groups)}
    return lax.all_to_all(
        blocks, AXES, split_axis=0, concat_axis=0, tiled=True,
        axis_index_groups=[[members[i] for i in range(len(members))]],
    )


def with_arrays(fields, rates, walls, square_y, square_x, y_tables, x_tables):
    scalars, planes, lines, length = fields.shape
    groups = lax.axis_size("row")
    devices = walls * groups
    waves = length // devices
    count = walls * planes
    order = np.array([slot(w, r, groups) for w in range(walls) for r in range(groups)])
    dot = functools.partial(jnp.matmul, precision=lax.Precision.HIGHEST)

    def whole(tables):
        pairs = [jnp.asarray(t).astype(jnp.float32) for t in (*tables[0], tables[1])]
        return [t[0] + t[1] for t in pairs]

    def forward(value, tables):
        first, second, third, fourth = fold(jnp.split(value, 4, axis=-1))
        parts = (first, second, jnp.concatenate([third, fourth], axis=-1))
        return jnp.concatenate([dot(v, t.T) for v, t in zip(parts, whole(tables))], axis=-1)

    def inverse(value, tables):
        parts = jnp.split(value, [value.shape[-1] // 4, value.shape[-1] // 2], axis=-1)
        first, second, third = (dot(v, t) for v, t in zip(parts, whole(tables)))
        return jnp.concatenate(unfold(first, second, *jnp.split(third, 2, axis=-1)), axis=-1)

    results = []
    for s in range(scalars):
        spectral = forward(fields[s], y_tables).reshape(planes * lines, devices, waves)
        received = exchange(spectral.transpose(1, 2, 0))[order]
        received = received.reshape(walls, groups, waves, planes, lines).transpose(0, 3, 2, 1, 4)
        field = forward(received.reshape(count, waves, groups * lines), x_tables)
        rate = rates[s][:, None, None]
        damping = jnp.exp(-rate * (square_y + square_x))
        for step in range(STEPS):
            padded = jnp.pad(field, ((1, 1), (0, 0), (0, 0)))
            field = damping * (field + rate * (padded[2:] + padded[:-2] - 2.0 * field))
        back = inverse(field, x_tables).reshape(walls, planes, waves, groups, lines)
        back = back.transpose(0, 3, 2, 1, 4).reshape(devices, waves, planes * lines)
        spectrum = exchange(back[np.argsort(order)]).reshape(length, -1)
        results.append(inverse(spectrum.T, y_tables).reshape(planes, lines, length))
    return jnp.stack(results) * (1.0 / (length * groups * lines))


def signed_square(waves, length):
    signed = jnp.where(waves > length // 2, waves - length, waves)
    scaled = 2.0 * np.pi / length * signed.astype(jnp.float32)
    return scaled * scaled


def per_device(thermal_scalars, conductive_number):
    scalars, planes, lines, length = thermal_scalars.shape
    walls, groups = lax.axis_size("wall"), lax.axis_size("row")
    length_x = lines * groups
    waves = length // (walls * groups)
    rates = lax.all_gather(conductive_number, "wall", axis=1, tiled=True)
    own = slot(lax.axis_index("wall"), lax.axis_index("row"), groups)
    place = own * waves + jnp.arange(waves, dtype=jnp.int32)
    square_y = signed_square(wave_order(place, length), length)[:, None]
    square_x = signed_square(wave_order(jnp.arange(length_x), length_x), length_x)[None, :]
    fits = lines == 64 and planes % 2 == 0 and waves % 8 == 0 and groups % 8 == 0
    if fits and length == length_x and walls * groups % 4 == 0:
        return with_kernels(thermal_scalars, rates, walls, square_y, square_x, tables_of(length))
    return with_arrays(
        thermal_scalars, rates, walls, square_y, square_x, tables_of(length), tables_of(length_x)
    )


def solution(mesh):
    return jax.shard_map(
        per_device,
        mesh=mesh,
        in_specs=(P(None, "wall", "row", None), P(None, "wall")),
        out_specs=P(None, "wall", "row", None),
        check_vma=False,
    )
```

```python
import functools

import jax
import jax.numpy as jnp
import ml_dtypes
import numpy as np
from jax import lax
from jax.experimental import pallas as pl
from jax.experimental.pallas import tpu as pltpu
from jax.sharding import PartitionSpec as P

STEPS = 3
AXES = ("wall", "row")
LEVELS = 4
MIB = 1024 * 1024
TABLE_BYTES = 13 * MIB


def wave_order(place, length):
    quarter = length // 4
    even = jnp.where(place < quarter, 4 * place, 4 * (place - quarter) + 2)
    return jnp.where(place < 2 * quarter, even, 2 * (place - 2 * quarter) + 1)


def cas_table(length, first, step):
    size = length // step
    waves = first + step * np.arange(size, dtype=np.int64)
    samples = np.arange(size, dtype=np.int64)
    angle = (waves[:, None] * samples[None, :] % length) * (2.0 * np.pi / length)
    table = np.cos(angle) + np.sin(angle)
    high = table.astype(np.float32).astype(ml_dtypes.bfloat16)
    low = (table - high.astype(np.float64)).astype(np.float32).astype(ml_dtypes.bfloat16)
    return np.stack([high, low])


def tables_of(length):
    even = np.stack([cas_table(length, 0, 4), cas_table(length, 2, 4)])
    return even, cas_table(length, 1, 2)


def fold(q):
    low, high = q[0] + q[2], q[1] + q[3]
    return low + high, low - high, q[0] - q[2], q[1] - q[3]


def unfold(first, second, third, fourth):
    low, high = first + second, first - second
    return low + third, high + fourth, low - third, high - fourth


def split(value):
    high = value.astype(jnp.bfloat16)
    low = (value - high.astype(jnp.float32)).astype(jnp.bfloat16)
    return high, low


def product(a, b, dims):
    left = jnp.concatenate([a[0], a[1], a[0]], axis=dims[0][0])
    right = jnp.concatenate([b[0], b[0], b[1]], axis=dims[1][0])
    return lax.dot_general(left, right, (dims, ((), ())), preferred_element_type=jnp.float32)


NN = ((1,), (0,))
NT = ((1,), (1,))


def stacked(tables, rows):
    even, odd = tables
    top = np.concatenate([even[0], even[1]], axis=2)
    rest = np.zeros((2, rows - top.shape[1] - odd.shape[1], odd.shape[2]), odd.dtype)
    return np.concatenate([top, odd, rest], axis=1)


def part_tables(table_ref):
    quarter = table_ref.shape[2] // 2
    places = (
        (slice(0, quarter), slice(0, quarter)),
        (slice(0, quarter), slice(quarter, 2 * quarter)),
        (slice(quarter, 3 * quarter), slice(0, 2 * quarter)),
    )
    return [(table_ref[0, rows, columns], table_ref[1, rows, columns]) for rows, columns in places]


def table_loads(table_hbm, table_ref, sem):
    quarter = table_ref.shape[2] // 2
    return [
        pltpu.make_async_copy(table_hbm.at[:, rows], table_ref.at[:, rows], sem.at[i])
        for i, rows in enumerate((pl.ds(0, quarter), pl.ds(quarter, 2 * quarter)))
    ]


def part_ranges(total):
    return (0, total // 4), (total // 4, total // 2), (total // 2, total)


def slot(w, r, groups):
    per_level = groups // LEVELS
    return (w * per_level + r % per_level) * LEVELS + r // per_level


def y_forward_kernel(
    field_hbm, table_hbm, out_hbm, field_ref, table_ref, out_ref, in_sem, table_sem, out_sem
):
    scalars, planes, lines, length = field_ref.shape
    rows = planes * lines
    quarter = length // 4
    ranges = part_ranges(out_ref.shape[0])
    loads = [
        pltpu.make_async_copy(field_hbm.at[s], field_ref.at[s], in_sem.at[s]) for s in range(scalars)
    ]
    even_load, odd_load = table_loads(table_hbm, table_ref, table_sem)
    loads[0].start()
    even_load.start()
    odd_load.start()
    for load in loads[1:]:
        load.start()
    stores = []
    for s in range(scalars):
        loads[s].wait()
        first, second, third, fourth = fold([
            field_ref[s, :, :, q * quarter : (q + 1) * quarter].reshape(rows, quarter) for q in range(4)
        ])
        parts = [split(v) for v in (first, second, jnp.concatenate([third, fourth], axis=1))]
        for p in (0, 1, 2) if s == 0 else (2, 0, 1):
            if s == 0 and p == 0:
                even_load.wait()
            if s == 0 and p == 2:
                odd_load.wait()
            low, high = ranges[p]
            out_ref[low:high, s] = product(part_tables(table_ref)[p], parts[p], NT).reshape(high - low, -1, rows)
            store = pltpu.make_async_copy(
                out_ref.at[pl.ds(low, high - low), s],
                out_hbm.at[pl.ds(low, high - low), s],
                out_sem.at[s, p],
            )
            store.start()
            stores.append(store)
    for store in stores:
        store.wait()


def hold_kernel(after_hbm, table_hbm, table_ref, sem):
    del after_hbm
    load = pltpu.make_async_copy(table_hbm.at[:, pl.ds(0, table_ref.shape[1])], table_ref, sem.at[0])
    load.start()
    load.wait()


def y_inverse_kernel(norm, table_ref, spectrum_ref, out_hbm, out_ref, out_sem):
    devices, scalars, waves, rows = spectrum_ref.shape
    planes, lines, length = out_ref.shape[1:]
    quarter = length // 4
    tables = part_tables(table_ref)
    stores = []
    for s in range(scalars):
        first, second, third = (
            product(split(spectrum_ref[low:high, s].reshape(-1, rows).T), table, NN)
            for table, (low, high) in zip(tables, part_ranges(devices))
        )
        quarters = unfold(first * norm, second * norm, third[:, :quarter] * norm, third[:, quarter:] * norm)
        for q, value in enumerate(quarters):
            out_ref[s, :, :, q * quarter : (q + 1) * quarter] = value.reshape(planes, lines, quarter)
        for z in range(planes):
            store = pltpu.make_async_copy(out_ref.at[s, z], out_hbm.at[s, z], out_sem.at[s, z])
            store.start()
            stores.append(store)
    for store in stores:
        store.wait()


def x_kernel(
    walls, rate_ref, square_y_ref, square_x_ref, table_ref, received_ref, out_ref, *line_refs
):
    devices, scalars, waves, rows = received_ref.shape
    groups = devices // walls
    length = line_refs[0].shape[1]
    quarter = length // 4
    lines = length // groups
    planes = rows // lines
    count = walls * planes
    lower = lax.broadcasted_iota(jnp.int32, (waves, 128), 1) < lines
    tables = part_tables(table_ref)
    ranges = part_ranges(length)

    def paired(a, b):
        return (
            jnp.where(lower, a, pltpu.roll(b, lines, 1)),
            jnp.where(lower, pltpu.roll(a, lines, 1), b),
        )

    def tiles():
        for w in range(walls):
            for p in range(planes // 2):
                yield w, slice(128 * p, 128 * (p + 1)), (w * planes + 2 * p) * waves

    def forward(s):
        line_ref = line_refs[s]
        for w, lanes, top in tiles():
            for i in range(groups // 8):
                left, right = (
                    fold([
                        received_ref[slot(w, groups // 4 * q + 2 * i + side, groups), s, :, lanes]
                        for q in range(4)
                    ])
                    for side in range(2)
                )
                for q in range(4):
                    a, b = paired(left[q], right[q])
                    columns = slice(quarter * q + 128 * i, quarter * q + 128 * (i + 1))
                    line_ref[top : top + waves, columns] = a
                    line_ref[top + waves : top + 2 * waves, columns] = b
        for table, (low, high) in zip(tables, ranges):
            line_ref[:, low:high] = product(split(line_ref[:, low:high]), table, NT)

    def diffuse(s):
        line_ref = line_refs[s]
        rates = [rate_ref[s, z] for z in range(count)]
        damping_y = [jnp.exp(-rate * square_y_ref[...]) for rate in rates]
        for j in range(length // 128):
            columns = slice(128 * j, 128 * (j + 1))
            square_x = square_x_ref[:, columns]
            damping = [jnp.exp(-rate * square_x) * dy for rate, dy in zip(rates, damping_y)]
            own = [d * (1.0 - 2.0 * rate) for d, rate in zip(damping, rates)]
            share = [d * rate for d, rate in zip(damping, rates)]
            field = [line_ref[z * waves : (z + 1) * waves, columns] for z in range(count)]
            for step in range(STEPS):
                updated = []
                for z in range(count):
                    if z == 0:
                        around = field[1]
                    elif z == count - 1:
                        around = field[z - 1]
                    else:
                        around = field[z - 1] + field[z + 1]
                    updated.append(own[z] * field[z] + share[z] * around)
                field = updated
            for z in range(count):
                line_ref[z * waves : (z + 1) * waves, columns] = field[z]

    def inverse(s):
        line_ref = line_refs[s]
        first, second, third = (
            product(split(line_ref[:, low:high]), table, NN) for table, (low, high) in zip(tables, ranges)
        )
        quarters = unfold(first, second, third[:, :quarter], third[:, quarter:])
        for q, value in enumerate(quarters):
            line_ref[:, q * quarter : (q + 1) * quarter] = value
        for w, lanes, top in tiles():
            for j in range(groups // 2):
                columns = slice(128 * j, 128 * (j + 1))
                a, b = paired(
                    line_ref[top : top + waves, columns],
                    line_ref[top + waves : top + 2 * waves, columns],
                )
                out_ref[slot(w, 2 * j, groups), s, :, lanes] = a
                out_ref[slot(w, 2 * j + 1, groups), s, :, lanes] = b

    for phase in (forward, diffuse, inverse):
        for s in range(scalars):
            phase(s)


def grant(mebibytes):
    return pltpu.CompilerParams(vmem_limit_bytes=mebibytes * MIB)


VMEM = pl.BlockSpec(memory_space=pltpu.VMEM)
ANY = pl.BlockSpec(memory_space=pl.ANY)


def cost(terms, total):
    return pl.CostEstimate(flops=2 * terms, bytes_accessed=total, transcendentals=0)


def with_kernels(fields, rates, walls, square_y, square_x, tables):
    scalars, planes, lines, length = fields.shape
    groups = lax.axis_size("row")
    devices = walls * groups
    waves = length // devices
    rows = planes * lines
    blocks = jax.ShapeDtypeStruct((devices, scalars, waves, rows), jnp.float32)
    total = 8 * scalars * rows * length
    work = 9 * scalars * rows * length * length // 8
    table = stacked(tables, TABLE_BYTES // (2 * length))
    table_shape = (2, 3 * length // 4, length // 2)

    spectrum = pl.pallas_call(
        y_forward_kernel,
        in_specs=[ANY] * 2,
        out_specs=ANY,
        out_shape=blocks,
        scratch_shapes=[
            pltpu.VMEM(fields.shape, jnp.float32),
            pltpu.VMEM(table_shape, jnp.bfloat16),
            pltpu.VMEM(blocks.shape, jnp.float32),
            pltpu.SemaphoreType.DMA((scalars,)),
            pltpu.SemaphoreType.DMA((2,)),
            pltpu.SemaphoreType.DMA((scalars, 3)),
        ],
        compiler_params=grant(60),
        cost_estimate=cost(work, total),
        name="y_forward",
    )(fields, table)
    held = pl.pallas_call(
        hold_kernel,
        in_specs=[ANY] * 2,
        out_specs=VMEM,
        out_shape=jax.ShapeDtypeStruct(table_shape, jnp.bfloat16),
        scratch_shapes=[pltpu.SemaphoreType.DMA((1,))],
        compiler_params=grant(48),
        cost_estimate=cost(0, 2 * MIB),
        name="hold",
    )(spectrum[0, 0, :8, :128], table)
    filtered = pl.pallas_call(
        functools.partial(x_kernel, walls),
        in_specs=[pl.BlockSpec(memory_space=pltpu.SMEM)] + [VMEM] * 4,
        out_specs=VMEM,
        out_shape=blocks,
        scratch_shapes=[pltpu.VMEM((walls * planes * waves, lines * groups), jnp.float32)] * scalars,
        compiler_params=grant(40),
        cost_estimate=cost(2 * work, total),
        name="x_filter",
    )(rates, square_y, square_x, held, exchange(spectrum))
    return pl.pallas_call(
        functools.partial(y_inverse_kernel, 1.0 / (length * lines * groups)),
        in_specs=[VMEM] * 2,
        out_specs=ANY,
        out_shape=jax.ShapeDtypeStruct(fields.shape, jnp.float32),
        scratch_shapes=[
            pltpu.VMEM(fields.shape, jnp.float32),
            pltpu.SemaphoreType.DMA((scalars, planes)),
        ],
        compiler_params=grant(40),
        cost_estimate=cost(work, total),
        name="y_inverse",
    )(held, exchange(filtered))


def exchange(blocks):
    walls, groups = lax.axis_size("wall"), lax.axis_size("row")
    members = {slot(w, r, groups): w * groups + r for w in range(walls) for r in range(groups)}
    return lax.all_to_all(
        blocks, AXES, split_axis=0, concat_axis=0, tiled=True,
        axis_index_groups=[[members[i] for i in range(len(members))]],
    )


def with_arrays(fields, rates, walls, square_y, square_x, y_tables, x_tables):
    scalars, planes, lines, length = fields.shape
    groups = lax.axis_size("row")
    devices = walls * groups
    waves = length // devices
    count = walls * planes
    order = np.array([slot(w, r, groups) for w in range(walls) for r in range(groups)])
    dot = functools.partial(jnp.matmul, precision=lax.Precision.HIGHEST)

    def whole(tables):
        pairs = [jnp.asarray(t).astype(jnp.float32) for t in (*tables[0], tables[1])]
        return [t[0] + t[1] for t in pairs]

    def forward(value, tables):
        first, second, third, fourth = fold(jnp.split(value, 4, axis=-1))
        parts = (first, second, jnp.concatenate([third, fourth], axis=-1))
        return jnp.concatenate([dot(v, t.T) for v, t in zip(parts, whole(tables))], axis=-1)

    def inverse(value, tables):
        parts = jnp.split(value, [value.shape[-1] // 4, value.shape[-1] // 2], axis=-1)
        first, second, third = (dot(v, t) for v, t in zip(parts, whole(tables)))
        return jnp.concatenate(unfold(first, second, *jnp.split(third, 2, axis=-1)), axis=-1)

    results = []
    for s in range(scalars):
        spectral = forward(fields[s], y_tables).reshape(planes * lines, devices, waves)
        received = exchange(spectral.transpose(1, 2, 0))[order]
        received = received.reshape(walls, groups, waves, planes, lines).transpose(0, 3, 2, 1, 4)
        field = forward(received.reshape(count, waves, groups * lines), x_tables)
        rate = rates[s][:, None, None]
        damping = jnp.exp(-rate * (square_y + square_x))
        for step in range(STEPS):
            padded = jnp.pad(field, ((1, 1), (0, 0), (0, 0)))
            field = damping * (field + rate * (padded[2:] + padded[:-2] - 2.0 * field))
        back = inverse(field, x_tables).reshape(walls, planes, waves, groups, lines)
        back = back.transpose(0, 3, 2, 1, 4).reshape(devices, waves, planes * lines)
        spectrum = exchange(back[np.argsort(order)]).reshape(length, -1)
        results.append(inverse(spectrum.T, y_tables).reshape(planes, lines, length))
    return jnp.stack(results) * (1.0 / (length * groups * lines))


def signed_square(waves, length):
    signed = jnp.where(waves > length // 2, waves - length, waves)
    scaled = 2.0 * np.pi / length * signed.astype(jnp.float32)
    return scaled * scaled


def per_device(thermal_scalars, conductive_number):
    scalars, planes, lines, length = thermal_scalars.shape
    walls, groups = lax.axis_size("wall"), lax.axis_size("row")
    length_x = lines * groups
    waves = length // (walls * groups)
    rates = lax.all_gather(conductive_number, "wall", axis=1, tiled=True)
    own = slot(lax.axis_index("wall"), lax.axis_index("row"), groups)
    place = own * waves + jnp.arange(waves, dtype=jnp.int32)
    square_y = signed_square(wave_order(place, length), length)[:, None]
    square_x = signed_square(wave_order(jnp.arange(length_x), length_x), length_x)[None, :]
    fits = lines == 64 and planes % 2 == 0 and waves % 8 == 0 and groups % 8 == 0
    if fits and length == length_x and walls * groups % 4 == 0:
        return with_kernels(thermal_scalars, rates, walls, square_y, square_x, tables_of(length))
    return with_arrays(
        thermal_scalars, rates, walls, square_y, square_x, tables_of(length), tables_of(length_x)
    )


def solution(mesh):
    return jax.shard_map(
        per_device,
        mesh=mesh,
        in_specs=(P(None, "wall", "row", None), P(None, "wall")),
        out_specs=P(None, "wall", "row", None),
        check_vma=False,
    )
```
